128 devices in a mesh: grp: 8 (over x, core), dev: 16 (over y, z).
Axes of the slice: x: 4, y: 4, z: 4, core: 2. Of those that a mesh axis runs over, the one named last changes fastest.
Arguments:
- node_features: float32 [65536, 768], P(('grp', 'dev')), may hold values from -6 to 6
- tiles: bfloat16 [6656, 128, 128], P(('grp', 'dev')), may hold values from -0.15625 to 0.15625
- tile_list: int32 [6656, 2], replicated, may hold values from 0 to 511, as said below
- weight: float32 [768, 768], replicated, may hold values from -0.21875 to 0.21875
- texts: float32 [4096, 768], P(('grp', 'dev')), may hold values from -6 to 6
- selected: int32 [4096], P(('grp', 'dev')), may hold values from 0 to 65535, as said below
- pairing: int32 [4096], P(('grp', 'dev')), may hold values from 0 to 4095, each once
Outputs:
- contrast_loss: float32 [], replicated
- grad_nodes: float32 [65536, 768], P(('grp', 'dev'))
- grad_weight: float32 [768, 768], replicated
- grad_texts: float32 [4096, 768], P(('grp', 'dev'))
The draws below stay inside these ranges and needn't reach their ends.
Inputs may be any that keep to these rules, and one draw needn't show every extreme that they name: `tile_list`: device number p = grp index * (devices along dev) + dev index holds node blocks p * 4 to (p + 1) * 4 - 1 and tiles p * 52 to (p + 1) * 52 - 1. A tile's row block lies on the device that holds the tile; its column block lies on that device, on another device of the same grp index, or on the device of the same dev index in another grp. At most 2 tiles of one device have column blocks on any one other device; in every draw each device has one other device of its grp index and one of its dev index at that most. `selected`: distinct ids; the ids listed on a device are nodes of that device.
All inputs are finite; a program needn't handle non-finite values.
Results may differ from the reference program's by a relative error of at most 0.0004.
The reference program's roundings to bfloat16 on the way (of `rounded` and `rounded_grads`) count: a program that leaves them out, or rounds other values in their place, can miss the bound.
Values may be sent and summed in bfloat16 or wider, within the bound.
A program may use at most 128 MiB of HBM per device.

```python
import jax
import jax.numpy as jnp
from jax import lax

D = 768
BLOCK = 128
NB_DEV = 4
CAP = 2
SEL_DEV = 32
TILE_DEV = 52
NODES = 65536
TILES = 6656
SEL = 4096
N_GRP = 8
N_DEV = 16


def draw_tile_list(key, part):
    pool_dev = CAP * (N_DEV - 1)
    pool_all = pool_dev + CAP * (N_GRP - 1)

    def one_device(device):
        sub_key = jax.random.fold_in(jax.random.fold_in(key, 7151), device)
        keys = jax.random.split(sub_key, 7)
        grp_index = device // N_DEV
        dev_index = device % N_DEV
        entries = jnp.arange(pool_all, dtype=jnp.int32)
        is_dev = entries < pool_dev
        near_pick = entries // CAP
        far_pick = (entries - pool_dev) // CAP
        peer_dev = near_pick + (near_pick >= dev_index).astype(jnp.int32)
        peer_grp = far_pick + (far_pick >= grp_index).astype(jnp.int32)
        peer = jnp.where(is_dev, grp_index * N_DEV + peer_dev, peer_grp * N_DEV + dev_index)
        forced_dev = jax.random.randint(keys[0], (), 0, N_DEV - 1)
        forced_grp = jax.random.randint(keys[1], (), 0, N_GRP - 1)
        forced = is_dev & (near_pick == forced_dev) | jnp.logical_not(is_dev) & (far_pick == forced_grp)
        priority = jax.random.permutation(keys[2], pool_all).astype(jnp.int32) + pool_all * forced.astype(jnp.int32)
        order_list = jnp.argsort(-priority)
        chosen_peers = peer[order_list]
        lowest = max(pool_all // 2, 2 * CAP)
        count = jax.random.randint(keys[3], (), lowest, pool_all + 1)
        slots = jnp.arange(TILE_DEV, dtype=jnp.int32)
        col_owner = jnp.where(slots < count, chosen_peers[jnp.minimum(slots, pool_all - 1)], device)
        col_owner = col_owner[jax.random.permutation(keys[4], TILE_DEV)]
        col_block = col_owner * NB_DEV + jax.random.randint(keys[5], (TILE_DEV,), 0, NB_DEV)
        row_block = device * NB_DEV + jax.random.randint(keys[6], (TILE_DEV,), 0, NB_DEV)
        return jnp.stack([row_block, col_block], axis=1).astype(jnp.int32)
    listed = jax.vmap(one_device)(jnp.arange(N_GRP * N_DEV, dtype=jnp.int32))
    return listed.reshape(TILES, 2).astype(jnp.int32)


def draw_selected(key, part):

    def one_device(device):
        sub_key = jax.random.fold_in(jax.random.fold_in(key, 9203), device)
        order_list = jax.random.permutation(sub_key, NB_DEV * BLOCK).astype(jnp.int32)
        return order_list[:SEL_DEV] + device * NB_DEV * BLOCK
    listed = jax.vmap(one_device)(jnp.arange(N_GRP * N_DEV, dtype=jnp.int32))
    return listed.reshape(SEL).astype(jnp.int32)


def shard_levels(own_key, dims, pieces, least, high):
    gain = 1.0
    for dim, parts in pieces:
        draws = jax.random.uniform(jax.random.fold_in(jax.random.fold_in(own_key, 6), dim), (parts,), jnp.float32, least / len(pieces), high / len(pieces))
        gain = gain * jnp.repeat(jnp.exp(draws), dims[dim] // parts).reshape((-1,) + (1,) * (len(dims) - 1 - dim))
    return gain


def bell_draw(key, extent, width, bound, cuts=(), kind=jnp.bfloat16):
    result = width * jax.random.normal(key, extent, jnp.float32)
    if cuts:
        result = result * shard_levels(key, extent, cuts, -0.22, 0.18)
    return jnp.clip(result, -bound, bound).astype(kind)


def setup_inputs(seed: int = 0) -> dict:
    streams_of = jax.random.split(jax.random.key(seed), 8)
    node_features = bell_draw(streams_of[0], (NODES, D), 1.0, 6.0, ((0, 128),), jnp.float32)
    tiles = bell_draw(streams_of[1], (TILES, BLOCK, BLOCK), (BLOCK * TILE_DEV // NB_DEV) ** -0.5, 0.15625, ((0, 128),))
    tile_list = draw_tile_list(jax.random.fold_in(streams_of[7], 71), 0)
    weight = bell_draw(streams_of[3], (D, D), D ** -0.5, 0.21875, (), jnp.float32)
    texts = bell_draw(streams_of[4], (SEL, D), 1.0, 6.0, ((0, 128),), jnp.float32)
    selected = draw_selected(jax.random.fold_in(streams_of[7], 71), 0)
    pairing = jax.random.permutation(streams_of[6], SEL).astype(jnp.int32)
    return dict(node_features=node_features, tiles=tiles, tile_list=tile_list, weight=weight, texts=texts, selected=selected, pairing=pairing)


SCALE = 1.0 / 0.07
EPS = 1e-06
PRECISE = lax.Precision.HIGHEST
ROOT_HALF = 0.7071067811865476
INV_ROOT_TWO_PI = 0.3989422804014327

def gelu_value(value):
    return 0.5 * value * (1.0 + lax.erf(value * ROOT_HALF))

def gelu_slope(value):
    return 0.5 * (1.0 + lax.erf(value * ROOT_HALF)) + value * jnp.exp(-0.5 * value * value) * INV_ROOT_TWO_PI

def reference(node_features, tiles, tile_list, weight, texts, selected, pairing):
    blocks_all = NODES // BLOCK
    rounded = lax.optimization_barrier(node_features.astype(jnp.bfloat16))
    source = rounded.astype(jnp.float32).reshape(blocks_all, BLOCK, D)
    row_blocks = tile_list[:, 0]
    col_blocks = tile_list[:, 1]

    def forward_step(total, device):
        start = (device * TILE_DEV).astype(jnp.int32)
        matrices = lax.dynamic_slice_in_dim(tiles, start, TILE_DEV, 0).astype(jnp.float32)
        rows_here = lax.dynamic_slice_in_dim(row_blocks, start, TILE_DEV, 0)
        cols_here = lax.dynamic_slice_in_dim(col_blocks, start, TILE_DEV, 0)
        products = jnp.einsum('tij,tjd->tid', matrices, source[cols_here], precision=PRECISE)
        return (total.at[rows_here].add(products), None)
    devices_all = jnp.arange(N_GRP * N_DEV, dtype=jnp.int32)
    messages, _ = lax.scan(forward_step, jnp.zeros((blocks_all, BLOCK, D), jnp.float32), devices_all)
    mixed = node_features + messages.reshape(NODES, D)
    chosen = mixed[selected]
    before = jnp.dot(chosen, weight, precision=PRECISE)
    hidden = gelu_value(before)
    node_norm = jnp.sqrt(lax.optimization_barrier(jnp.sum(hidden * hidden, axis=1, keepdims=True)) + EPS)
    unit_nodes = hidden / node_norm
    text_norm = jnp.sqrt(lax.optimization_barrier(jnp.sum(texts * texts, axis=1, keepdims=True)) + EPS)
    unit_texts = texts / text_norm
    scores = SCALE * jnp.dot(unit_nodes, unit_texts.T, precision=PRECISE)
    row_lse = jnp.log(lax.optimization_barrier(jnp.sum(jnp.exp(scores), axis=1)))
    col_lse = jnp.log(lax.optimization_barrier(jnp.sum(jnp.exp(scores), axis=0)))
    target = pairing[:, None] == jnp.arange(SEL, dtype=jnp.int32)[None, :]
    positive = jnp.sum(jnp.where(target, scores, jnp.zeros_like(scores)))
    contrast_loss = (jnp.sum(row_lse) + jnp.sum(col_lse)) / (2.0 * SEL) - positive / SEL
    score_grads = 0.5 * (jnp.exp(scores - row_lse[:, None]) + jnp.exp(scores - col_lse[None, :])) - target.astype(jnp.float32)
    node_dir = SCALE * jnp.dot(score_grads, unit_texts, precision=PRECISE)
    text_dir = SCALE * jnp.dot(score_grads.T, unit_nodes, precision=PRECISE)
    node_back = (node_dir - unit_nodes * lax.optimization_barrier(jnp.sum(unit_nodes * node_dir, axis=1, keepdims=True))) / node_norm
    grad_texts = (text_dir - unit_texts * lax.optimization_barrier(jnp.sum(unit_texts * text_dir, axis=1, keepdims=True))) / text_norm
    pre_grad = node_back * gelu_slope(before)
    grad_weight = jnp.dot(chosen.T, pre_grad, precision=PRECISE)
    row_grads = jnp.dot(pre_grad, weight.T, precision=PRECISE)
    dense_grads = jnp.zeros((NODES, D), jnp.float32).at[selected].add(row_grads)
    rounded_grads = lax.optimization_barrier(dense_grads.astype(jnp.bfloat16))
    grad_source = rounded_grads.astype(jnp.float32).reshape(blocks_all, BLOCK, D)

    def backward_step(total, device):
        start = (device * TILE_DEV).astype(jnp.int32)
        matrices = lax.dynamic_slice_in_dim(tiles, start, TILE_DEV, 0).astype(jnp.float32)
        rows_here = lax.dynamic_slice_in_dim(row_blocks, start, TILE_DEV, 0)
        cols_here = lax.dynamic_slice_in_dim(col_blocks, start, TILE_DEV, 0)
        products = jnp.einsum('tij,tid->tjd', matrices, grad_source[rows_here], precision=PRECISE)
        return (total.at[cols_here].add(products), None)
    back_terms, _ = lax.scan(backward_step, jnp.zeros((blocks_all, BLOCK, D), jnp.float32), devices_all)
    grad_nodes = dense_grads + back_terms.reshape(NODES, D)
    return (contrast_loss, grad_nodes, grad_weight, grad_texts)
```

```python
import functools

import jax
import jax.numpy as jnp
from jax import lax
from jax.experimental import pallas as pl
from jax.experimental.pallas import tpu as pltpu
from jax.sharding import PartitionSpec as P

MESH = pl.DeviceIdType.MESH
CAP = 2
SCALE = 1.0 / 0.07
EPS = 1e-06
ROOT_HALF = 0.7071067811865476
INV_ROOT_TWO_PI = 0.3989422804014327
F32 = jnp.float32
BF16 = jnp.bfloat16
NG, ND = 8, 16
NPEER = NG + ND
SEMS = 320


def split(value):
    hi = value.astype(BF16)
    return hi, (value - hi.astype(F32)).astype(BF16)


def dot(a, b, ca=1, cb=0):
    return lax.dot_general(a, b, (((ca,), (cb,)), ((), ())), preferred_element_type=F32)


def dot3(a, b, ca=1, cb=0):
    return dot(a[0], b[0], ca, cb) + (dot(a[0], b[1], ca, cb) + dot(a[1], b[0], ca, cb))


def prep_kernel(list_ref, sel_ref, tiles_ref, rows_ref, local_ref, acc, onehot, count, meta):
    g, d = lax.axis_index("grp"), lax.axis_index("dev")
    device = g * ND + d
    n_tiles, block = tiles_ref.shape[0], tiles_ref.shape[1]
    sel_dev = sel_ref.shape[0]
    nb = local_ref.shape[2] // block
    rows_ref[...] = jnp.zeros_like(rows_ref)
    acc[...] = jnp.zeros_like(acc)
    lane = lax.broadcasted_iota(jnp.int32, (sel_dev, block), 1)
    sel = sel_ref[...]
    for b in range(nb):
        onehot[b] = (sel == lane + b * block).astype(F32).astype(BF16)
    for p in range(NPEER + 1):
        count[p] = 0
        meta[p] = 0
    for t in range(n_tiles):
        row_block = list_ref[2 * t] - device * nb
        col = list_ref[2 * t + 1]
        owner = col // nb
        col_block = col - owner * nb
        og = owner // ND
        od = owner - og * ND
        local = owner == device
        peer = jnp.where(local, NPEER, jnp.where(og == g, od, ND + og))
        rank = jnp.minimum(count[peer], 1)
        count[peer] = rank + 1
        meta[peer] = meta[peer] + col_block * jnp.where(rank == 0, 1, nb)
        picked = dot(onehot[row_block], tiles_ref[t])
        rows_ref[rank, peer] = picked.astype(BF16)
        acc[col_block] += picked * local.astype(F32)
    for p in range(NPEER):
        rows_ref[2, p] = jnp.full((sel_dev, block), meta[p].astype(F32), F32).astype(BF16)
    for b in range(nb):
        hi, lo = split(acc[b])
        local_ref[0, :, b * block : (b + 1) * block] = hi
        local_ref[1, :, b * block : (b + 1) * block] = lo


class Links:
    def __init__(self, send_sem, recv_sem):
        self.g, self.d = lax.axis_index("grp"), lax.axis_index("dev")
        self.x, self.c = self.g // 2, self.g % 2
        self.y, self.z = self.d // 4, self.d % 4
        self.send_sem, self.recv_sem = send_sem, recv_sem
        self.used, self.copies = 0, []

    def to(self, src, dst, grp=None, dev=None):
        k = self.used
        self.used += 1
        copy = pltpu.make_async_remote_copy(
            src_ref=src,
            dst_ref=dst,
            send_sem=self.send_sem.at[k],
            recv_sem=self.recv_sem.at[k],
            device_id=(self.g if grp is None else grp, self.d if dev is None else dev),
            device_id_type=MESH,
        )
        copy.start()
        self.copies.append(copy)
        return copy

    def pos(self, axis):
        return {"x": self.x, "y": self.y, "z": self.z}[axis]

    def shift(self, src, dst, axis, step):
        if axis == "x":
            return self.to(src, dst, grp=(self.x + step) % 4 * 2 + self.c)
        if axis == "y":
            return self.to(src, dst, dev=(self.y + step) % 4 * 4 + self.z)
        return self.to(src, dst, dev=self.y * 4 + (self.z + step) % 4)

    def core(self, src, dst):
        return self.to(src, dst, grp=self.x * 2 + 1 - self.c)

    def all_dev(self, src, dst):
        out = []
        for i in range(1, ND):
            e = (self.d + i) % ND
            out.append(self.to(src(e), dst, dev=e))
        return out

    def all_grp(self, src, dst):
        out = []
        for i in range(1, NG):
            e = (self.g + i) % NG
            out.append(self.to(src(e), dst, grp=e))
        return out


def arrived(copies):
    for copy in copies:
        copy.wait_recv()


class Ring:
    def __init__(self, links, axis, chunk):
        self.links, self.axis, self.chunk = links, axis, chunk
        r = links.pos(axis)
        self.r, self.up, self.down, self.far = r, (r + 1) % 4, (r + 3) % 4, (r + 2) % 4

    def gather_1(self):
        own = self.chunk(self.r, None)
        self.a = self.links.shift(own, own, self.axis, 1)
        self.b = self.links.shift(own, own, self.axis, 3)

    def gather_2(self):
        self.a.wait_recv()
        part = self.chunk(self.down, 0)
        self.a = self.links.shift(part, part, self.axis, 1)
        self.b.wait_recv()
        part = self.chunk(self.up, 1)
        self.b = self.links.shift(part, part, self.axis, 3)

    def gather_3(self):
        self.a.wait_recv()
        self.b.wait_recv()

    def reduce_1(self, land):
        self.land = land
        send = self.links.shift
        self.a = send(self.chunk(self.far, 0), land(0, 0, 0), self.axis, 1)
        self.b = send(self.chunk(self.far, 1), land(0, 1, 1), self.axis, 3)
        self.a1 = send(self.chunk(self.up, 1), land(1, 0, 1), self.axis, 1)
        self.b1 = send(self.chunk(self.down, 0), land(1, 1, 0), self.axis, 3)

    def reduce_2(self):
        send, land = self.links.shift, self.land
        self.a.wait_recv()
        view = self.chunk(self.up, 0)
        view[...] += land(0, 0, 0)[...]
        self.a = send(view, land(1, 0, 0), self.axis, 1)
        self.b.wait_recv()
        view = self.chunk(self.down, 1)
        view[...] += land(0, 1, 1)[...]
        self.b = send(view, land(1, 1, 1), self.axis, 3)

    def reduce_3(self):
        arrived([self.a, self.b, self.a1, self.b1])
        for s in (0, 1):
            view = self.chunk(self.r, s)
            view[...] += self.land(1, 0, s)[...] + self.land(1, 1, s)[...]


def rows_of(ref, s, cut):
    if s is None:
        return ref
    n = ref.shape[0]
    return ref.at[pl.ds(0, cut)] if s == 0 else ref.at[pl.ds(cut, n - cut)]


class Plane:
    def __init__(self, links, buf):
        y, z = links.y, links.z
        cut = 16
        self.links, self.buf = links, buf

        def big(h):
            def view(i, s):
                some = slice(None) if s is None else pl.ds(2 * s, 2)
                return buf.at[0, i, some] if h == 0 else buf.at[1, some, i]

            return view

        def small(h):
            def view(i, s):
                return rows_of(buf.at[0, y, i] if h == 0 else buf.at[1, i, z], s, cut)

            return view

        self.cut = cut
        self.outer = [Ring(links, "y", big(0)), Ring(links, "z", big(1))]
        self.inner = [Ring(links, "z", small(0)), Ring(links, "y", small(1))]

    def gather(self):
        for name in ("gather_1", "gather_2", "gather_3"):
            for ring in self.inner:
                getattr(ring, name)()
            yield
        for name in ("gather_1", "gather_2", "gather_3"):
            for ring in self.outer:
                getattr(ring, name)()
            yield

    def reduce(self, big, small):
        rows = self.buf.shape[3]
        cut = self.cut

        def land_big(h):
            def view(k, way, s):
                return big.at[h, way, pl.ds(0, 2) if k == 0 else pl.ds(2 + 2 * s, 2)]

            return view

        def land_small(h):
            def view(k, way, s):
                n = (cut, rows - cut)[s]
                start = 0 if k == 0 else (cut if s == 0 else 2 * cut)
                return small.at[h, way, pl.ds(start, n)]

            return view

        for h, ring in enumerate(self.outer):
            ring.reduce_1(land_big(h))
        yield
        for ring in self.outer:
            ring.reduce_2()
        yield
        for h in (0, 1):
            self.outer[h].reduce_3()
            self.inner[h].reduce_1(land_small(h))
        yield
        for ring in self.inner:
            ring.reduce_2()
        yield
        for ring in self.inner:
            ring.reduce_3()
        yield


class Line:
    def __init__(self, links, buf):
        c = links.c
        self.links, self.buf = links, buf
        self.ring = Ring(links, "x", lambda i, s: rows_of(buf.at[i, c], s, 16))

    def gather(self):
        for name in ("gather_1", "gather_2", "gather_3"):
            getattr(self.ring, name)()
            yield
        view = self.buf.at[:, self.links.c]
        copy = self.links.core(view, view)
        yield
        copy.wait_recv()
        yield

    def reduce(self, pair, small):
        rows = self.buf.shape[2]

        def land(k, way, s):
            n = (16, rows - 16)[s]
            return small.at[way, pl.ds(0 if k == 0 else (16 if s == 0 else 32), n)]

        copy = self.links.core(self.buf.at[:, 1 - self.links.c], pair)
        yield
        copy.wait_recv()
        view = self.buf.at[:, self.links.c]
        view[...] += pair[...]
        self.ring.reduce_1(land)
        yield
        self.ring.reduce_2()
        yield
        self.ring.reduce_3()
        yield


def together(*runs):
    runs = list(runs)
    while runs:
        runs = [run for run in runs if next(run, "end") != "end"]


def main_kernel(
    rows_ref, local_ref, nodes_ref, weight_ref, texts_ref, sel_ref, sel_list, pair_ref,
    loss_ref, gn_ref, gw_ref, gt_ref,
    near_in, far_in, spread, spread_t, rounded, wh, wl,
    npart, nbig, nsmall, fpart, fpair, fsmall,
    units, cols, pairs, spart, sbig, ssmall, tpart, tpair, tsmall,
    row_in, col_in, loss_dev, loss_grp, g_near, g_far,
    gpart, gpair, gbig, gsmall, gx, gfull, chosen,
    send_sem, recv_sem,
):
    links = Links(send_sem, recv_sem)
    g, d, x, c, y, z = links.g, links.d, links.x, links.c, links.y, links.z
    sel_dev, feat = texts_ref.shape
    half = feat // 2
    nodes_dev = nodes_ref.shape[0]
    block = near_in.shape[3]
    nb = nodes_dev // block
    total_sel = sel_dev * NG * ND

    barrier = pltpu.get_barrier_semaphore()
    for i in range(1, ND):
        pl.semaphore_signal(barrier, inc=1, device_id=(g, (d + i) % ND), device_id_type=MESH)
    for i in range(1, NG):
        pl.semaphore_signal(barrier, inc=1, device_id=((g + i) % NG, d), device_id_type=MESH)

    texts = texts_ref[...]
    text_norm = jnp.sqrt(jnp.sum(texts * texts, axis=1, keepdims=True) + EPS)
    unit_texts = texts / text_norm
    cols[x, c] = unit_texts
    pairs[d] = jnp.broadcast_to(pair_ref[...], (sel_dev, block))
    near_in[:, d] = jnp.zeros((3, sel_dev, block), BF16)
    far_in[:, g] = jnp.zeros((3, sel_dev, block), BF16)
    pl.semaphore_wait(barrier, ND + NG - 2)

    near_copies = links.all_dev(lambda e: rows_ref.at[:, e], near_in.at[:, d])
    far_copies = links.all_grp(lambda e: rows_ref.at[:, ND + e], far_in.at[:, g])
    text_run = Line(links, cols).gather()
    next(text_run)
    pair_copies = links.all_dev(lambda e: pairs.at[d], pairs.at[d])

    rounded[...] = nodes_ref[...].astype(BF16)
    whole = weight_ref[...]
    hi, lo = split(whole)
    wh[...] = hi
    wl[...] = lo
    for k in range(sel_dev):
        chosen[pl.ds(k, 1), :] = nodes_ref[pl.ds(sel_list[k], 1), :]
    next(text_run)

    def expand(into, rows):
        tag = rows[2].astype(F32)
        second = jnp.floor(tag * (1.0 / nb) + 0.01)
        first = tag - second * nb
        for q, which in ((0, first), (1, second)):
            for b in range(nb):
                spread[q, into, :, b * block : (b + 1) * block] = jnp.where(
                    which == float(b), rows[q].astype(F32), 0.0
                ).astype(BF16)

    arrived(near_copies)
    for p in range(ND):
        expand(p, near_in[:, p])
    spread[0, d] = local_ref[0]
    spread[1, d] = local_ref[1]
    flat = (ND * sel_dev, nb * block)
    s0, s1 = spread[0, :ND].reshape(flat), spread[1, :ND].reshape(flat)
    for h in (0, 1):
        table = rounded[:, h * half : (h + 1) * half]
        npart[h] = (dot(s0, table) + dot(s1, table)).reshape(4, 4, sel_dev, half)
    near_run = Plane(links, npart).reduce(nbig, nsmall)
    next(near_run)
    arrived(far_copies)
    for p in range(NG):
        expand(ND + p, far_in[:, p])
    flat = (NG * sel_dev, nb * block)
    s0, s1 = spread[0, ND:].reshape(flat), spread[1, ND:].reshape(flat)
    fpart[...] = (dot(s0, rounded[...]) + dot(s1, rounded[...])).reshape(4, 2, sel_dev, feat)
    far_run = Line(links, fpart).reduce(fpair, fsmall)
    next(far_run)
    some = 128 // sel_dev
    for q in (0, 1):
        for i in range(NPEER // some):
            rows = spread[q, i * some : (i + 1) * some].reshape(128, nb * block)
            spread_t[q, :, i * 128 : (i + 1) * 128] = rows.astype(F32).T.astype(BF16)
    together(near_run, far_run, text_run)

    far_sum = fpart[x, c]
    for h in (0, 1):
        take = slice(h * half, (h + 1) * half)
        own = npart[h, y, z]
        chosen[:, take] += own + far_sum[:, take]
    picked = chosen[...]
    picked_parts = split(picked)
    before = dot3(picked_parts, (wh[...], wl[...]))
    curve = 0.5 * (1.0 + lax.erf(before * ROOT_HALF))
    hidden = before * curve
    node_norm = jnp.sqrt(jnp.sum(hidden * hidden, axis=1, keepdims=True) + EPS)
    unit_nodes = hidden / node_norm
    for h in (0, 1):
        units[h, y, z] = unit_nodes[:, h * half : (h + 1) * half]
    unit_run = Plane(links, units).gather()
    next(unit_run)
    arrived(pair_copies)
    col_parts = split(cols[...].reshape(NG * sel_dev, feat))
    together(unit_run)

    rows_all = ND * sel_dev
    cols_all = NG * sel_dev
    unit_parts = [split(units[h].reshape(rows_all, half)) for h in (0, 1)]
    scores = 0.0
    for h in (0, 1):
        text_half = tuple(v[:, h * half : (h + 1) * half] for v in col_parts)
        scores += dot3(unit_parts[h], text_half, 1, 1)
    scores = SCALE * scores
    exps = jnp.exp(scores)
    row_sum = jnp.sum(exps, axis=1, keepdims=True)
    row_in[d] = jnp.broadcast_to(row_sum, (rows_all, 128)).T[:8]
    row_copies = links.all_dev(lambda e: row_in.at[d], row_in.at[d])
    col_in[g] = jnp.broadcast_to(jnp.sum(exps, axis=0, keepdims=True), (8, cols_all))
    col_copies = links.all_grp(lambda e: col_in.at[g], col_in.at[g])
    lane = lax.broadcasted_iota(jnp.int32, (sel_dev, cols_all), 1)
    ids = (lane // sel_dev * ND + d) * sel_dev + lane % sel_dev
    target = (pairs[...].reshape(rows_all, block)[:, :1] == ids[:1]).astype(F32)
    positive = jnp.sum(jnp.sum(target * scores, axis=1, keepdims=True), axis=0, keepdims=True)
    arrived(col_copies)
    col_total = jnp.sum(col_in[...], axis=0)
    arrived(row_copies)
    row_total = jnp.sum(row_in[...], axis=0)
    log_rows = jnp.sum(jnp.log(row_total[:1]), axis=1, keepdims=True)
    log_cols = jnp.sum(jnp.log(col_total[:1]), axis=1, keepdims=True)
    part = (log_rows / ND + log_cols / NG) / (2.0 * total_sel) - positive / total_sel
    loss_dev[d] = jnp.broadcast_to(part, (8, 128))
    row_recip = jnp.broadcast_to(1.0 / row_total[:1], (128, rows_all)).T[:, :1]
    col_recip = 1.0 / col_total[:1]
    slope = 0.5 * exps * (row_recip + col_recip) - target
    slope_parts = split(slope)
    for h in (0, 1):
        text_half = tuple(v[:, h * half : (h + 1) * half] for v in col_parts)
        spart[h] = dot3(slope_parts, text_half).reshape(4, 4, sel_dev, half)
    node_run = Plane(links, spart).reduce(sbig, ssmall)
    next(node_run)
    for h in (0, 1):
        grown = dot3(slope_parts, unit_parts[h], 0, 0)
        tpart[:, :, :, h * half : (h + 1) * half] = grown.reshape(4, 2, sel_dev, half)
    loss_copies = links.all_dev(lambda e: loss_dev.at[d], loss_dev.at[d])
    together(node_run, Line(links, tpart).reduce(tpair, tsmall))
    arrived(loss_copies)
    loss_grp[g] = jnp.sum(loss_dev[...], axis=0)
    loss_copies = links.all_grp(lambda e: loss_grp.at[g], loss_grp.at[g])

    node_dir = SCALE * jnp.concatenate([spart[0, y, z], spart[1, y, z]], axis=1)
    node_back = (
        node_dir - unit_nodes * jnp.sum(unit_nodes * node_dir, axis=1, keepdims=True)
    ) / node_norm
    pre_grad = node_back * (curve + before * jnp.exp(-0.5 * before * before) * INV_ROOT_TWO_PI)
    pre_parts = split(pre_grad)
    row_grads = dot3(pre_parts, (wh[...], wl[...]), 1, 1)
    grads = row_grads.astype(BF16)
    for h in (0, 1):
        g_near[h, y, z] = grads[:, h * half : (h + 1) * half]
    g_far[x, c] = grads
    near_run = Plane(links, g_near).gather()
    far_run = Line(links, g_far).gather()
    next(near_run)
    next(far_run)

    deep = 2 * 16
    piece = feat // deep
    for h in (0, 1):
        right = tuple(v[:, h * half : (h + 1) * half] for v in pre_parts)
        gpart[:, h] = dot3(picked_parts, right, 0, 0).reshape(2, 4, 4, piece, half)
    copy = links.core(gpart.at[1 - c], gpair)
    next(near_run)
    next(far_run)
    copy.wait_recv()
    mine = gpart.at[c]
    mine[...] += gpair[...]
    plane = Plane(links, mine)
    weight_run = plane.reduce(gbig, gsmall)
    next(weight_run)
    together(near_run, far_run, weight_run)
    gx[x] = gpart[c, :, y, z]
    copies = []
    for i in (1, 2, 3):
        copies.append(links.shift(gx.at[x], gx.at[x], "x", i))

    text_dir = SCALE * tpart[x, c]
    gt_ref[...] = (
        text_dir - unit_texts * jnp.sum(unit_texts * text_dir, axis=1, keepdims=True)
    ) / text_norm
    arrived(copies)
    gfull[c, :, y, z] = gx[0] + gx[1] + gx[2] + gx[3]
    weight_run = Plane(links, gfull.at[c]).gather()
    next(weight_run)

    spot = lax.broadcasted_iota(jnp.int32, (sel_dev, nodes_dev), 1)
    hot = (sel_ref[...] == spot).astype(F32).astype(BF16)
    top, mid = split(row_grads)
    low = (row_grads - top.astype(F32) - mid.astype(F32)).astype(BF16)
    steps = [lambda: next(weight_run), lambda: next(weight_run)]
    for h in (0, 1):
        take = slice(h * half, (h + 1) * half)
        near = g_near[h].reshape(ND * sel_dev, half)
        far = g_far[:, :, :, take].reshape(NG * sel_dev, half)
        edge = ND * sel_dev
        total = dot(spread_t[0, :, :edge], near) + dot(spread_t[1, :, :edge], near)
        total += dot(spread_t[0, :, edge:], far) + dot(spread_t[1, :, edge:], far)
        total += dot(hot, top[:, take], 0, 0) + dot(hot, mid[:, take], 0, 0)
        gn_ref[:, take] = total + dot(hot, low[:, take], 0, 0)
        steps[h]()
    together(weight_run)
    view = gfull.at[c]
    copy = links.core(view, view)
    arrived(loss_copies)
    loss_ref[...] = jnp.sum(loss_grp[...], axis=0)
    copy.wait_recv()
    rows_half = feat // 2
    for core in (0, 1):
        for h in (0, 1):
            gw_ref[core * rows_half : (core + 1) * rows_half, h * half : (h + 1) * half] = gfull[
                core, h
            ].reshape(rows_half, half)
    for copy in links.copies:
        copy.wait_send()


def shards(node_features, tiles, tile_list, weight, texts, selected, pairing):
    device = lax.axis_index("grp") * ND + lax.axis_index("dev")
    tile_dev, block = tiles.shape[0], tiles.shape[1]
    nodes_dev, feat = node_features.shape
    sel_dev = selected.shape[0]
    nb = nodes_dev // block
    half = feat // 2
    piece = feat // 32
    my_list = lax.dynamic_slice_in_dim(tile_list, device * tile_dev, tile_dev, 0).reshape(-1)
    sel_own = selected - device * nodes_dev
    sel_col = sel_own.reshape(sel_dev, 1)
    vmem = pl.BlockSpec(memory_space=pltpu.VMEM)
    smem = pl.BlockSpec(memory_space=pltpu.SMEM)
    rows, local = pl.pallas_call(
        prep_kernel,
        out_shape=(
            jax.ShapeDtypeStruct((3, NPEER + 1, sel_dev, block), BF16),
            jax.ShapeDtypeStruct((2, sel_dev, nb * block), BF16),
        ),
        in_specs=[smem, vmem, vmem],
        out_specs=(vmem, vmem),
        scratch_shapes=[
            pltpu.VMEM((nb, sel_dev, block), F32),
            pltpu.VMEM((nb, sel_dev, block), BF16),
            pltpu.SMEM((NPEER + 1,), jnp.int32),
            pltpu.SMEM((NPEER + 1,), jnp.int32),
        ],
        compiler_params=pltpu.CompilerParams(vmem_limit_bytes=16 * 2**20),
    )(my_list, sel_col, tiles)

    def f32(*shape):
        return pltpu.VMEM(shape, F32)

    def bf16(*shape):
        return pltpu.VMEM(shape, BF16)

    def plane_buffers(rows):
        return [
            f32(2, 2, 6, rows, half),
            f32(2, 2, 16 + rows, half),
        ]

    def line_buffers():
        return [f32(4, 2, sel_dev, feat), f32(4, sel_dev, feat), f32(2, 16 + sel_dev, feat)]

    loss, grad_nodes, grad_weight, grad_texts = pl.pallas_call(
        main_kernel,
        out_shape=(
            jax.ShapeDtypeStruct((8, 128), F32),
            jax.ShapeDtypeStruct((nodes_dev, feat), F32),
            jax.ShapeDtypeStruct((feat, feat), F32),
            jax.ShapeDtypeStruct((sel_dev, feat), F32),
        ),
        in_specs=[vmem] * 6 + [smem, vmem],
        out_specs=(vmem,) * 4,
        scratch_shapes=[
            bf16(3, ND, sel_dev, block),
            bf16(3, NG, sel_dev, block),
            bf16(2, NPEER, sel_dev, nb * block),
            bf16(2, nb * block, NPEER * sel_dev),
            bf16(nodes_dev, feat),
            bf16(feat, feat),
            bf16(feat, feat),
            f32(2, 4, 4, sel_dev, half),
            *plane_buffers(sel_dev),
            *line_buffers(),
            f32(2, 4, 4, sel_dev, half),
            f32(4, 2, sel_dev, feat),
            pltpu.VMEM((ND, sel_dev, block), jnp.int32),
            f32(2, 4, 4, sel_dev, half),
            *plane_buffers(sel_dev),
            *line_buffers(),
            f32(ND, 8, ND * sel_dev),
            f32(NG, 8, NG * sel_dev),
            f32(ND, 8, 128),
            f32(NG, 8, 128),
            bf16(2, 4, 4, sel_dev, half),
            bf16(4, 2, sel_dev, feat),
            f32(2, 2, 4, 4, piece, half),
            f32(2, 4, 4, piece, half),
            *plane_buffers(piece),
            f32(4, 2, piece, half),
            f32(2, 2, 4, 4, piece, half),
            f32(sel_dev, feat),
            pltpu.SemaphoreType.DMA((SEMS,)),
            pltpu.SemaphoreType.DMA((SEMS,)),
        ],
        compiler_params=pltpu.CompilerParams(
            collective_id=0, has_side_effects=True, vmem_limit_bytes=60 * 2**20
        ),
    )(rows, local, node_features, weight, texts, sel_col, sel_own, pairing.reshape(sel_dev, 1))
    return loss[0, 0], grad_nodes, grad_weight, grad_texts


def solution(mesh):
    both = ("grp", "dev")
    placed = (
        P(both, None),
        P(both, None, None),
        P(),
        P(),
        P(both, None),
        P(both),
        P(both),
    )
    return jax.shard_map(
        shards,
        mesh=mesh,
        in_specs=placed,
        out_specs=(P(), P(both, None), P(), P(both, None)),
        check_vma=False,
    )
```

```python
import functools

import jax
import jax.numpy as jnp
from jax import lax
from jax.experimental import pallas as pl
from jax.experimental.pallas import tpu as pltpu
from jax.sharding import PartitionSpec as P

MESH = pl.DeviceIdType.MESH
CAP = 2
SCALE = 1.0 / 0.07
EPS = 1e-06
ROOT_HALF = 0.7071067811865476
INV_ROOT_TWO_PI = 0.3989422804014327
F32 = jnp.float32
BF16 = jnp.bfloat16
NG, ND = 8, 16
NPEER = NG + ND
SEMS = 384


def split(value):
    hi = value.astype(BF16)
    return hi, (value - hi.astype(F32)).astype(BF16)


def dot(a, b, ca=1, cb=0):
    return lax.dot_general(a, b, (((ca,), (cb,)), ((), ())), preferred_element_type=F32)


def dot3(a, b, ca=1, cb=0):
    return dot(a[0], b[0], ca, cb) + (dot(a[0], b[1], ca, cb) + dot(a[1], b[0], ca, cb))


def prep_kernel(
    list_ref, sel_ref, pair_ref, tiles_ref, nodes_ref,
    rows_ref, local_ref, rounded_ref, chosen_ref, spot_ref,
    acc, onehot, column, count, meta,
):
    g, d = lax.axis_index("grp"), lax.axis_index("dev")
    device = g * ND + d
    n_tiles, block = tiles_ref.shape[0], tiles_ref.shape[1]
    sel_dev = sel_ref.shape[0]
    nodes_dev = nodes_ref.shape[0]
    nb = nodes_dev // block
    rows_ref[...] = jnp.zeros_like(rows_ref)
    acc[...] = jnp.zeros_like(acc)
    for k in range(sel_dev):
        own = sel_ref[k] - device * nodes_dev
        spot_ref[pl.ds(k, 1), :] = jnp.full((1, block), own, jnp.int32)
        column[pl.ds(k, 1), :] = jnp.full((1, block), pair_ref[k], jnp.int32)
        chosen_ref[pl.ds(k, 1), :] = nodes_ref[pl.ds(own, 1), :]
    lane = lax.broadcasted_iota(jnp.int32, (sel_dev, block), 1)
    sel = spot_ref[...]
    for b in range(nb):
        onehot[b] = (sel == lane + b * block).astype(F32).astype(BF16)
    for p in range(NPEER + 1):
        count[p] = 0
        meta[p] = 0
    for t in range(n_tiles):
        row_block = list_ref[2 * t] - device * nb
        col = list_ref[2 * t + 1]
        owner = col // nb
        col_block = col - owner * nb
        og = owner // ND
        od = owner - og * ND
        local = owner == device
        peer = jnp.where(local, NPEER, jnp.where(og == g, od, ND + og))
        rank = jnp.minimum(count[peer], 1)
        count[peer] = rank + 1
        meta[peer] = meta[peer] + col_block * jnp.where(rank == 0, 1, nb)
        picked = dot(onehot[row_block], tiles_ref[t])
        rows_ref[rank, peer] = picked.astype(BF16)
        acc[col_block] += picked * local.astype(F32)
    pair = column[...]
    high = pair // 64
    tag = jnp.where(lane == 1, high, pair - high * 64)
    for p in range(NPEER):
        rows_ref[2, p] = jnp.where(lane == 0, meta[p], tag).astype(F32).astype(BF16)
    rows_ref[2, d] = jnp.where(lane == 0, 0, tag).astype(F32).astype(BF16)
    for b in range(nb):
        hi, lo = split(acc[b])
        local_ref[0, :, b * block : (b + 1) * block] = hi
        local_ref[1, :, b * block : (b + 1) * block] = lo
    rounded_ref[...] = nodes_ref[...].astype(BF16)


class Links:
    def __init__(self, send_sem, recv_sem):
        self.g, self.d = lax.axis_index("grp"), lax.axis_index("dev")
        self.x, self.c = self.g // 2, self.g % 2
        self.y, self.z = self.d // 4, self.d % 4
        self.send_sem, self.recv_sem = send_sem, recv_sem
        self.used, self.copies = 0, []

    def to(self, src, dst, grp=None, dev=None):
        k = self.used
        self.used += 1
        copy = pltpu.make_async_remote_copy(
            src_ref=src,
            dst_ref=dst,
            send_sem=self.send_sem.at[k],
            recv_sem=self.recv_sem.at[k],
            device_id=(self.g if grp is None else grp, self.d if dev is None else dev),
            device_id_type=MESH,
        )
        copy.start()
        self.copies.append(copy)
        return copy

    def pos(self, axis):
        return {"x": self.x, "y": self.y, "z": self.z}[axis]

    def shift(self, src, dst, axis, step):
        if axis == "x":
            return self.to(src, dst, grp=(self.x + step) % 4 * 2 + self.c)
        if axis == "y":
            return self.to(src, dst, dev=(self.y + step) % 4 * 4 + self.z)
        return self.to(src, dst, dev=self.y * 4 + (self.z + step) % 4)

    def core(self, src, dst):
        return self.to(src, dst, grp=self.x * 2 + 1 - self.c)

    def all_dev(self, src, dst):
        out = []
        for i in range(1, ND):
            e = (self.d + i) % ND
            out.append(self.to(src(e), dst, dev=e))
        return out

    def all_grp(self, src, dst):
        out = []
        for i in range(1, NG):
            e = (self.g + i) % NG
            out.append(self.to(src(e), dst, grp=e))
        return out


def arrived(copies):
    for copy in copies:
        copy.wait_recv()


class Ring:
    def __init__(self, links, axis, chunk):
        self.links, self.axis, self.chunk = links, axis, chunk
        r = links.pos(axis)
        self.r, self.up, self.down, self.far = r, (r + 1) % 4, (r + 3) % 4, (r + 2) % 4

    def gather_1(self):
        own = self.chunk(self.r, None)
        self.a = self.links.shift(own, own, self.axis, 1)
        self.b = self.links.shift(own, own, self.axis, 3)

    def gather_2(self):
        self.a.wait_recv()
        part = self.chunk(self.down, 0)
        self.a = self.links.shift(part, part, self.axis, 1)
        self.b.wait_recv()
        part = self.chunk(self.up, 1)
        self.b = self.links.shift(part, part, self.axis, 3)

    def gather_3(self):
        self.a.wait_recv()
        self.b.wait_recv()

    def reduce_1(self, land):
        self.land = land
        send = self.links.shift
        self.a = send(self.chunk(self.far, 0), land(0, 0, 0), self.axis, 1)
        self.b = send(self.chunk(self.far, 1), land(0, 1, 1), self.axis, 3)
        self.a1 = send(self.chunk(self.up, 1), land(1, 0, 1), self.axis, 1)
        self.b1 = send(self.chunk(self.down, 0), land(1, 1, 0), self.axis, 3)

    def reduce_2(self):
        send, land = self.links.shift, self.land
        self.a.wait_recv()
        view = self.chunk(self.up, 0)
        view[...] += land(0, 0, 0)[...]
        self.a = send(view, land(1, 0, 0), self.axis, 1)
        self.b.wait_recv()
        view = self.chunk(self.down, 1)
        view[...] += land(0, 1, 1)[...]
        self.b = send(view, land(1, 1, 1), self.axis, 3)

    def reduce_3(self):
        arrived([self.a, self.b, self.a1, self.b1])
        for s in (0, 1):
            view = self.chunk(self.r, s)
            view[...] += self.land(1, 0, s)[...] + self.land(1, 1, s)[...]


def rows_of(ref, s, cut):
    if s is None:
        return ref
    n = ref.shape[0]
    return ref.at[pl.ds(0, cut)] if s == 0 else ref.at[pl.ds(cut, n - cut)]


class Plane:
    def __init__(self, links, buf):
        self.links, self.buf = links, buf
        self.outer, self.inner = ("y", "z"), ("z", "y")

    def at(self, h, out, into):
        links = self.links
        out = (links.pos(self.outer[h]) + out) % 4
        into = (links.pos(self.inner[h]) + into) % 4
        return self.buf.at[0, out, into] if h == 0 else self.buf.at[1, into, out]

    def gather(self, relay=lambda view: None):
        shift, at, outer, inner = self.links.shift, self.at, self.outer, self.inner
        halves = (0, 1)
        first, far, out, onward = {}, {}, {}, {}

        def send_out(h, o):
            view = at(h, 0, o)
            out[h, o] = shift(view, view, outer[h], 1), shift(view, view, outer[h], 3)
            relay(view)

        def landed(h, o):
            for k, side in ((0, 3), (1, 1)):
                out[h, o][k].wait_recv()
                view = at(h, side, o)
                if (o in (0, 3)) == (side == 3):
                    onward[h, o] = shift(view, view, outer[h], 1 if side == 3 else 3)
                relay(view)

        for h in halves:
            view = at(h, 0, 0)
            first[h] = shift(view, view, inner[h], 1), shift(view, view, inner[h], 3)
        for h in halves:
            send_out(h, 0)
        yield
        for h in halves:
            first[h][0].wait_recv()
            view = at(h, 0, 3)
            far[h] = shift(view, view, inner[h], 1)
            send_out(h, 3)
            first[h][1].wait_recv()
            send_out(h, 1)
        yield
        for h in halves:
            landed(h, 0)
        for h in halves:
            far[h].wait_recv()
            send_out(h, 2)
        yield
        for o in (3, 1):
            for h in halves:
                landed(h, o)
        yield
        for h in halves:
            landed(h, 2)
        yield
        for o in (0, 3, 1, 2):
            for h in halves:
                onward[h, o].wait_recv()
                relay(at(h, 2, o))
        yield

    def reduce(self, land):
        shift, at, outer, inner = self.links.shift, self.at, self.outer, self.inner
        order = (2, 3, 1, 0)
        early, direct, late, last = {}, {}, {}, {}

        def way(o):
            return 1 if o in (2, 3) else 3

        for o in order:
            for h in (0, 1):
                w = way(o)
                early[h, o] = shift(at(h, 2, o), land.at[h, o], outer[h], w)
                direct[h, o] = shift(at(h, 4 - w, o), land.at[h, 4 + o], outer[h], 4 - w)
        yield
        for o in order:
            for h in (0, 1):
                w = way(o)
                early[h, o].wait_recv()
                view = at(h, w, o)
                view[...] += land[h, o]
                late[h, o] = shift(view, land.at[h, 8 + o], outer[h], w)
            if o == 3:
                yield
        yield
        for o in order:
            for h in (0, 1):
                direct[h, o].wait_recv()
                late[h, o].wait_recv()
                view = at(h, 0, o)
                total = view[...] + land[h, 4 + o] + land[h, 8 + o]
                if o == 1:
                    last[h, 2].wait_recv()
                    total += land[h, 12]
                view[...] = total
                if o == 2:
                    last[h, 2] = shift(view, land.at[h, 12], inner[h], 1)
                if o == 3:
                    last[h, 3] = shift(view, land.at[h, 14], inner[h], 3)
                if o == 1:
                    last[h, 1] = shift(view, land.at[h, 13], inner[h], 1)
            yield
        for h in (0, 1):
            last[h, 1].wait_recv()
            last[h, 3].wait_recv()
            view = at(h, 0, 0)
            view[...] += land[h, 13] + land[h, 14]
        yield


class Line:
    def __init__(self, links, buf):
        c = links.c
        self.links, self.buf = links, buf
        self.ring = Ring(links, "x", lambda i, s: rows_of(buf.at[i, c], s, 16))

    def gather(self):
        for name in ("gather_1", "gather_2", "gather_3"):
            getattr(self.ring, name)()
            yield
        view = self.buf.at[:, self.links.c]
        copy = self.links.core(view, view)
        yield
        copy.wait_recv()
        yield

    def reduce(self, pair, small):
        rows = self.buf.shape[2]

        def land(k, way, s):
            n = (16, rows - 16)[s]
            return small.at[way, pl.ds(0 if k == 0 else (16 if s == 0 else 32), n)]

        copy = self.links.core(self.buf.at[:, 1 - self.links.c], pair)
        yield
        copy.wait_recv()
        view = self.buf.at[:, self.links.c]
        view[...] += pair[...]
        self.ring.reduce_1(land)
        yield
        self.ring.reduce_2()
        yield
        self.ring.reduce_3()
        yield


def together(*runs):
    runs = list(runs)
    while runs:
        runs = [run for run in runs if next(run, "end") != "end"]


def to_lanes(column):
    n = column.shape[0]
    wide = jnp.broadcast_to(column, (n, 128)).T
    rows = [wide[:1, 128 * i : 128 * (i + 1)] for i in range(n // 128)]
    return jnp.concatenate(rows + [jnp.zeros((8 - len(rows), 128), F32)], axis=0)


def as_row(packed, n):
    return jnp.concatenate([packed[i : i + 1] for i in range(n // 128)], axis=1)


def main_kernel(
    rows_ref, local_ref, rounded, chosen0, spot_ref, weight_ref, texts_ref,
    loss_ref, gn_ref, gw_ref, gt_ref,
    near_in, far_in, spread, spread_t, wh, wl,
    npart, nland, fpart, fpair, fsmall,
    units, cols, spart, sland, tpart, tpair, tsmall,
    row_in, col_in, loss_dev, loss_grp, slices_out, slices, pre_all, pre_stack, g_far,
    gpart, gpair, gx, gfull, chosen,
    send_sem, recv_sem,
):
    links = Links(send_sem, recv_sem)
    g, d, x, c, y, z = links.g, links.d, links.x, links.c, links.y, links.z
    sel_dev, feat = texts_ref.shape
    half = feat // 2
    nodes_dev = rounded.shape[0]
    block = near_in.shape[3]
    nb = nodes_dev // block
    total_sel = sel_dev * NG * ND
    rows_all = ND * sel_dev
    cols_all = NG * sel_dev
    takes = [slice(h * half, (h + 1) * half) for h in (0, 1)]

    barrier = pltpu.get_barrier_semaphore()
    for i in range(1, ND):
        pl.semaphore_signal(barrier, inc=1, device_id=(g, (d + i) % ND), device_id_type=MESH)
    for i in range(1, NG):
        pl.semaphore_signal(barrier, inc=1, device_id=((g + i) % NG, d), device_id_type=MESH)

    texts = texts_ref[...]
    text_norm = jnp.sqrt(jnp.sum(texts * texts, axis=1, keepdims=True) + EPS)
    unit_texts = texts / text_norm
    cols[x, c] = unit_texts
    near_in[:2, d] = jnp.zeros((2, sel_dev, block), BF16)
    near_in[2, d] = rows_ref[2, d]
    far_in[:, g] = jnp.zeros((3, sel_dev, block), BF16)
    pl.semaphore_wait(barrier, ND + NG - 2)

    near_copies = links.all_dev(lambda e: rows_ref.at[:, e], near_in.at[:, d])
    far_copies = links.all_grp(lambda e: rows_ref.at[:, ND + e], far_in.at[:, g])
    text_run = Line(links, cols).gather()
    next(text_run)
    hi, lo = split(weight_ref[...])
    wh[...] = hi
    wl[...] = lo

    def expand(into, rows):
        tag = rows[2].astype(F32)[:, :1]
        second = jnp.floor(tag * (1.0 / nb) + 0.01)
        first = tag - second * nb
        for q, which in ((0, first), (1, second)):
            for b in range(nb):
                spread[q, into, :, b * block : (b + 1) * block] = jnp.where(
                    which == float(b), rows[q].astype(F32), 0.0
                ).astype(BF16)

    arrived(near_copies)
    for p in range(ND):
        expand(p, near_in[:, p])
    spread[0, d] = local_ref[0]
    spread[1, d] = local_ref[1]
    flat = (rows_all, nb * block)
    s0, s1 = spread[0, :ND].reshape(flat), spread[1, :ND].reshape(flat)
    for h in (0, 1):
        table = rounded[:, takes[h]]
        npart[h] = (dot(s0, table) + dot(s1, table)).reshape(4, 4, sel_dev, half)
    near_run = Plane(links, npart).reduce(nland)
    next(near_run)
    arrived(far_copies)
    for p in range(NG):
        expand(ND + p, far_in[:, p])
    flat = (cols_all, nb * block)
    s0, s1 = spread[0, ND:].reshape(flat), spread[1, ND:].reshape(flat)
    fpart[...] = (dot(s0, rounded[...]) + dot(s1, rounded[...])).reshape(4, 2, sel_dev, feat)
    far_run = Line(links, fpart).reduce(fpair, fsmall)
    next(far_run)
    next(near_run)
    next(far_run)
    next(near_run)
    together(near_run, far_run, text_run)

    far_sum = fpart[x, c]
    for h in (0, 1):
        chosen[:, takes[h]] = chosen0[:, takes[h]] + npart[h, y, z] + far_sum[:, takes[h]]
    picked = chosen[...]
    picked_parts = split(picked)
    before = dot3(picked_parts, (wh[...], wl[...]))
    curve = 0.5 * (1.0 + lax.erf(before * ROOT_HALF))
    hidden = before * curve
    node_norm = jnp.sqrt(jnp.sum(hidden * hidden, axis=1, keepdims=True) + EPS)
    unit_nodes = hidden / node_norm
    for h in (0, 1):
        units[h, y, z] = unit_nodes[:, takes[h]]
    unit_run = Plane(links, units).gather()
    next(unit_run)
    col_parts = split(cols[...].reshape(cols_all, feat))
    text_halves = [tuple(v[:, takes[h]] for v in col_parts) for h in (0, 1)]
    next(unit_run)
    next(unit_run)
    lane = lax.broadcasted_iota(jnp.int32, (8, cols_all), 1)
    ids = ((lane // sel_dev * ND + d) * sel_dev + lane % sel_dev)[:1]
    tags = near_in[2].reshape(rows_all, block).astype(F32)
    target = (tags[:, 1:2] * 64.0 + tags[:, 2:3] == ids.astype(F32)).astype(F32)
    wide = jnp.concatenate(
        [v.astype(F32) for v in (*picked_parts, picked_parts[0])] + [jnp.zeros_like(picked)], axis=0
    )
    slices_out[...] = wide.T.astype(BF16).reshape(slices_out.shape)
    slices[d] = slices_out[d]
    together(unit_run)
    slice_copies = links.all_dev(lambda e: slices_out.at[e], slices.at[d])

    unit_parts = [split(units[h].reshape(rows_all, half)) for h in (0, 1)]
    scores = dot3(unit_parts[0], text_halves[0], 1, 1) + dot3(unit_parts[1], text_halves[1], 1, 1)
    scores = SCALE * scores
    exps = jnp.exp(scores)
    row_in[d] = to_lanes(jnp.sum(exps, axis=1, keepdims=True))
    row_copies = links.all_dev(lambda e: row_in.at[d], row_in.at[d])
    col_sum = jnp.sum(exps, axis=0, keepdims=True)
    col_in[g] = jnp.broadcast_to(col_sum, (8, cols_all))
    col_copies = links.all_grp(lambda e: col_in.at[g], col_in.at[g])
    positive = jnp.sum(jnp.sum(target * scores, axis=1, keepdims=True), axis=0, keepdims=True)
    arrived(col_copies)
    col_total = jnp.sum(col_in[...], axis=0)[:1]
    arrived(row_copies)
    row_total = as_row(jnp.sum(row_in[...], axis=0), rows_all)
    row_recip = jnp.broadcast_to(1.0 / row_total, (128, rows_all)).T[:, :1]
    col_recip = 1.0 / col_total
    slope = 0.5 * exps * (row_recip + col_recip) - target
    slope_parts = split(slope)
    for h in (0, 1):
        spart[h] = dot3(slope_parts, text_halves[h]).reshape(4, 4, sel_dev, half)
    node_run = Plane(links, spart).reduce(sland)
    next(node_run)
    log_rows = jnp.sum(jnp.log(row_total), axis=1, keepdims=True)
    log_cols = jnp.sum(jnp.log(col_total), axis=1, keepdims=True)
    part = (log_rows / ND + log_cols / NG) / (2.0 * total_sel) - positive / total_sel
    loss_dev[d] = jnp.broadcast_to(part, (8, 128))
    for h in (0, 1):
        grown = dot3(slope_parts, unit_parts[h], 0, 0)
        tpart[:, :, :, takes[h]] = grown.reshape(4, 2, sel_dev, half)
    next(node_run)
    text_run = Line(links, tpart).reduce(tpair, tsmall)
    next(text_run)
    loss_copies = links.all_dev(lambda e: loss_dev.at[d], loss_dev.at[d])
    next(node_run)
    together(node_run, text_run)

    node_dir = SCALE * jnp.concatenate([spart[0, y, z], spart[1, y, z]], axis=1)
    node_back = (
        node_dir - unit_nodes * jnp.sum(unit_nodes * node_dir, axis=1, keepdims=True)
    ) / node_norm
    pre_grad = node_back * (curve + before * jnp.exp(-0.5 * before * before) * INV_ROOT_TWO_PI)
    for h in (0, 1):
        pre_all[h, y, z] = pre_grad[:, takes[h]]
    pre_run = Plane(links, pre_all).gather()
    next(pre_run)
    row_grads = dot3(split(pre_grad), (wh[...], wl[...]), 1, 1)
    g_far[x, c] = row_grads.astype(BF16)
    far_run = Line(links, g_far).gather()
    next(far_run)
    next(pre_run)
    arrived(loss_copies)
    loss_grp[g] = jnp.sum(loss_dev[...], axis=0)
    loss_copies = links.all_grp(lambda e: loss_grp.at[g], loss_grp.at[g])
    next(pre_run)
    next(far_run)
    some = 128 // sel_dev
    for q in (0, 1):
        for i in range(NPEER // some):
            rows = spread[q, i * some : (i + 1) * some].reshape(128, nb * block)
            spread_t[q, :, i * 128 : (i + 1) * 128] = rows.astype(F32).T.astype(BF16)
    next(pre_run)
    arrived(slice_copies)
    together(pre_run, far_run)

    pre_parts = []
    for h in (0, 1):
        hi, lo = split(pre_all[h].reshape(rows_all, half))
        pre_parts.append((hi, lo))
        for i, v in enumerate((hi, hi, lo, hi)):
            pre_stack[h, :, i] = v.reshape(ND, sel_dev, half)
        piece = 0.0
        for p in range(ND):
            piece += dot(slices[p], pre_stack[h, p].reshape(4 * sel_dev, half))
        gpart[:, h] = piece.reshape(2, piece.shape[0] // 2, half)
    core_copy = links.core(gpart.at[1 - c], gpair)
    group_grads = dot3(pre_parts[0], (wh[:, takes[0]], wl[:, takes[0]]), 1, 1)
    group_grads += dot3(pre_parts[1], (wh[:, takes[1]], wl[:, takes[1]]), 1, 1)
    group_grads = group_grads.astype(BF16)
    core_copy.wait_recv()
    gx[x] = gpart[c] + gpair[...]
    copies = [links.shift(gx.at[x], gx.at[x], "x", i) for i in (1, 2, 3)]

    spot = lax.broadcasted_iota(jnp.int32, (sel_dev, nodes_dev), 1)
    hot = (spot_ref[:, :1] == spot).astype(F32).astype(BF16)
    top, mid = split(row_grads)
    low = (row_grads - top.astype(F32) - mid.astype(F32)).astype(BF16)

    def node_grads(h):
        take = takes[h]
        near = group_grads[:, take]
        far = g_far[:, :, :, take].reshape(cols_all, half)
        total = dot(spread_t[0, :, :rows_all], near) + dot(spread_t[1, :, :rows_all], near)
        total += dot(spread_t[0, :, rows_all:], far) + dot(spread_t[1, :, rows_all:], far)
        total += dot(hot, top[:, take], 0, 0) + dot(hot, mid[:, take], 0, 0)
        gn_ref[:, take] = total + dot(hot, low[:, take], 0, 0)

    node_grads(0)
    arrived(copies)
    gfull[c, :, y, z] = gx[0] + gx[1] + gx[2] + gx[3]
    crossings = []
    weight_run = Plane(links, gfull.at[c]).gather(lambda view: crossings.append(links.core(view, view)))
    next(weight_run)
    node_grads(1)
    next(weight_run)
    text_dir = SCALE * tpart[x, c]
    gt_ref[...] = (
        text_dir - unit_texts * jnp.sum(unit_texts * text_dir, axis=1, keepdims=True)
    ) / text_norm
    arrived(loss_copies)
    loss_ref[...] = jnp.sum(loss_grp[...], axis=0)[:1, :1]
    together(weight_run)
    arrived(crossings)
    deep = gfull.shape[4]
    for e in range(ND):
        for core in (0, 1):
            for h in (0, 1):
                start = (2 * e + core) * deep
                gw_ref[start : start + deep, takes[h]] = gfull[core, h, e // 4, e % 4]
    for copy in links.copies:
        copy.wait_send()


def shards(node_features, tiles, tile_list, weight, texts, selected, pairing):
    device = lax.axis_index("grp") * ND + lax.axis_index("dev")
    tile_dev, block = tiles.shape[0], tiles.shape[1]
    nodes_dev, feat = node_features.shape
    sel_dev = selected.shape[0]
    nb = nodes_dev // block
    half = feat // 2
    deep = feat // 32
    my_list = lax.dynamic_slice_in_dim(tile_list, device * tile_dev, tile_dev, 0).reshape(-1)
    vmem = pl.BlockSpec(memory_space=pltpu.VMEM)
    smem = pl.BlockSpec(memory_space=pltpu.SMEM)
    made = pl.pallas_call(
        prep_kernel,
        out_shape=(
            jax.ShapeDtypeStruct((3, NPEER + 1, sel_dev, block), BF16),
            jax.ShapeDtypeStruct((2, sel_dev, nb * block), BF16),
            jax.ShapeDtypeStruct((nodes_dev, feat), BF16),
            jax.ShapeDtypeStruct((sel_dev, feat), F32),
            jax.ShapeDtypeStruct((sel_dev, block), jnp.int32),
        ),
        in_specs=[smem, smem, smem, vmem, vmem],
        out_specs=(vmem,) * 5,
        scratch_shapes=[
            pltpu.VMEM((nb, sel_dev, block), F32),
            pltpu.VMEM((nb, sel_dev, block), BF16),
            pltpu.VMEM((sel_dev, block), jnp.int32),
            pltpu.SMEM((NPEER + 1,), jnp.int32),
            pltpu.SMEM((NPEER + 1,), jnp.int32),
        ],
        compiler_params=pltpu.CompilerParams(vmem_limit_bytes=24 * 2**20),
    )(my_list, selected, pairing, tiles, node_features)

    def f32(*shape):
        return pltpu.VMEM(shape, F32)

    def bf16(*shape):
        return pltpu.VMEM(shape, BF16)

    plane = f32(2, 4, 4, sel_dev, half)
    landing = f32(2, 15, sel_dev, half)
    line = [f32(4, 2, sel_dev, feat), f32(4, sel_dev, feat), f32(2, 16 + sel_dev, feat)]
    loss, grad_nodes, grad_weight, grad_texts = pl.pallas_call(
        main_kernel,
        out_shape=(
            jax.ShapeDtypeStruct((1, 1), F32),
            jax.ShapeDtypeStruct((nodes_dev, feat), F32),
            jax.ShapeDtypeStruct((feat, feat), F32),
            jax.ShapeDtypeStruct((sel_dev, feat), F32),
        ),
        in_specs=[vmem] * 7,
        out_specs=(vmem,) * 4,
        scratch_shapes=[
            bf16(3, ND, sel_dev, block),
            bf16(3, NG, sel_dev, block),
            bf16(2, NPEER, sel_dev, nb * block),
            bf16(2, nb * block, NPEER * sel_dev),
            bf16(feat, feat),
            bf16(feat, feat),
            plane, landing, *line,
            plane, f32(4, 2, sel_dev, feat),
            plane, landing, *line,
            f32(ND, 8, 128),
            f32(NG, 8, NG * sel_dev),
            f32(ND, 8, 128),
            f32(NG, 8, 128),
            bf16(ND, 2 * deep, 4 * sel_dev),
            bf16(ND, 2 * deep, 4 * sel_dev),
            plane,
            bf16(2, ND, 4, sel_dev, half),
            bf16(4, 2, sel_dev, feat),
            f32(2, 2, deep, half),
            f32(2, deep, half),
            f32(4, 2, deep, half),
            f32(2, 2, 4, 4, deep, half),
            f32(sel_dev, feat),
            pltpu.SemaphoreType.DMA((SEMS,)),
            pltpu.SemaphoreType.DMA((SEMS,)),
        ],
        compiler_params=pltpu.CompilerParams(
            collective_id=0, has_side_effects=True, vmem_limit_bytes=60 * 2**20
        ),
    )(*made, weight, texts)
    return loss.reshape(()), grad_nodes, grad_weight, grad_texts


def solution(mesh):
    both = ("grp", "dev")
    placed = (
        P(both, None),
        P(both, None, None),
        P(),
        P(),
        P(both, None),
        P(both),
        P(both),
    )
    return jax.shard_map(
        shards,
        mesh=mesh,
        in_specs=placed,
        out_specs=(P(), P(both, None), P(), P(both, None)),
        check_vma=False,
    )
```

```python
import functools

import jax
import jax.numpy as jnp
from jax import lax
from jax.experimental import pallas as pl
from jax.experimental.pallas import tpu as pltpu
from jax.sharding import PartitionSpec as P

MESH = pl.DeviceIdType.MESH
CAP = 2
SCALE = 1.0 / 0.07
EPS = 1e-06
ROOT_HALF = 0.7071067811865476
INV_ROOT_TWO_PI = 0.3989422804014327
F32 = jnp.float32
BF16 = jnp.bfloat16
NG, ND = 8, 16
NPEER = NG + ND
SEMS = 384


def split(value):
    hi = value.astype(BF16)
    return hi, (value - hi.astype(F32)).astype(BF16)


def dot(a, b, ca=1, cb=0):
    return lax.dot_general(a, b, (((ca,), (cb,)), ((), ())), preferred_element_type=F32)


def dot3(a, b, ca=1, cb=0):
    return dot(a[0], b[0], ca, cb) + (dot(a[0], b[1], ca, cb) + dot(a[1], b[0], ca, cb))


def prep_kernel(
    list_ref, sel_ref, pair_ref, tiles_ref, nodes_ref,
    rows_ref, local_ref, rounded_ref, chosen_ref, spot_ref,
    acc, onehot, column, count, meta,
):
    g, d = lax.axis_index("grp"), lax.axis_index("dev")
    device = g * ND + d
    n_tiles, block = tiles_ref.shape[0], tiles_ref.shape[1]
    sel_dev = sel_ref.shape[0]
    nodes_dev = nodes_ref.shape[0]
    nb = nodes_dev // block
    rows_ref[...] = jnp.zeros_like(rows_ref)
    acc[...] = jnp.zeros_like(acc)
    for k in range(sel_dev):
        own = sel_ref[k] - device * nodes_dev
        spot_ref[pl.ds(k, 1), :] = jnp.full((1, block), own, jnp.int32)
        column[pl.ds(k, 1), :] = jnp.full((1, block), pair_ref[k], jnp.int32)
        chosen_ref[pl.ds(k, 1), :] = nodes_ref[pl.ds(own, 1), :]
    lane = lax.broadcasted_iota(jnp.int32, (sel_dev, block), 1)
    sel = spot_ref[...]
    for b in range(nb):
        onehot[b] = (sel == lane + b * block).astype(F32).astype(BF16)
    for p in range(NPEER + 1):
        count[p] = 0
        meta[p] = 0
    for t in range(n_tiles):
        row_block = list_ref[2 * t] - device * nb
        col = list_ref[2 * t + 1]
        owner = col // nb
        col_block = col - owner * nb
        og = owner // ND
        od = owner - og * ND
        local = owner == device
        peer = jnp.where(local, NPEER, jnp.where(og == g, od, ND + og))
        rank = jnp.minimum(count[peer], 1)
        count[peer] = rank + 1
        meta[peer] = meta[peer] + col_block * jnp.where(rank == 0, 1, nb)
        picked = dot(onehot[row_block], tiles_ref[t])
        rows_ref[rank, peer] = picked.astype(BF16)
        acc[col_block] += picked * local.astype(F32)
    pair = column[...]
    high = pair // 64
    tag = jnp.where(lane == 1, high, pair - high * 64)
    for p in range(NPEER):
        rows_ref[2, p] = jnp.where(lane == 0, meta[p], tag).astype(F32).astype(BF16)
    rows_ref[2, d] = jnp.where(lane == 0, 0, tag).astype(F32).astype(BF16)
    for b in range(nb):
        hi, lo = split(acc[b])
        local_ref[0, :, b * block : (b + 1) * block] = hi
        local_ref[1, :, b * block : (b + 1) * block] = lo
    rounded_ref[...] = nodes_ref[...].astype(BF16)


class Links:
    def __init__(self, send_sem, recv_sem):
        self.g, self.d = lax.axis_index("grp"), lax.axis_index("dev")
        self.x, self.c = self.g // 2, self.g % 2
        self.y, self.z = self.d // 4, self.d % 4
        self.send_sem, self.recv_sem = send_sem, recv_sem
        self.used, self.copies = 0, []

    def to(self, src, dst, grp=None, dev=None):
        k = self.used
        self.used += 1
        copy = pltpu.make_async_remote_copy(
            src_ref=src,
            dst_ref=dst,
            send_sem=self.send_sem.at[k],
            recv_sem=self.recv_sem.at[k],
            device_id=(self.g if grp is None else grp, self.d if dev is None else dev),
            device_id_type=MESH,
        )
        copy.start()
        self.copies.append(copy)
        return copy

    def pos(self, axis):
        return {"x": self.x, "y": self.y, "z": self.z}[axis]

    def shift(self, src, dst, axis, step):
        if axis == "x":
            return self.to(src, dst, grp=(self.x + step) % 4 * 2 + self.c)
        if axis == "y":
            return self.to(src, dst, dev=(self.y + step) % 4 * 4 + self.z)
        return self.to(src, dst, dev=self.y * 4 + (self.z + step) % 4)

    def core(self, src, dst):
        return self.to(src, dst, grp=self.x * 2 + 1 - self.c)

    def all_dev(self, src, dst):
        out = []
        for i in range(1, ND):
            e = (self.d + i) % ND
            out.append(self.to(src(e), dst, dev=e))
        return out

    def all_grp(self, src, dst):
        out = []
        for i in range(1, NG):
            e = (self.g + i) % NG
            out.append(self.to(src(e), dst, grp=e))
        return out


def arrived(copies):
    for copy in copies:
        copy.wait_recv()


class Plane:
    def __init__(self, links, buf):
        self.links, self.buf = links, buf
        self.outer, self.inner = ("y", "z"), ("z", "y")

    def at(self, h, out, into):
        links = self.links
        out = (links.pos(self.outer[h]) + out) % 4
        if into is None:
            return self.buf.at[0, out] if h == 0 else self.buf.at[1, :, out]
        into = (links.pos(self.inner[h]) + into) % 4
        return self.buf.at[0, out, into] if h == 0 else self.buf.at[1, into, out]

    def gather(self, cross=None):
        shift, at, outer, inner = self.links.shift, self.at, self.outer, self.inner
        near, away = {}, {}

        def send_out(h, o):
            view = at(h, 0, o)
            for i in (2, 1, 3):
                away[h, i, o] = shift(view, view, outer[h], i)

        for h in (0, 1):
            view = at(h, 0, 0)
            for i in (2, 1, 3):
                near[h, i] = shift(view, view, inner[h], i)
        for h in (0, 1):
            send_out(h, 0)
        yield
        for i in (2, 1, 3):
            for h in (0, 1):
                near[h, i].wait_recv()
                send_out(h, 4 - i)
        if cross:
            for h in (0, 1):
                cross(at(h, 0, None))
        yield
        for i in (2, 1, 3):
            for h in (0, 1):
                for o in (0, 2, 3, 1):
                    away[h, i, o].wait_recv()
                if cross:
                    cross(at(h, 4 - i, None))
        yield

    def reduce(self, land):
        shift, at, outer, inner = self.links.shift, self.at, self.outer, self.inner
        order = (2, 1, 3, 0)
        away, near = {}, {}
        for o in order:
            for h in (0, 1):
                for i in (2, 1, 3):
                    away[h, i, o] = shift(at(h, i, o), land.at[h, 4 * (i - 1) + o], outer[h], i)
        yield
        for o in order:
            for h in (0, 1):
                for i in (2, 1, 3):
                    away[h, i, o].wait_recv()
                view = at(h, 0, o)
                view[...] += land[h, o] + land[h, 4 + o] + land[h, 8 + o]
                if o:
                    near[h, o] = shift(view, land.at[h, 11 + o], inner[h], o)
            yield
        for h in (0, 1):
            for o in (2, 1, 3):
                near[h, o].wait_recv()
            view = at(h, 0, 0)
            view[...] += land[h, 12] + land[h, 13] + land[h, 14]
        yield


class Line:
    def __init__(self, links, buf):
        self.links, self.buf = links, buf

    def gather(self):
        links = self.links
        x, c = links.x, links.c
        own = self.buf.at[x, c]
        ways = [links.shift(own, own, "x", i) for i in (2, 1, 3)]
        crossed = [links.core(own, own)]
        yield
        for i, way in zip((2, 1, 3), ways):
            way.wait_recv()
            view = self.buf.at[(x + 4 - i) % 4, c]
            crossed.append(links.core(view, view))
        yield
        arrived(crossed)
        yield

    def reduce(self, pair, land):
        links = self.links
        x, c = links.x, links.c
        copy = links.core(self.buf.at[:, 1 - c], pair)
        yield
        copy.wait_recv()
        view = self.buf.at[:, c]
        view[...] += pair[...]
        ways = [
            links.shift(self.buf.at[(x + i) % 4, c], land.at[i - 1], "x", i) for i in (2, 1, 3)
        ]
        yield
        arrived(ways)
        view = self.buf.at[x, c]
        view[...] += land[0] + land[1] + land[2]
        yield


def together(*runs):
    runs = list(runs)
    while runs:
        runs = [run for run in runs if next(run, "end") != "end"]


def to_lanes(column):
    n = column.shape[0]
    wide = jnp.broadcast_to(column, (n, 128)).T
    rows = [wide[:1, 128 * i : 128 * (i + 1)] for i in range(n // 128)]
    return jnp.concatenate(rows + [jnp.zeros((8 - len(rows), 128), F32)], axis=0)


def as_row(packed, n):
    return jnp.concatenate([packed[i : i + 1] for i in range(n // 128)], axis=1)


def main_kernel(
    rows_ref, local_ref, rounded, chosen0, spot_ref, weight_ref, texts_ref,
    loss_ref, gn_ref, gw_ref, gt_ref,
    near_in, far_in, spread, spread_t, wh, wl,
    npart, nland, fpart, fpair, fsmall,
    units, cols, spart, sland, tpart, tpair, tsmall,
    row_in, col_in, loss_dev, loss_grp, slices_out, slices, pre_all, pre_stack, g_far,
    gpart, gpair, gx, gfull, chosen,
    send_sem, recv_sem,
):
    links = Links(send_sem, recv_sem)
    g, d, x, c, y, z = links.g, links.d, links.x, links.c, links.y, links.z
    sel_dev, feat = texts_ref.shape
    half = feat // 2
    nodes_dev = rounded.shape[0]
    block = near_in.shape[3]
    nb = nodes_dev // block
    total_sel = sel_dev * NG * ND
    rows_all = ND * sel_dev
    cols_all = NG * sel_dev
    takes = [slice(h * half, (h + 1) * half) for h in (0, 1)]

    barrier = pltpu.get_barrier_semaphore()
    for i in range(1, ND):
        pl.semaphore_signal(barrier, inc=1, device_id=(g, (d + i) % ND), device_id_type=MESH)
    for i in range(1, NG):
        pl.semaphore_signal(barrier, inc=1, device_id=((g + i) % NG, d), device_id_type=MESH)

    texts = texts_ref[...]
    text_norm = jnp.sqrt(jnp.sum(texts * texts, axis=1, keepdims=True) + EPS)
    unit_texts = texts / text_norm
    cols[x, c] = unit_texts
    near_in[:2, d] = jnp.zeros((2, sel_dev, block), BF16)
    near_in[2, d] = rows_ref[2, d]
    far_in[:, g] = jnp.zeros((3, sel_dev, block), BF16)
    pl.semaphore_wait(barrier, ND + NG - 2)

    near_copies = links.all_dev(lambda e: rows_ref.at[:, e], near_in.at[:, d])
    far_copies = links.all_grp(lambda e: rows_ref.at[:, ND + e], far_in.at[:, g])
    text_run = Line(links, cols).gather()
    next(text_run)
    hi, lo = split(weight_ref[...])
    wh[...] = hi
    wl[...] = lo

    def expand(into, rows):
        tag = rows[2].astype(F32)[:, :1]
        second = jnp.floor(tag * (1.0 / nb) + 0.01)
        first = tag - second * nb
        for q, which in ((0, first), (1, second)):
            for b in range(nb):
                spread[q, into, :, b * block : (b + 1) * block] = jnp.where(
                    which == float(b), rows[q].astype(F32), 0.0
                ).astype(BF16)

    arrived(near_copies)
    for p in range(ND):
        expand(p, near_in[:, p])
    spread[0, d] = local_ref[0]
    spread[1, d] = local_ref[1]
    flat = (rows_all, nb * block)
    s0, s1 = spread[0, :ND].reshape(flat), spread[1, :ND].reshape(flat)
    for h in (0, 1):
        table = rounded[:, takes[h]]
        npart[h] = (dot(s0, table) + dot(s1, table)).reshape(4, 4, sel_dev, half)
    near_run = Plane(links, npart).reduce(nland)
    next(near_run)
    arrived(far_copies)
    for p in range(NG):
        expand(ND + p, far_in[:, p])
    flat = (cols_all, nb * block)
    s0, s1 = spread[0, ND:].reshape(flat), spread[1, ND:].reshape(flat)
    fpart[...] = (dot(s0, rounded[...]) + dot(s1, rounded[...])).reshape(4, 2, sel_dev, feat)
    far_run = Line(links, fpart).reduce(fpair, fsmall)
    next(far_run)
    next(far_run)
    together(near_run, far_run, text_run)

    far_sum = fpart[x, c]
    for h in (0, 1):
        chosen[:, takes[h]] = chosen0[:, takes[h]] + npart[h, y, z] + far_sum[:, takes[h]]
    picked = chosen[...]
    picked_parts = split(picked)
    before = dot3(picked_parts, (wh[...], wl[...]))
    curve = 0.5 * (1.0 + lax.erf(before * ROOT_HALF))
    hidden = before * curve
    node_norm = jnp.sqrt(jnp.sum(hidden * hidden, axis=1, keepdims=True) + EPS)
    unit_nodes = hidden / node_norm
    for h in (0, 1):
        units[h, y, z] = unit_nodes[:, takes[h]]
    unit_run = Plane(links, units).gather()
    next(unit_run)
    col_parts = split(cols[...].reshape(cols_all, feat))
    text_halves = [tuple(v[:, takes[h]] for v in col_parts) for h in (0, 1)]
    next(unit_run)
    lane = lax.broadcasted_iota(jnp.int32, (8, cols_all), 1)
    ids = ((lane // sel_dev * ND + d) * sel_dev + lane % sel_dev)[:1]
    tags = near_in[2].reshape(rows_all, block).astype(F32)
    target = (tags[:, 1:2] * 64.0 + tags[:, 2:3] == ids.astype(F32)).astype(F32)
    wide = jnp.concatenate(
        [v.astype(F32) for v in (*picked_parts, picked_parts[0])] + [jnp.zeros_like(picked)], axis=0
    )
    slices_out[...] = wide.T.astype(BF16).reshape(slices_out.shape)
    slices[d] = slices_out[d]
    together(unit_run)

    unit_parts = [split(units[h].reshape(rows_all, half)) for h in (0, 1)]
    scores = dot3(unit_parts[0], text_halves[0], 1, 1) + dot3(unit_parts[1], text_halves[1], 1, 1)
    scores = SCALE * scores
    exps = jnp.exp(scores)
    row_in[d] = to_lanes(jnp.sum(exps, axis=1, keepdims=True))
    row_copies = links.all_dev(lambda e: row_in.at[d], row_in.at[d])
    col_sum = jnp.sum(exps, axis=0, keepdims=True)
    col_in[g] = jnp.broadcast_to(col_sum, (8, cols_all))
    col_copies = links.all_grp(lambda e: col_in.at[g], col_in.at[g])
    slice_copies = links.all_dev(lambda e: slices_out.at[e], slices.at[d])
    positive = jnp.sum(jnp.sum(target * scores, axis=1, keepdims=True), axis=0, keepdims=True)
    arrived(col_copies)
    col_total = jnp.sum(col_in[...], axis=0)[:1]
    arrived(row_copies)
    row_total = as_row(jnp.sum(row_in[...], axis=0), rows_all)
    row_recip = jnp.broadcast_to(1.0 / row_total, (128, rows_all)).T[:, :1]
    col_recip = 1.0 / col_total
    slope = 0.5 * exps * (row_recip + col_recip) - target
    slope_parts = split(slope)
    for h in (0, 1):
        spart[h] = dot3(slope_parts, text_halves[h]).reshape(4, 4, sel_dev, half)
    node_run = Plane(links, spart).reduce(sland)
    next(node_run)
    log_rows = jnp.sum(jnp.log(row_total), axis=1, keepdims=True)
    log_cols = jnp.sum(jnp.log(col_total), axis=1, keepdims=True)
    part = (log_rows / ND + log_cols / NG) / (2.0 * total_sel) - positive / total_sel
    loss_dev[d] = jnp.broadcast_to(part, (8, 128))
    for h in (0, 1):
        grown = dot3(slope_parts, unit_parts[h], 0, 0)
        tpart[:, :, :, takes[h]] = grown.reshape(4, 2, sel_dev, half)
    text_run = Line(links, tpart).reduce(tpair, tsmall)
    next(text_run)
    loss_copies = links.all_dev(lambda e: loss_dev.at[d], loss_dev.at[d])
    together(node_run, text_run)

    node_dir = SCALE * jnp.concatenate([spart[0, y, z], spart[1, y, z]], axis=1)
    node_back = (
        node_dir - unit_nodes * jnp.sum(unit_nodes * node_dir, axis=1, keepdims=True)
    ) / node_norm
    pre_grad = node_back * (curve + before * jnp.exp(-0.5 * before * before) * INV_ROOT_TWO_PI)
    for h in (0, 1):
        pre_all[h, y, z] = pre_grad[:, takes[h]]
    pre_run = Plane(links, pre_all).gather()
    next(pre_run)
    row_grads = dot3(split(pre_grad), (wh[...], wl[...]), 1, 1)
    g_far[x, c] = row_grads.astype(BF16)
    far_run = Line(links, g_far).gather()
    next(far_run)
    next(pre_run)
    next(far_run)
    arrived(loss_copies)
    loss_grp[g] = jnp.sum(loss_dev[...], axis=0)
    loss_copies = links.all_grp(lambda e: loss_grp.at[g], loss_grp.at[g])
    some = 128 // sel_dev
    for q in (0, 1):
        for i in range(NPEER // some):
            rows = spread[q, i * some : (i + 1) * some].reshape(128, nb * block)
            spread_t[q, :, i * 128 : (i + 1) * 128] = rows.astype(F32).T.astype(BF16)
    arrived(slice_copies)
    together(pre_run, far_run)

    pre_parts = []
    for h in (0, 1):
        hi, lo = split(pre_all[h].reshape(rows_all, half))
        pre_parts.append((hi, lo))
        for i, v in enumerate((hi, hi, lo, hi)):
            pre_stack[h, :, i] = v.reshape(ND, sel_dev, half)
        piece = 0.0
        for p in range(ND):
            piece += dot(slices[p], pre_stack[h, p].reshape(4 * sel_dev, half))
        gpart[:, h] = piece.reshape(2, piece.shape[0] // 2, half)
    core_copy = links.core(gpart.at[1 - c], gpair)
    group_grads = dot3(pre_parts[0], (wh[:, takes[0]], wl[:, takes[0]]), 1, 1)
    group_grads += dot3(pre_parts[1], (wh[:, takes[1]], wl[:, takes[1]]), 1, 1)
    group_grads = group_grads.astype(BF16)
    core_copy.wait_recv()
    gx[x] = gpart[c] + gpair[...]
    copies = [links.shift(gx.at[x], gx.at[x], "x", i) for i in (1, 2, 3)]

    spot = lax.broadcasted_iota(jnp.int32, (sel_dev, nodes_dev), 1)
    hot = (spot_ref[:, :1] == spot).astype(F32).astype(BF16)
    top, mid = split(row_grads)
    low = (row_grads - top.astype(F32) - mid.astype(F32)).astype(BF16)

    def node_grads(h):
        take = takes[h]
        near = group_grads[:, take]
        far = g_far[:, :, :, take].reshape(cols_all, half)
        total = dot(spread_t[0, :, :rows_all], near) + dot(spread_t[1, :, :rows_all], near)
        total += dot(spread_t[0, :, rows_all:], far) + dot(spread_t[1, :, rows_all:], far)
        total += dot(hot, top[:, take], 0, 0) + dot(hot, mid[:, take], 0, 0)
        gn_ref[:, take] = total + dot(hot, low[:, take], 0, 0)

    node_grads(0)
    arrived(copies)
    gfull[c, :, y, z] = gx[0] + gx[1] + gx[2] + gx[3]
    crossings = []
    weight_run = Plane(links, gfull.at[c]).gather(lambda view: crossings.append(links.core(view, view)))
    next(weight_run)
    next(weight_run)
    node_grads(1)
    text_dir = SCALE * tpart[x, c]
    gt_ref[...] = (
        text_dir - unit_texts * jnp.sum(unit_texts * text_dir, axis=1, keepdims=True)
    ) / text_norm
    arrived(loss_copies)
    loss_ref[...] = jnp.sum(loss_grp[...], axis=0)[:1, :1]
    together(weight_run)
    arrived(crossings)
    deep = gfull.shape[4]
    for e in range(ND):
        for core in (0, 1):
            for h in (0, 1):
                start = (2 * e + core) * deep
                gw_ref[start : start + deep, takes[h]] = gfull[core, h, e // 4, e % 4]
    for copy in links.copies:
        copy.wait_send()


def shards(node_features, tiles, tile_list, weight, texts, selected, pairing):
    device = lax.axis_index("grp") * ND + lax.axis_index("dev")
    tile_dev, block = tiles.shape[0], tiles.shape[1]
    nodes_dev, feat = node_features.shape
    sel_dev = selected.shape[0]
    nb = nodes_dev // block
    half = feat // 2
    deep = feat // 32
    my_list = lax.dynamic_slice_in_dim(tile_list, device * tile_dev, tile_dev, 0).reshape(-1)
    vmem = pl.BlockSpec(memory_space=pltpu.VMEM)
    smem = pl.BlockSpec(memory_space=pltpu.SMEM)
    made = pl.pallas_call(
        prep_kernel,
        out_shape=(
            jax.ShapeDtypeStruct((3, NPEER + 1, sel_dev, block), BF16),
            jax.ShapeDtypeStruct((2, sel_dev, nb * block), BF16),
            jax.ShapeDtypeStruct((nodes_dev, feat), BF16),
            jax.ShapeDtypeStruct((sel_dev, feat), F32),
            jax.ShapeDtypeStruct((sel_dev, block), jnp.int32),
        ),
        in_specs=[smem, smem, smem, vmem, vmem],
        out_specs=(vmem,) * 5,
        scratch_shapes=[
            pltpu.VMEM((nb, sel_dev, block), F32),
            pltpu.VMEM((nb, sel_dev, block), BF16),
            pltpu.VMEM((sel_dev, block), jnp.int32),
            pltpu.SMEM((NPEER + 1,), jnp.int32),
            pltpu.SMEM((NPEER + 1,), jnp.int32),
        ],
        compiler_params=pltpu.CompilerParams(vmem_limit_bytes=60 * 2**20),
    )(my_list, selected, pairing, tiles, node_features)

    def f32(*shape):
        return pltpu.VMEM(shape, F32)

    def bf16(*shape):
        return pltpu.VMEM(shape, BF16)

    plane = f32(2, 4, 4, sel_dev, half)
    landing = f32(2, 15, sel_dev, half)
    line = [f32(4, 2, sel_dev, feat), f32(4, sel_dev, feat), f32(3, sel_dev, feat)]
    loss, grad_nodes, grad_weight, grad_texts = pl.pallas_call(
        main_kernel,
        out_shape=(
            jax.ShapeDtypeStruct((1, 1), F32),
            jax.ShapeDtypeStruct((nodes_dev, feat), F32),
            jax.ShapeDtypeStruct((feat, feat), F32),
            jax.ShapeDtypeStruct((sel_dev, feat), F32),
        ),
        in_specs=[vmem] * 7,
        out_specs=(vmem,) * 4,
        scratch_shapes=[
            bf16(3, ND, sel_dev, block),
            bf16(3, NG, sel_dev, block),
            bf16(2, NPEER, sel_dev, nb * block),
            bf16(2, nb * block, NPEER * sel_dev),
            bf16(feat, feat),
            bf16(feat, feat),
            plane, landing, *line,
            plane, f32(4, 2, sel_dev, feat),
            plane, landing, *line,
            f32(ND, 8, 128),
            f32(NG, 8, NG * sel_dev),
            f32(ND, 8, 128),
            f32(NG, 8, 128),
            bf16(ND, 2 * deep, 4 * sel_dev),
            bf16(ND, 2 * deep, 4 * sel_dev),
            plane,
            bf16(2, ND, 4, sel_dev, half),
            bf16(4, 2, sel_dev, feat),
            f32(2, 2, deep, half),
            f32(2, deep, half),
            f32(4, 2, deep, half),
            f32(2, 2, 4, 4, deep, half),
            f32(sel_dev, feat),
            pltpu.SemaphoreType.DMA((SEMS,)),
            pltpu.SemaphoreType.DMA((SEMS,)),
        ],
        compiler_params=pltpu.CompilerParams(
            collective_id=0, has_side_effects=True, vmem_limit_bytes=60 * 2**20
        ),
    )(*made, weight, texts)
    return loss.reshape(()), grad_nodes, grad_weight, grad_texts


def solution(mesh):
    both = ("grp", "dev")
    placed = (
        P(both, None),
        P(both, None, None),
        P(),
        P(),
        P(both, None),
        P(both),
        P(both),
    )
    return jax.shard_map(
        shards,
        mesh=mesh,
        in_specs=placed,
        out_specs=(P(), P(both, None), P(), P(both, None)),
        check_vma=False,
    )
```

```python
import functools

import jax
import jax.numpy as jnp
from jax import lax
from jax.experimental import pallas as pl
from jax.experimental.pallas import tpu as pltpu
from jax.sharding import PartitionSpec as P

MESH = pl.DeviceIdType.MESH
CAP = 2
SCALE = 1.0 / 0.07
EPS = 1e-06
ROOT_HALF = 0.7071067811865476
INV_ROOT_TWO_PI = 0.3989422804014327
F32 = jnp.float32
BF16 = jnp.bfloat16
NG, ND = 8, 16
NPEER = NG + ND
SEMS = 384


def split(value):
    hi = value.astype(BF16)
    return hi, (value - hi.astype(F32)).astype(BF16)


def dot(a, b, ca=1, cb=0):
    return lax.dot_general(a, b, (((ca,), (cb,)), ((), ())), preferred_element_type=F32)


def dot3(a, b, ca=1, cb=0):
    return dot(a[0], b[0], ca, cb) + (dot(a[0], b[1], ca, cb) + dot(a[1], b[0], ca, cb))


def prep_kernel(
    list_ref, sel_ref, pair_ref, tiles_ref,
    rows_ref, local_ref, spot_ref, own_ref,
    acc, onehot, column, count, meta, window, sem,
):
    g, d = lax.axis_index("grp"), lax.axis_index("dev")
    device = g * ND + d
    n_tiles, block = tiles_ref.shape[0], tiles_ref.shape[1]
    wide = window.shape[1]
    first = jnp.minimum(device * n_tiles // 128 * 128, list_ref.shape[1] - wide)
    first = pl.multiple_of(first, 128)
    fetch = pltpu.make_async_copy(list_ref.at[:, pl.ds(first, wide)], window, sem)
    fetch.start()
    sel_dev = sel_ref.shape[0]
    nb = local_ref.shape[2] // block
    nodes_dev = nb * block
    rows_ref[...] = jnp.zeros_like(rows_ref)
    acc[...] = jnp.zeros_like(acc)
    for k in range(sel_dev):
        own = sel_ref[k] - device * nodes_dev
        own_ref[k] = own
        spot_ref[pl.ds(k, 1), :] = jnp.full((1, block), own, jnp.int32)
        column[pl.ds(k, 1), :] = jnp.full((1, block), pair_ref[k], jnp.int32)
    lane = lax.broadcasted_iota(jnp.int32, (sel_dev, block), 1)
    sel = spot_ref[...]
    for b in range(nb):
        onehot[b] = (sel == lane + b * block).astype(F32).astype(BF16)
    for p in range(NPEER + 1):
        count[p] = 0
        meta[p] = 0
    fetch.wait()
    skip = device * n_tiles - first
    for t in range(n_tiles):
        row_block = window[0, skip + t] - device * nb
        col = window[1, skip + t]
        owner = col // nb
        col_block = col - owner * nb
        og = owner // ND
        od = owner - og * ND
        local = owner == device
        peer = jnp.where(local, NPEER, jnp.where(og == g, od, ND + og))
        rank = jnp.minimum(count[peer], 1)
        count[peer] = rank + 1
        meta[peer] = meta[peer] + col_block * jnp.where(rank == 0, 1, nb)
        picked = dot(onehot[row_block], tiles_ref[t])
        rows_ref[rank, peer] = picked.astype(BF16)
        acc[col_block] += picked * local.astype(F32)
    pair = column[...]
    high = pair // 64
    tag = jnp.where(lane == 1, high, pair - high * 64)
    for p in range(NPEER):
        rows_ref[2, p] = jnp.where(lane == 0, meta[p], tag).astype(F32).astype(BF16)
    rows_ref[2, d] = jnp.where(lane == 0, 0, tag).astype(F32).astype(BF16)
    for b in range(nb):
        hi, lo = split(acc[b])
        local_ref[0, :, b * block : (b + 1) * block] = hi
        local_ref[1, :, b * block : (b + 1) * block] = lo


class Links:
    def __init__(self, send_sem, recv_sem):
        self.g, self.d = lax.axis_index("grp"), lax.axis_index("dev")
        self.x, self.c = self.g // 2, self.g % 2
        self.y, self.z = self.d // 4, self.d % 4
        self.send_sem, self.recv_sem = send_sem, recv_sem
        self.used, self.copies = 0, []

    def to(self, src, dst, grp=None, dev=None):
        k = self.used
        self.used += 1
        copy = pltpu.make_async_remote_copy(
            src_ref=src,
            dst_ref=dst,
            send_sem=self.send_sem.at[k],
            recv_sem=self.recv_sem.at[k],
            device_id=(self.g if grp is None else grp, self.d if dev is None else dev),
            device_id_type=MESH,
        )
        copy.start()
        self.copies.append(copy)
        return copy

    def pos(self, axis):
        return {"x": self.x, "y": self.y, "z": self.z}[axis]

    def shift(self, src, dst, axis, step):
        if axis == "x":
            return self.to(src, dst, grp=(self.x + step) % 4 * 2 + self.c)
        if axis == "y":
            return self.to(src, dst, dev=(self.y + step) % 4 * 4 + self.z)
        return self.to(src, dst, dev=self.y * 4 + (self.z + step) % 4)

    def core(self, src, dst):
        return self.to(src, dst, grp=self.x * 2 + 1 - self.c)

    def all_dev(self, src, dst):
        out = []
        for i in range(1, ND):
            e = (self.d + i) % ND
            out.append(self.to(src(e), dst, dev=e))
        return out

    def all_grp(self, src, dst):
        out = []
        for i in range(1, NG):
            e = (self.g + i) % NG
            out.append(self.to(src(e), dst, grp=e))
        return out


def arrived(copies):
    for copy in copies:
        copy.wait_recv()


class Plane:
    def __init__(self, links, buf):
        self.links, self.buf = links, buf
        self.outer, self.inner = ("y", "z"), ("z", "y")

    def at(self, h, out, into):
        links = self.links
        out = (links.pos(self.outer[h]) + out) % 4
        if into is None:
            return self.buf.at[0, out] if h == 0 else self.buf.at[1, :, out]
        into = (links.pos(self.inner[h]) + into) % 4
        return self.buf.at[0, out, into] if h == 0 else self.buf.at[1, into, out]

    def gather(self, cross=None):
        shift, at, outer, inner = self.links.shift, self.at, self.outer, self.inner
        near, away = {}, {}

        def send_out(h, o):
            view = at(h, 0, o)
            for i in (2, 1, 3):
                away[h, i, o] = shift(view, view, outer[h], i)

        for h in (0, 1):
            view = at(h, 0, 0)
            for i in (2, 1, 3):
                near[h, i] = shift(view, view, inner[h], i)
        for h in (0, 1):
            send_out(h, 0)
        yield
        for i in (2, 1, 3):
            for h in (0, 1):
                near[h, i].wait_recv()
                send_out(h, 4 - i)
        if cross:
            for h in (0, 1):
                cross(at(h, 0, None))
        yield
        for i in (2, 1, 3):
            for h in (0, 1):
                for o in (0, 2, 3, 1):
                    away[h, i, o].wait_recv()
                if cross:
                    cross(at(h, 4 - i, None))
        yield

    def reduce(self, land):
        shift, at, outer, inner = self.links.shift, self.at, self.outer, self.inner
        order = (2, 1, 3, 0)
        away, near = {}, {}
        for h in (0, 1):
            for o in order:
                for i in (2, 1, 3):
                    away[h, i, o] = shift(at(h, i, o), land.at[h, 4 * (i - 1) + o], outer[h], i)
            yield
        for o in order:
            for h in (0, 1):
                for i in (2, 1, 3):
                    away[h, i, o].wait_recv()
                view = at(h, 0, o)
                view[...] += land[h, o] + land[h, 4 + o] + land[h, 8 + o]
                if o:
                    near[h, o] = shift(view, land.at[h, 11 + o], inner[h], o)
            yield
        for h in (0, 1):
            for o in (2, 1, 3):
                near[h, o].wait_recv()
            view = at(h, 0, 0)
            view[...] += land[h, 12] + land[h, 13] + land[h, 14]
        yield


class Line:
    def __init__(self, links, buf):
        self.links, self.buf = links, buf

    def gather(self):
        links = self.links
        x, c = links.x, links.c
        own = self.buf.at[x, c]
        ways = [links.shift(own, own, "x", i) for i in (2, 1, 3)]
        crossed = [links.core(own, own)]
        yield
        for i, way in zip((2, 1, 3), ways):
            way.wait_recv()
            view = self.buf.at[(x + 4 - i) % 4, c]
            crossed.append(links.core(view, view))
        yield
        arrived(crossed)
        yield

    def reduce(self, pair, land):
        links = self.links
        x, c = links.x, links.c
        copy = links.core(self.buf.at[:, 1 - c], pair)
        yield
        copy.wait_recv()
        view = self.buf.at[:, c]
        view[...] += pair[...]
        ways = [
            links.shift(self.buf.at[(x + i) % 4, c], land.at[i - 1], "x", i) for i in (2, 1, 3)
        ]
        yield
        arrived(ways)
        view = self.buf.at[x, c]
        view[...] += land[0] + land[1] + land[2]
        yield


def together(*runs):
    runs = list(runs)
    while runs:
        runs = [run for run in runs if next(run, "end") != "end"]


def to_lanes(column):
    n = column.shape[0]
    wide = jnp.broadcast_to(column, (n, 128)).T
    rows = [wide[:1, 128 * i : 128 * (i + 1)] for i in range(n // 128)]
    return jnp.concatenate(rows + [jnp.zeros((8 - len(rows), 128), F32)], axis=0)


def as_row(packed, n):
    return jnp.concatenate([packed[i : i + 1] for i in range(n // 128)], axis=1)


def main_kernel(
    rows_ref, local_ref, spot_ref, own_ref, nodes_hbm, weight_hbm, texts_ref,
    loss_ref, gn_out, gw_out, gt_ref,
    nodes_ref, weight_ref, rounded, gn_ref,
    near_in, far_in, spread, spread_t, wh, wl,
    npart, nland, fpart, fpair, fsmall,
    units, cols, spart, sland, tpart, tpair, tsmall,
    row_in, col_in, loss_dev, loss_grp, slices_out, slices, pre_all, pre_stack, g_far,
    gpart, gpair, gx, gfull, chosen,
    send_sem, recv_sem, local_sem,
):
    links = Links(send_sem, recv_sem)
    g, d, x, c, y, z = links.g, links.d, links.x, links.c, links.y, links.z
    sel_dev, feat = texts_ref.shape
    half = feat // 2
    nodes_dev = nodes_ref.shape[0]
    block = near_in.shape[3]
    nb = nodes_dev // block
    total_sel = sel_dev * NG * ND
    rows_all = ND * sel_dev
    cols_all = NG * sel_dev
    takes = [slice(h * half, (h + 1) * half) for h in (0, 1)]

    barrier = pltpu.get_barrier_semaphore()
    for i in range(1, ND):
        pl.semaphore_signal(barrier, inc=1, device_id=(g, (d + i) % ND), device_id_type=MESH)
    for i in range(1, NG):
        pl.semaphore_signal(barrier, inc=1, device_id=((g + i) % NG, d), device_id_type=MESH)

    nodes_copy = pltpu.make_async_copy(nodes_hbm, nodes_ref, local_sem.at[0])
    weight_copy = pltpu.make_async_copy(weight_hbm, weight_ref, local_sem.at[1])
    nodes_copy.start()
    weight_copy.start()

    texts = texts_ref[...]
    text_norm = jnp.sqrt(jnp.sum(texts * texts, axis=1, keepdims=True) + EPS)
    unit_texts = texts / text_norm
    cols[x, c] = unit_texts
    near_in[:2, d] = jnp.zeros((2, sel_dev, block), BF16)
    near_in[2, d] = rows_ref[2, d]
    far_in[:, g] = jnp.zeros((3, sel_dev, block), BF16)
    pl.semaphore_wait(barrier, ND + NG - 2)

    near_copies = links.all_dev(lambda e: rows_ref.at[:, e], near_in.at[:, d])
    far_copies = links.all_grp(lambda e: rows_ref.at[:, ND + e], far_in.at[:, g])
    text_run = Line(links, cols).gather()
    next(text_run)
    nodes_copy.wait()
    rounded[...] = nodes_ref[...].astype(BF16)
    for k in range(sel_dev):
        chosen[pl.ds(k, 1), :] = nodes_ref[pl.ds(own_ref[k], 1), :]
    weight_copy.wait()
    hi, lo = split(weight_ref[...])
    wh[...] = hi
    wl[...] = lo

    def expand(into, rows):
        tag = rows[2].astype(F32)[:, :1]
        second = jnp.floor(tag * (1.0 / nb) + 0.01)
        first = tag - second * nb
        for q, which in ((0, first), (1, second)):
            for b in range(nb):
                spread[q, into, :, b * block : (b + 1) * block] = jnp.where(
                    which == float(b), rows[q].astype(F32), 0.0
                ).astype(BF16)

    arrived(near_copies)
    for p in range(ND):
        expand(p, near_in[:, p])
    spread[0, d] = local_ref[0]
    spread[1, d] = local_ref[1]
    flat = (rows_all, nb * block)
    s0, s1 = spread[0, :ND].reshape(flat), spread[1, :ND].reshape(flat)
    near_run = Plane(links, npart).reduce(nland)
    for h in (0, 1):
        table = rounded[:, takes[h]]
        npart[h] = (dot(s0, table) + dot(s1, table)).reshape(4, 4, sel_dev, half)
        next(near_run)
    arrived(far_copies)
    for p in range(NG):
        expand(ND + p, far_in[:, p])
    flat = (cols_all, nb * block)
    s0, s1 = spread[0, ND:].reshape(flat), spread[1, ND:].reshape(flat)
    fpart[...] = (dot(s0, rounded[...]) + dot(s1, rounded[...])).reshape(4, 2, sel_dev, feat)
    far_run = Line(links, fpart).reduce(fpair, fsmall)
    next(far_run)
    next(far_run)
    together(near_run, far_run, text_run)

    far_sum = fpart[x, c]
    for h in (0, 1):
        chosen[:, takes[h]] += npart[h, y, z] + far_sum[:, takes[h]]
    picked = chosen[...]
    picked_parts = split(picked)
    before = dot3(picked_parts, (wh[...], wl[...]))
    curve = 0.5 * (1.0 + lax.erf(before * ROOT_HALF))
    hidden = before * curve
    node_norm = jnp.sqrt(jnp.sum(hidden * hidden, axis=1, keepdims=True) + EPS)
    unit_nodes = hidden / node_norm
    for h in (0, 1):
        units[h, y, z] = unit_nodes[:, takes[h]]
    unit_run = Plane(links, units).gather()
    next(unit_run)
    col_parts = split(cols[...].reshape(cols_all, feat))
    text_halves = [tuple(v[:, takes[h]] for v in col_parts) for h in (0, 1)]
    next(unit_run)
    lane = lax.broadcasted_iota(jnp.int32, (8, cols_all), 1)
    ids = ((lane // sel_dev * ND + d) * sel_dev + lane % sel_dev)[:1]
    tags = near_in[2].reshape(rows_all, block).astype(F32)
    target = (tags[:, 1:2] * 64.0 + tags[:, 2:3] == ids.astype(F32)).astype(F32)
    wide = jnp.concatenate(
        [v.astype(F32) for v in (*picked_parts, picked_parts[0])] + [jnp.zeros_like(picked)], axis=0
    )
    slices_out[...] = wide.T.astype(BF16).reshape(slices_out.shape)
    slices[d] = slices_out[d]
    together(unit_run)

    unit_parts = [split(units[h].reshape(rows_all, half)) for h in (0, 1)]
    scores = dot3(unit_parts[0], text_halves[0], 1, 1) + dot3(unit_parts[1], text_halves[1], 1, 1)
    scores = SCALE * scores
    exps = jnp.exp(scores)
    row_in[d] = to_lanes(jnp.sum(exps, axis=1, keepdims=True))
    row_copies = links.all_dev(lambda e: row_in.at[d], row_in.at[d])
    col_sum = jnp.sum(exps, axis=0, keepdims=True)
    col_in[g] = jnp.broadcast_to(col_sum, (8, cols_all))
    col_copies = links.all_grp(lambda e: col_in.at[g], col_in.at[g])
    slice_copies = links.all_dev(lambda e: slices_out.at[e], slices.at[d])
    positive = jnp.sum(jnp.sum(target * scores, axis=1, keepdims=True), axis=0, keepdims=True)
    arrived(col_copies)
    col_total = jnp.sum(col_in[...], axis=0)[:1]
    arrived(row_copies)
    row_total = as_row(jnp.sum(row_in[...], axis=0), rows_all)
    row_recip = jnp.broadcast_to(1.0 / row_total, (128, rows_all)).T[:, :1]
    col_recip = 1.0 / col_total
    slope = 0.5 * exps * (row_recip + col_recip) - target
    slope_parts = split(slope)
    node_run = Plane(links, spart).reduce(sland)
    for h in (0, 1):
        spart[h] = dot3(slope_parts, text_halves[h]).reshape(4, 4, sel_dev, half)
        next(node_run)
    log_rows = jnp.sum(jnp.log(row_total), axis=1, keepdims=True)
    log_cols = jnp.sum(jnp.log(col_total), axis=1, keepdims=True)
    part = (log_rows / ND + log_cols / NG) / (2.0 * total_sel) - positive / total_sel
    loss_dev[d] = jnp.broadcast_to(part, (8, 128))
    for h in (0, 1):
        grown = dot3(slope_parts, unit_parts[h], 0, 0)
        tpart[:, :, :, takes[h]] = grown.reshape(4, 2, sel_dev, half)
    text_run = Line(links, tpart).reduce(tpair, tsmall)
    next(text_run)
    loss_copies = links.all_dev(lambda e: loss_dev.at[d], loss_dev.at[d])
    together(node_run, text_run)

    node_dir = SCALE * jnp.concatenate([spart[0, y, z], spart[1, y, z]], axis=1)
    node_back = (
        node_dir - unit_nodes * jnp.sum(unit_nodes * node_dir, axis=1, keepdims=True)
    ) / node_norm
    pre_grad = node_back * (curve + before * jnp.exp(-0.5 * before * before) * INV_ROOT_TWO_PI)
    for h in (0, 1):
        pre_all[h, y, z] = pre_grad[:, takes[h]]
    pre_run = Plane(links, pre_all).gather()
    next(pre_run)
    row_grads = dot3(split(pre_grad), (wh[...], wl[...]), 1, 1)
    g_far[x, c] = row_grads.astype(BF16)
    far_run = Line(links, g_far).gather()
    next(far_run)
    next(pre_run)
    next(far_run)
    arrived(loss_copies)
    loss_grp[g] = jnp.sum(loss_dev[...], axis=0)
    loss_copies = links.all_grp(lambda e: loss_grp.at[g], loss_grp.at[g])
    some = 128 // sel_dev
    for q in (0, 1):
        for i in range(NPEER // some):
            rows = spread[q, i * some : (i + 1) * some].reshape(128, nb * block)
            spread_t[q, :, i * 128 : (i + 1) * 128] = rows.astype(F32).T.astype(BF16)
    arrived(slice_copies)
    together(pre_run, far_run)

    pre_parts = []
    for h in (0, 1):
        hi, lo = split(pre_all[h].reshape(rows_all, half))
        pre_parts.append((hi, lo))
        for i, v in enumerate((hi, hi, lo, hi)):
            pre_stack[h, :, i] = v.reshape(ND, sel_dev, half)
        piece = 0.0
        for p in range(ND):
            piece += dot(slices[p], pre_stack[h, p].reshape(4 * sel_dev, half))
        gpart[:, h] = piece.reshape(2, piece.shape[0] // 2, half)
    core_copy = links.core(gpart.at[1 - c], gpair)
    group_grads = dot3(pre_parts[0], (wh[:, takes[0]], wl[:, takes[0]]), 1, 1)
    group_grads += dot3(pre_parts[1], (wh[:, takes[1]], wl[:, takes[1]]), 1, 1)
    group_grads = group_grads.astype(BF16)
    core_copy.wait_recv()
    gx[x] = gpart[c] + gpair[...]
    copies = [links.shift(gx.at[x], gx.at[x], "x", i) for i in (1, 2, 3)]

    spot = lax.broadcasted_iota(jnp.int32, (sel_dev, nodes_dev), 1)
    hot = (spot_ref[:, :1] == spot).astype(F32).astype(BF16)
    top, mid = split(row_grads)
    low = (row_grads - top.astype(F32) - mid.astype(F32)).astype(BF16)

    def node_grads(h):
        take = takes[h]
        near = group_grads[:, take]
        far = g_far[:, :, :, take].reshape(cols_all, half)
        total = dot(spread_t[0, :, :rows_all], near) + dot(spread_t[1, :, :rows_all], near)
        total += dot(spread_t[0, :, rows_all:], far) + dot(spread_t[1, :, rows_all:], far)
        total += dot(hot, top[:, take], 0, 0) + dot(hot, mid[:, take], 0, 0)
        gn_ref[:, take] = total + dot(hot, low[:, take], 0, 0)
        copy = pltpu.make_async_copy(gn_ref.at[:, take], gn_out.at[:, take], local_sem.at[2 + h])
        copy.start()
        return copy

    out_copies = [node_grads(0)]
    arrived(copies)
    gfull[c, :, y, z] = gx[0] + gx[1] + gx[2] + gx[3]
    crossings = []
    weight_run = Plane(links, gfull.at[c]).gather(lambda view: crossings.append(links.core(view, view)))
    next(weight_run)
    next(weight_run)
    out_copies.append(node_grads(1))
    text_dir = SCALE * tpart[x, c]
    gt_ref[...] = (
        text_dir - unit_texts * jnp.sum(unit_texts * text_dir, axis=1, keepdims=True)
    ) / text_norm
    arrived(loss_copies)
    loss_ref[...] = jnp.sum(loss_grp[...], axis=0)[:1, :1]
    together(weight_run)
    for i, core in enumerate((c, 1 - c)):
        if i:
            arrived(crossings)
        copy = pltpu.make_async_copy(gfull.at[core], gw_out.at[core], local_sem.at[4 + i])
        copy.start()
        out_copies.append(copy)
    for copy in links.copies:
        copy.wait_send()
    for copy in out_copies:
        copy.wait()


def finish_kernel(gn_in, gw_in, gt_in, gn_out, gw_out, gt_out, sem):
    half = gw_in.shape[5]
    rows = gn_in.shape[0] // 4
    pairs = [(gn_in.at[pl.ds(i * rows, rows)], gn_out.at[pl.ds(i * rows, rows)]) for i in range(4)]
    for core in (0, 1):
        for h in (0, 1):
            for y in range(4):
                take = pl.ds(h * half, half)
                pairs.append((gw_in.at[core, h, y], gw_out.at[y, :, core, :, take]))
    pairs.append((gt_in, gt_out))
    copies = [pltpu.make_async_copy(a, b, sem.at[i]) for i, (a, b) in enumerate(pairs)]
    for copy in copies:
        copy.start()
    for copy in copies:
        copy.wait()


def shards(node_features, tiles, tile_list, weight, texts, selected, pairing):
    block = tiles.shape[1]
    nodes_dev, feat = node_features.shape
    sel_dev = selected.shape[0]
    nb = nodes_dev // block
    half = feat // 2
    deep = feat // 32
    vmem = pl.BlockSpec(memory_space=pltpu.VMEM)
    smem = pl.BlockSpec(memory_space=pltpu.SMEM)
    hbm = pl.BlockSpec(memory_space=pl.ANY)
    made = pl.pallas_call(
        prep_kernel,
        out_shape=(
            jax.ShapeDtypeStruct((3, NPEER + 1, sel_dev, block), BF16),
            jax.ShapeDtypeStruct((2, sel_dev, nb * block), BF16),
            jax.ShapeDtypeStruct((sel_dev, block), jnp.int32),
            jax.ShapeDtypeStruct((sel_dev,), jnp.int32),
        ),
        in_specs=[hbm, smem, smem, vmem],
        out_specs=(vmem, vmem, vmem, smem),
        scratch_shapes=[
            pltpu.VMEM((nb, sel_dev, block), F32),
            pltpu.VMEM((nb, sel_dev, block), BF16),
            pltpu.VMEM((sel_dev, block), jnp.int32),
            pltpu.SMEM((NPEER + 1,), jnp.int32),
            pltpu.SMEM((NPEER + 1,), jnp.int32),
            pltpu.SMEM((2, 256), jnp.int32),
            pltpu.SemaphoreType.DMA,
        ],
        compiler_params=pltpu.CompilerParams(vmem_limit_bytes=60 * 2**20),
    )(tile_list.T, selected, pairing, tiles)

    def f32(*shape):
        return pltpu.VMEM(shape, F32)

    def bf16(*shape):
        return pltpu.VMEM(shape, BF16)

    plane = f32(2, 4, 4, sel_dev, half)
    landing = f32(2, 15, sel_dev, half)
    line = [f32(4, 2, sel_dev, feat), f32(4, sel_dev, feat), f32(3, sel_dev, feat)]
    loss, *results = pl.pallas_call(
        main_kernel,
        out_shape=(
            jax.ShapeDtypeStruct((1, 1), F32),
            jax.ShapeDtypeStruct((nodes_dev, feat), F32),
            jax.ShapeDtypeStruct((2, 2, 4, 4, deep, half), F32),
            jax.ShapeDtypeStruct((sel_dev, feat), F32),
        ),
        in_specs=[vmem, vmem, vmem, smem, hbm, hbm, vmem],
        out_specs=(vmem, hbm, hbm, vmem),
        scratch_shapes=[
            f32(nodes_dev, feat),
            f32(feat, feat),
            bf16(nodes_dev, feat),
            f32(nodes_dev, feat),
            bf16(3, ND, sel_dev, block),
            bf16(3, NG, sel_dev, block),
            bf16(2, NPEER, sel_dev, nb * block),
            bf16(2, nb * block, NPEER * sel_dev),
            bf16(feat, feat),
            bf16(feat, feat),
            plane, landing, *line,
            plane, f32(4, 2, sel_dev, feat),
            plane, landing, *line,
            f32(ND, 8, 128),
            f32(NG, 8, NG * sel_dev),
            f32(ND, 8, 128),
            f32(NG, 8, 128),
            bf16(ND, 2 * deep, 4 * sel_dev),
            bf16(ND, 2 * deep, 4 * sel_dev),
            plane,
            bf16(2, ND, 4, sel_dev, half),
            bf16(4, 2, sel_dev, feat),
            f32(2, 2, deep, half),
            f32(2, deep, half),
            f32(4, 2, deep, half),
            f32(2, 2, 4, 4, deep, half),
            f32(sel_dev, feat),
            pltpu.SemaphoreType.DMA((SEMS,)),
            pltpu.SemaphoreType.DMA((SEMS,)),
            pltpu.SemaphoreType.DMA((6,)),
        ],
        compiler_params=pltpu.CompilerParams(
            collective_id=0, has_side_effects=True, vmem_limit_bytes=60 * 2**20
        ),
    )(*made, node_features, weight, texts)
    grad_nodes, grad_weight, grad_texts = pl.pallas_call(
        finish_kernel,
        out_shape=(
            jax.ShapeDtypeStruct((nodes_dev, feat), F32),
            jax.ShapeDtypeStruct((4, 4, 2, deep, feat), F32),
            jax.ShapeDtypeStruct((sel_dev, feat), F32),
        ),
        in_specs=[hbm] * 3,
        out_specs=(hbm,) * 3,
        scratch_shapes=[pltpu.SemaphoreType.DMA((21,))],
        compiler_params=pltpu.CompilerParams(vmem_limit_bytes=60 * 2**20),
    )(*results)
    return loss.reshape(()), grad_nodes, grad_weight.reshape(feat, feat), grad_texts


def solution(mesh):
    both = ("grp", "dev")
    placed = (
        P(both, None),
        P(both, None, None),
        P(),
        P(),
        P(both, None),
        P(both),
        P(both),
    )
    return jax.shard_map(
        shards,
        mesh=mesh,
        in_specs=placed,
        out_specs=(P(), P(both, None), P(), P(both, None)),
        check_vma=False,
    )
```

```python
import functools

import jax
import jax.numpy as jnp
from jax import lax
from jax.experimental import pallas as pl
from jax.experimental.pallas import tpu as pltpu
from jax.sharding import PartitionSpec as P

MESH = pl.DeviceIdType.MESH
CAP = 2
SCALE = 1.0 / 0.07
EPS = 1e-06
ROOT_HALF = 0.7071067811865476
INV_ROOT_TWO_PI = 0.3989422804014327
F32 = jnp.float32
BF16 = jnp.bfloat16
NG, ND = 8, 16
NPEER = NG + ND
SEMS = 384


def split(value):
    hi = value.astype(BF16)
    return hi, (value - hi.astype(F32)).astype(BF16)


def dot(a, b, ca=1, cb=0):
    return lax.dot_general(a, b, (((ca,), (cb,)), ((), ())), preferred_element_type=F32)


def dot3(a, b, ca=1, cb=0):
    return dot(a[0], b[0], ca, cb) + (dot(a[0], b[1], ca, cb) + dot(a[1], b[0], ca, cb))


def prep_kernel(
    list_ref, sel_ref, pair_ref, tiles_ref,
    rows_ref, local_ref, spot_ref, own_ref,
    acc, onehot, column, count, meta, window, sem,
):
    g, d = lax.axis_index("grp"), lax.axis_index("dev")
    device = g * ND + d
    n_tiles, block = tiles_ref.shape[0], tiles_ref.shape[1]
    wide = window.shape[1]
    first = jnp.minimum(device * n_tiles // 128 * 128, list_ref.shape[1] - wide)
    first = pl.multiple_of(first, 128)
    fetch = pltpu.make_async_copy(list_ref.at[:, pl.ds(first, wide)], window, sem)
    fetch.start()
    sel_dev = sel_ref.shape[0]
    nb = local_ref.shape[2] // block
    nodes_dev = nb * block
    rows_ref[...] = jnp.zeros_like(rows_ref)
    acc[...] = jnp.zeros_like(acc)
    for k in range(sel_dev):
        own = sel_ref[k] - device * nodes_dev
        own_ref[k] = own
        spot_ref[pl.ds(k, 1), :] = jnp.full((1, block), own, jnp.int32)
        column[pl.ds(k, 1), :] = jnp.full((1, block), pair_ref[k], jnp.int32)
    lane = lax.broadcasted_iota(jnp.int32, (sel_dev, block), 1)
    sel = spot_ref[...]
    for b in range(nb):
        onehot[b] = (sel == lane + b * block).astype(F32).astype(BF16)
    for p in range(NPEER + 1):
        count[p] = 0
        meta[p] = 0
    fetch.wait()
    skip = device * n_tiles - first
    for t in range(n_tiles):
        row_block = window[0, skip + t] - device * nb
        col = window[1, skip + t]
        owner = col // nb
        col_block = col - owner * nb
        og = owner // ND
        od = owner - og * ND
        local = owner == device
        peer = jnp.where(local, NPEER, jnp.where(og == g, od, ND + og))
        rank = jnp.minimum(count[peer], 1)
        count[peer] = rank + 1
        meta[peer] = meta[peer] + col_block * jnp.where(rank == 0, 1, nb)
        picked = dot(onehot[row_block], tiles_ref[t])
        rows_ref[rank, peer] = picked.astype(BF16)
        acc[col_block] += picked * local.astype(F32)
    pair = column[...]
    high = pair // 64
    tag = jnp.where(lane == 1, high, pair - high * 64)
    for p in range(NPEER):
        rows_ref[2, p] = jnp.where(lane == 0, meta[p], tag).astype(F32).astype(BF16)
    rows_ref[2, d] = jnp.where(lane == 0, 0, tag).astype(F32).astype(BF16)
    for b in range(nb):
        hi, lo = split(acc[b])
        local_ref[0, :, b * block : (b + 1) * block] = hi
        local_ref[1, :, b * block : (b + 1) * block] = lo


class Links:
    def __init__(self, send_sem, recv_sem):
        self.g, self.d = lax.axis_index("grp"), lax.axis_index("dev")
        self.x, self.c = self.g // 2, self.g % 2
        self.y, self.z = self.d // 4, self.d % 4
        self.send_sem, self.recv_sem = send_sem, recv_sem
        self.used, self.copies = 0, []

    def to(self, src, dst, grp=None, dev=None):
        k = self.used
        self.used += 1
        copy = pltpu.make_async_remote_copy(
            src_ref=src,
            dst_ref=dst,
            send_sem=self.send_sem.at[k],
            recv_sem=self.recv_sem.at[k],
            device_id=(self.g if grp is None else grp, self.d if dev is None else dev),
            device_id_type=MESH,
        )
        copy.start()
        self.copies.append(copy)
        return copy

    def pos(self, axis):
        return {"x": self.x, "y": self.y, "z": self.z}[axis]

    def shift(self, src, dst, axis, step):
        if axis == "x":
            return self.to(src, dst, grp=(self.x + step) % 4 * 2 + self.c)
        if axis == "y":
            return self.to(src, dst, dev=(self.y + step) % 4 * 4 + self.z)
        return self.to(src, dst, dev=self.y * 4 + (self.z + step) % 4)

    def core(self, src, dst):
        return self.to(src, dst, grp=self.x * 2 + 1 - self.c)

    def all_dev(self, src, dst):
        out = []
        for i in range(1, ND):
            e = (self.d + i) % ND
            out.append(self.to(src(e), dst, dev=e))
        return out

    def all_grp(self, src, dst):
        out = []
        for i in range(1, NG):
            e = (self.g + i) % NG
            out.append(self.to(src(e), dst, grp=e))
        return out


def arrived(copies):
    for copy in copies:
        copy.wait_recv()


class Plane:
    def __init__(self, links, buf):
        self.links, self.buf = links, buf
        self.outer, self.inner = ("y", "z"), ("z", "y")

    def at(self, h, out, into):
        links = self.links
        out = (links.pos(self.outer[h]) + out) % 4
        if into is None:
            return self.buf.at[0, out] if h == 0 else self.buf.at[1, :, out]
        into = (links.pos(self.inner[h]) + into) % 4
        return self.buf.at[0, out, into] if h == 0 else self.buf.at[1, into, out]

    def gather(self, cross=None):
        shift, at, outer, inner = self.links.shift, self.at, self.outer, self.inner
        near, away = {}, {}

        def send_out(h, o):
            view = at(h, 0, o)
            for i in (2, 1, 3):
                away[h, i, o] = shift(view, view, outer[h], i)

        for h in (0, 1):
            view = at(h, 0, 0)
            for i in (2, 1, 3):
                near[h, i] = shift(view, view, inner[h], i)
        for h in (0, 1):
            send_out(h, 0)
        yield
        for i in (2, 1, 3):
            for h in (0, 1):
                near[h, i].wait_recv()
                send_out(h, 4 - i)
        if cross:
            for h in (0, 1):
                cross(at(h, 0, None))
        yield
        for i in (2, 1, 3):
            for h in (0, 1):
                for o in (0, 2, 3, 1):
                    away[h, i, o].wait_recv()
                if cross:
                    cross(at(h, 4 - i, None))
        yield

    def reduce(self, land):
        shift, at, outer, inner = self.links.shift, self.at, self.outer, self.inner
        order = (2, 1, 3, 0)
        away, near = {}, {}
        for h in (0, 1):
            for o in order:
                for i in (2, 1, 3):
                    away[h, i, o] = shift(at(h, i, o), land.at[h, 4 * (i - 1) + o], outer[h], i)
            yield
        for o in order:
            for h in (0, 1):
                for i in (2, 1, 3):
                    away[h, i, o].wait_recv()
                view = at(h, 0, o)
                view[...] += land[h, o] + land[h, 4 + o] + land[h, 8 + o]
                if o:
                    near[h, o] = shift(view, land.at[h, 11 + o], inner[h], o)
            yield
        for h in (0, 1):
            for o in (2, 1, 3):
                near[h, o].wait_recv()
            view = at(h, 0, 0)
            view[...] += land[h, 12] + land[h, 13] + land[h, 14]
        yield


class Line:
    def __init__(self, links, buf):
        self.links, self.buf = links, buf

    def gather(self):
        links = self.links
        x, c = links.x, links.c
        own = self.buf.at[x, c]
        ways = [links.shift(own, own, "x", i) for i in (2, 1, 3)]
        crossed = [links.core(own, own)]
        yield
        for i, way in zip((2, 1, 3), ways):
            way.wait_recv()
            view = self.buf.at[(x + 4 - i) % 4, c]
            crossed.append(links.core(view, view))
        yield
        arrived(crossed)
        yield

    def reduce(self, pair, land):
        links = self.links
        x, c = links.x, links.c
        copy = links.core(self.buf.at[:, 1 - c], pair)
        yield
        copy.wait_recv()
        view = self.buf.at[:, c]
        view[...] += pair[...]
        ways = [
            links.shift(self.buf.at[(x + i) % 4, c], land.at[i - 1], "x", i) for i in (2, 1, 3)
        ]
        yield
        arrived(ways)
        view = self.buf.at[x, c]
        view[...] += land[0] + land[1] + land[2]
        yield


def together(*runs):
    runs = list(runs)
    while runs:
        runs = [run for run in runs if next(run, "end") != "end"]


def to_lanes(column):
    n = column.shape[0]
    wide = jnp.broadcast_to(column, (n, 128)).T
    rows = [wide[:1, 128 * i : 128 * (i + 1)] for i in range(n // 128)]
    return jnp.concatenate(rows + [jnp.zeros((8 - len(rows), 128), F32)], axis=0)


def as_row(packed, n):
    return jnp.concatenate([packed[i : i + 1] for i in range(n // 128)], axis=1)


def main_kernel(
    rows_ref, local_ref, spot_ref, own_ref, nodes_hbm, weight_hbm, texts_ref,
    loss_ref, gn_out, gw_out, gt_ref,
    nodes_ref, weight_ref, rounded, gn_ref,
    near_in, far_in, spread, spread_t, wh, wl,
    npart, nland, fpart, fpair, fsmall,
    units, cols, spart, sland, tpart, tpair, tsmall,
    row_in, col_in, loss_dev, loss_grp, slices_out, slices, pre_all, pre_stack, g_far,
    gpart, gpair, gx, gfull, chosen,
    send_sem, recv_sem, local_sem,
):
    links = Links(send_sem, recv_sem)
    g, d, x, c, y, z = links.g, links.d, links.x, links.c, links.y, links.z
    sel_dev, feat = texts_ref.shape
    half = feat // 2
    nodes_dev = nodes_ref.shape[0]
    block = near_in.shape[3]
    nb = nodes_dev // block
    total_sel = sel_dev * NG * ND
    rows_all = ND * sel_dev
    cols_all = NG * sel_dev
    takes = [slice(h * half, (h + 1) * half) for h in (0, 1)]

    barrier = pltpu.get_barrier_semaphore()
    for i in range(1, ND):
        pl.semaphore_signal(barrier, inc=1, device_id=(g, (d + i) % ND), device_id_type=MESH)
    for i in range(1, NG):
        pl.semaphore_signal(barrier, inc=1, device_id=((g + i) % NG, d), device_id_type=MESH)

    nodes_copy = pltpu.make_async_copy(nodes_hbm, nodes_ref, local_sem.at[0])
    weight_copy = pltpu.make_async_copy(weight_hbm, weight_ref, local_sem.at[1])
    nodes_copy.start()
    weight_copy.start()

    texts = texts_ref[...]
    text_norm = jnp.sqrt(jnp.sum(texts * texts, axis=1, keepdims=True) + EPS)
    unit_texts = texts / text_norm
    cols[x, c] = unit_texts
    near_in[:2, d] = jnp.zeros((2, sel_dev, block), BF16)
    near_in[2, d] = rows_ref[2, d]
    far_in[:, g] = jnp.zeros((3, sel_dev, block), BF16)
    pl.semaphore_wait(barrier, ND + NG - 2)

    near_copies = links.all_dev(lambda e: rows_ref.at[:, e], near_in.at[:, d])
    far_copies = links.all_grp(lambda e: rows_ref.at[:, ND + e], far_in.at[:, g])
    text_run = Line(links, cols).gather()
    next(text_run)
    nodes_copy.wait()
    rounded[...] = nodes_ref[...].astype(BF16)
    for k in range(sel_dev):
        chosen[pl.ds(k, 1), :] = nodes_ref[pl.ds(own_ref[k], 1), :]
    weight_copy.wait()
    hi, lo = split(weight_ref[...])
    wh[...] = hi
    wl[...] = lo

    def expand(into, rows):
        tag = rows[2].astype(F32)[:, :1]
        second = jnp.floor(tag * (1.0 / nb) + 0.01)
        first = tag - second * nb
        for q, which in ((0, first), (1, second)):
            for b in range(nb):
                spread[q, into, :, b * block : (b + 1) * block] = jnp.where(
                    which == float(b), rows[q].astype(F32), 0.0
                ).astype(BF16)

    arrived(near_copies)
    for p in range(ND):
        expand(p, near_in[:, p])
    spread[0, d] = local_ref[0]
    spread[1, d] = local_ref[1]
    flat = (rows_all, nb * block)
    s0, s1 = spread[0, :ND].reshape(flat), spread[1, :ND].reshape(flat)
    near_run = Plane(links, npart).reduce(nland)
    for h in (0, 1):
        table = rounded[:, takes[h]]
        npart[h] = (dot(s0, table) + dot(s1, table)).reshape(4, 4, sel_dev, half)
        next(near_run)
    arrived(far_copies)
    for p in range(NG):
        expand(ND + p, far_in[:, p])
    flat = (cols_all, nb * block)
    s0, s1 = spread[0, ND:].reshape(flat), spread[1, ND:].reshape(flat)
    fpart[...] = (dot(s0, rounded[...]) + dot(s1, rounded[...])).reshape(4, 2, sel_dev, feat)
    far_run = Line(links, fpart).reduce(fpair, fsmall)
    next(far_run)
    next(far_run)
    together(near_run, far_run, text_run)

    far_sum = fpart[x, c]
    for h in (0, 1):
        chosen[:, takes[h]] += npart[h, y, z] + far_sum[:, takes[h]]
    picked = chosen[...]
    picked_parts = split(picked)
    before = dot3(picked_parts, (wh[...], wl[...]))
    curve = 0.5 * (1.0 + lax.erf(before * ROOT_HALF))
    hidden = before * curve
    node_norm = jnp.sqrt(jnp.sum(hidden * hidden, axis=1, keepdims=True) + EPS)
    unit_nodes = hidden / node_norm
    for h in (0, 1):
        units[h, y, z] = unit_nodes[:, takes[h]]
    unit_run = Plane(links, units).gather()
    next(unit_run)
    col_parts = split(cols[...].reshape(cols_all, feat))
    text_halves = [tuple(v[:, takes[h]] for v in col_parts) for h in (0, 1)]
    next(unit_run)
    lane = lax.broadcasted_iota(jnp.int32, (8, cols_all), 1)
    ids = ((lane // sel_dev * ND + d) * sel_dev + lane % sel_dev)[:1]
    tags = near_in[2].reshape(rows_all, block).astype(F32)
    target = (tags[:, 1:2] * 64.0 + tags[:, 2:3] == ids.astype(F32)).astype(F32)
    wide = jnp.concatenate(
        [v.astype(F32) for v in (*picked_parts, picked_parts[0])] + [jnp.zeros_like(picked)], axis=0
    )
    slices_out[...] = wide.T.astype(BF16).reshape(slices_out.shape)
    slices[d] = slices_out[d]
    together(unit_run)

    unit_parts = [split(units[h].reshape(rows_all, half)) for h in (0, 1)]
    scores = dot3(unit_parts[0], text_halves[0], 1, 1) + dot3(unit_parts[1], text_halves[1], 1, 1)
    scores = SCALE * scores
    exps = jnp.exp(scores)
    row_in[d] = to_lanes(jnp.sum(exps, axis=1, keepdims=True))
    row_copies = links.all_dev(lambda e: row_in.at[d], row_in.at[d])
    col_sum = jnp.sum(exps, axis=0, keepdims=True)
    col_in[g] = jnp.broadcast_to(col_sum, (8, cols_all))
    col_copies = links.all_grp(lambda e: col_in.at[g], col_in.at[g])
    slice_copies = links.all_dev(lambda e: slices_out.at[e], slices.at[d])
    positive = jnp.sum(jnp.sum(target * scores, axis=1, keepdims=True), axis=0, keepdims=True)
    arrived(col_copies)
    col_total = jnp.sum(col_in[...], axis=0)[:1]
    arrived(row_copies)
    row_total = as_row(jnp.sum(row_in[...], axis=0), rows_all)
    row_recip = jnp.broadcast_to(1.0 / row_total, (128, rows_all)).T[:, :1]
    col_recip = 1.0 / col_total
    slope = 0.5 * exps * (row_recip + col_recip) - target
    slope_parts = split(slope)
    node_run = Plane(links, spart).reduce(sland)
    for h in (0, 1):
        spart[h] = dot3(slope_parts, text_halves[h]).reshape(4, 4, sel_dev, half)
        next(node_run)
    log_rows = jnp.sum(jnp.log(row_total), axis=1, keepdims=True)
    log_cols = jnp.sum(jnp.log(col_total), axis=1, keepdims=True)
    part = (log_rows / ND + log_cols / NG) / (2.0 * total_sel) - positive / total_sel
    loss_dev[d] = jnp.broadcast_to(part, (8, 128))
    for h in (0, 1):
        grown = dot3(slope_parts, unit_parts[h], 0, 0)
        tpart[:, :, :, takes[h]] = grown.reshape(4, 2, sel_dev, half)
    text_run = Line(links, tpart).reduce(tpair, tsmall)
    next(text_run)
    loss_copies = links.all_dev(lambda e: loss_dev.at[d], loss_dev.at[d])
    together(node_run, text_run)

    node_dir = SCALE * jnp.concatenate([spart[0, y, z], spart[1, y, z]], axis=1)
    node_back = (
        node_dir - unit_nodes * jnp.sum(unit_nodes * node_dir, axis=1, keepdims=True)
    ) / node_norm
    pre_grad = node_back * (curve + before * jnp.exp(-0.5 * before * before) * INV_ROOT_TWO_PI)
    for h in (0, 1):
        pre_all[h, y, z] = pre_grad[:, takes[h]]
    pre_run = Plane(links, pre_all).gather()
    next(pre_run)
    row_grads = dot3(split(pre_grad), (wh[...], wl[...]), 1, 1)
    g_far[x, c] = row_grads.astype(BF16)
    far_run = Line(links, g_far).gather()
    next(far_run)
    next(pre_run)
    next(far_run)
    arrived(loss_copies)
    loss_grp[g] = jnp.sum(loss_dev[...], axis=0)
    loss_copies = links.all_grp(lambda e: loss_grp.at[g], loss_grp.at[g])
    some = 128 // sel_dev
    for q in (0, 1):
        for i in range(NPEER // some):
            rows = spread[q, i * some : (i + 1) * some].reshape(128, nb * block)
            spread_t[q, :, i * 128 : (i + 1) * 128] = rows.astype(F32).T.astype(BF16)
    arrived(slice_copies)
    together(pre_run, far_run)

    pre_parts = []
    for h in (0, 1):
        hi, lo = split(pre_all[h].reshape(rows_all, half))
        pre_parts.append((hi, lo))
        for i, v in enumerate((hi, hi, lo, hi)):
            pre_stack[h, :, i] = v.reshape(ND, sel_dev, half)
        piece = 0.0
        for p in range(ND):
            piece += dot(slices[p], pre_stack[h, p].reshape(4 * sel_dev, half))
        gpart[:, h] = piece.reshape(2, piece.shape[0] // 2, half)
    core_copy = links.core(gpart.at[1 - c], gpair)
    group_grads = dot3(pre_parts[0], (wh[:, takes[0]], wl[:, takes[0]]), 1, 1)
    group_grads += dot3(pre_parts[1], (wh[:, takes[1]], wl[:, takes[1]]), 1, 1)
    group_grads = group_grads.astype(BF16)
    core_copy.wait_recv()
    gx[x] = gpart[c] + gpair[...]
    copies = [links.shift(gx.at[x], gx.at[x], "x", i) for i in (1, 2, 3)]

    spot = lax.broadcasted_iota(jnp.int32, (sel_dev, nodes_dev), 1)
    hot = (spot_ref[:, :1] == spot).astype(F32).astype(BF16)
    top, mid = split(row_grads)
    low = (row_grads - top.astype(F32) - mid.astype(F32)).astype(BF16)

    def node_grads(h):
        take = takes[h]
        near = group_grads[:, take]
        far = g_far[:, :, :, take].reshape(cols_all, half)
        total = dot(spread_t[0, :, :rows_all], near) + dot(spread_t[1, :, :rows_all], near)
        total += dot(spread_t[0, :, rows_all:], far) + dot(spread_t[1, :, rows_all:], far)
        total += dot(hot, top[:, take], 0, 0) + dot(hot, mid[:, take], 0, 0)
        gn_ref[:, take] = total + dot(hot, low[:, take], 0, 0)
        copy = pltpu.make_async_copy(gn_ref.at[:, take], gn_out.at[:, take], local_sem.at[2 + h])
        copy.start()
        return copy

    out_copies = [node_grads(0)]
    arrived(copies)
    gfull[c, :, y, z] = gx[0] + gx[1] + gx[2] + gx[3]
    crossings = []
    weight_run = Plane(links, gfull.at[c]).gather(lambda view: crossings.append(links.core(view, view)))
    next(weight_run)
    next(weight_run)
    out_copies.append(node_grads(1))
    text_dir = SCALE * tpart[x, c]
    gt_ref[...] = (
        text_dir - unit_texts * jnp.sum(unit_texts * text_dir, axis=1, keepdims=True)
    ) / text_norm
    arrived(loss_copies)
    loss_ref[...] = jnp.sum(loss_grp[...], axis=0)[:1, :1]
    together(weight_run)
    for i, core in enumerate((c, 1 - c)):
        if i:
            arrived(crossings)
        copy = pltpu.make_async_copy(gfull.at[core], gw_out.at[core], local_sem.at[4 + i])
        copy.start()
        out_copies.append(copy)
    for copy in links.copies:
        copy.wait_send()
    for copy in out_copies:
        copy.wait()


def finish_kernel(gn_in, gw_in, gt_in, gn_out, gw_out, gt_out, gn, gw, gt, in_sem, out_sem):
    half = gw_in.shape[5]
    rows = gn_in.shape[0] // 4
    steps = []
    for i in range(4):
        some = pl.ds(i * rows, rows)
        steps.append((gn_in.at[some], gn.at[some], gn_out.at[some]))
    for core in (0, 1):
        for h in (0, 1):
            for y in (0, 2):
                some = pl.ds(y, 2)
                out = gw_out.at[some, :, core, :, pl.ds(h * half, half)]
                steps.append((gw_in.at[core, h, some], gw.at[core, h, some], out))
    steps.append((gt_in, gt, gt_out))
    fetches = [pltpu.make_async_copy(a, b, in_sem.at[i]) for i, (a, b, _) in enumerate(steps)]
    stores = [pltpu.make_async_copy(b, c, out_sem.at[i]) for i, (_, b, c) in enumerate(steps)]
    for copy in fetches:
        copy.start()
    for fetch, store in zip(fetches, stores):
        fetch.wait()
        store.start()
    for copy in stores:
        copy.wait()


def shards(node_features, tiles, tile_list, weight, texts, selected, pairing):
    block = tiles.shape[1]
    nodes_dev, feat = node_features.shape
    sel_dev = selected.shape[0]
    nb = nodes_dev // block
    half = feat // 2
    deep = feat // 32
    vmem = pl.BlockSpec(memory_space=pltpu.VMEM)
    smem = pl.BlockSpec(memory_space=pltpu.SMEM)
    hbm = pl.BlockSpec(memory_space=pl.ANY)
    made = pl.pallas_call(
        prep_kernel,
        out_shape=(
            jax.ShapeDtypeStruct((3, NPEER + 1, sel_dev, block), BF16),
            jax.ShapeDtypeStruct((2, sel_dev, nb * block), BF16),
            jax.ShapeDtypeStruct((sel_dev, block), jnp.int32),
            jax.ShapeDtypeStruct((sel_dev,), jnp.int32),
        ),
        in_specs=[hbm, smem, smem, vmem],
        out_specs=(vmem, vmem, vmem, smem),
        scratch_shapes=[
            pltpu.VMEM((nb, sel_dev, block), F32),
            pltpu.VMEM((nb, sel_dev, block), BF16),
            pltpu.VMEM((sel_dev, block), jnp.int32),
            pltpu.SMEM((NPEER + 1,), jnp.int32),
            pltpu.SMEM((NPEER + 1,), jnp.int32),
            pltpu.SMEM((2, 256), jnp.int32),
            pltpu.SemaphoreType.DMA,
        ],
        compiler_params=pltpu.CompilerParams(vmem_limit_bytes=60 * 2**20),
    )(tile_list.T, selected, pairing, tiles)

    def f32(*shape):
        return pltpu.VMEM(shape, F32)

    def bf16(*shape):
        return pltpu.VMEM(shape, BF16)

    plane = f32(2, 4, 4, sel_dev, half)
    landing = f32(2, 15, sel_dev, half)
    line = [f32(4, 2, sel_dev, feat), f32(4, sel_dev, feat), f32(3, sel_dev, feat)]
    loss, *results = pl.pallas_call(
        main_kernel,
        out_shape=(
            jax.ShapeDtypeStruct((1, 1), F32),
            jax.ShapeDtypeStruct((nodes_dev, feat), F32),
            jax.ShapeDtypeStruct((2, 2, 4, 4, deep, half), F32),
            jax.ShapeDtypeStruct((sel_dev, feat), F32),
        ),
        in_specs=[vmem, vmem, vmem, smem, hbm, hbm, vmem],
        out_specs=(vmem, hbm, hbm, vmem),
        scratch_shapes=[
            f32(nodes_dev, feat),
            f32(feat, feat),
            bf16(nodes_dev, feat),
            f32(nodes_dev, feat),
            bf16(3, ND, sel_dev, block),
            bf16(3, NG, sel_dev, block),
            bf16(2, NPEER, sel_dev, nb * block),
            bf16(2, nb * block, NPEER * sel_dev),
            bf16(feat, feat),
            bf16(feat, feat),
            plane, landing, *line,
            plane, f32(4, 2, sel_dev, feat),
            plane, landing, *line,
            f32(ND, 8, 128),
            f32(NG, 8, NG * sel_dev),
            f32(ND, 8, 128),
            f32(NG, 8, 128),
            bf16(ND, 2 * deep, 4 * sel_dev),
            bf16(ND, 2 * deep, 4 * sel_dev),
            plane,
            bf16(2, ND, 4, sel_dev, half),
            bf16(4, 2, sel_dev, feat),
            f32(2, 2, deep, half),
            f32(2, deep, half),
            f32(4, 2, deep, half),
            f32(2, 2, 4, 4, deep, half),
            f32(sel_dev, feat),
            pltpu.SemaphoreType.DMA((SEMS,)),
            pltpu.SemaphoreType.DMA((SEMS,)),
            pltpu.SemaphoreType.DMA((6,)),
        ],
        compiler_params=pltpu.CompilerParams(
            collective_id=0, has_side_effects=True, vmem_limit_bytes=60 * 2**20
        ),
    )(*made, node_features, weight, texts)
    grad_nodes, grad_weight, grad_texts = pl.pallas_call(
        finish_kernel,
        out_shape=(
            jax.ShapeDtypeStruct((nodes_dev, feat), F32),
            jax.ShapeDtypeStruct((4, 4, 2, deep, feat), F32),
            jax.ShapeDtypeStruct((sel_dev, feat), F32),
        ),
        in_specs=[hbm] * 3,
        out_specs=(hbm,) * 3,
        scratch_shapes=[
            f32(nodes_dev, feat),
            f32(2, 2, 4, 4, deep, half),
            f32(sel_dev, feat),
            pltpu.SemaphoreType.DMA((13,)),
            pltpu.SemaphoreType.DMA((13,)),
        ],
        compiler_params=pltpu.CompilerParams(vmem_limit_bytes=60 * 2**20),
    )(*results)
    return loss.reshape(()), grad_nodes, grad_weight.reshape(feat, feat), grad_texts


def solution(mesh):
    both = ("grp", "dev")
    placed = (
        P(both, None),
        P(both, None, None),
        P(),
        P(),
        P(both, None),
        P(both),
        P(both),
    )
    return jax.shard_map(
        shards,
        mesh=mesh,
        in_specs=placed,
        out_specs=(P(), P(both, None), P(), P(both, None)),
        check_vma=False,
    )
```

```python
import functools

import jax
import jax.numpy as jnp
from jax import lax
from jax.experimental import pallas as pl
from jax.experimental.pallas import tpu as pltpu
from jax.sharding import PartitionSpec as P

MESH = pl.DeviceIdType.MESH
CAP = 2
SCALE = 1.0 / 0.07
EPS = 1e-06
ROOT_HALF = 0.7071067811865476
INV_ROOT_TWO_PI = 0.3989422804014327
F32 = jnp.float32
BF16 = jnp.bfloat16
NG, ND = 8, 16
NPEER = NG + ND
SEMS = 384


def split(value):
    hi = value.astype(BF16)
    return hi, (value - hi.astype(F32)).astype(BF16)


def dot(a, b, ca=1, cb=0):
    return lax.dot_general(a, b, (((ca,), (cb,)), ((), ())), preferred_element_type=F32)


def dot3(a, b, ca=1, cb=0):
    return dot(a[0], b[0], ca, cb) + (dot(a[0], b[1], ca, cb) + dot(a[1], b[0], ca, cb))


def prep_kernel(
    list_ref, sel_ref, pair_ref, tiles_ref,
    rows_ref, local_ref, spot_ref, own_ref,
    acc, onehot, column, count, meta, window, sem,
):
    g, d = lax.axis_index("grp"), lax.axis_index("dev")
    device = g * ND + d
    n_tiles, block = tiles_ref.shape[0], tiles_ref.shape[1]
    wide = window.shape[1]
    first = jnp.minimum(device * n_tiles // 128 * 128, list_ref.shape[1] - wide)
    first = pl.multiple_of(first, 128)
    fetch = pltpu.make_async_copy(list_ref.at[:, pl.ds(first, wide)], window, sem)
    fetch.start()
    sel_dev = sel_ref.shape[0]
    nb = local_ref.shape[2] // block
    nodes_dev = nb * block
    rows_ref[...] = jnp.zeros_like(rows_ref)
    acc[...] = jnp.zeros_like(acc)
    for k in range(sel_dev):
        own = sel_ref[k] - device * nodes_dev
        own_ref[k] = own
        spot_ref[pl.ds(k, 1), :] = jnp.full((1, block), own, jnp.int32)
        column[pl.ds(k, 1), :] = jnp.full((1, block), pair_ref[k], jnp.int32)
    lane = lax.broadcasted_iota(jnp.int32, (sel_dev, block), 1)
    sel = spot_ref[...]
    for b in range(nb):
        onehot[b] = (sel == lane + b * block).astype(F32).astype(BF16)
    for p in range(NPEER + 1):
        count[p] = 0
        meta[p] = 0
    fetch.wait()
    skip = device * n_tiles - first
    for t in range(n_tiles):
        row_block = window[0, skip + t] - device * nb
        col = window[1, skip + t]
        owner = col // nb
        col_block = col - owner * nb
        og = owner // ND
        od = owner - og * ND
        local = owner == device
        peer = jnp.where(local, NPEER, jnp.where(og == g, od, ND + og))
        rank = jnp.minimum(count[peer], 1)
        count[peer] = rank + 1
        meta[peer] = meta[peer] + col_block * jnp.where(rank == 0, 1, nb)
        picked = dot(onehot[row_block], tiles_ref[t])
        rows_ref[rank, peer] = picked.astype(BF16)
        acc[col_block] += picked * local.astype(F32)
    pair = column[...]
    high = pair // 64
    tag = jnp.where(lane == 1, high, pair - high * 64)
    for p in range(NPEER):
        rows_ref[2, p] = jnp.where(lane == 0, meta[p], tag).astype(F32).astype(BF16)
    rows_ref[2, d] = jnp.where(lane == 0, 0, tag).astype(F32).astype(BF16)
    for b in range(nb):
        hi, lo = split(acc[b])
        local_ref[0, :, b * block : (b + 1) * block] = hi
        local_ref[1, :, b * block : (b + 1) * block] = lo


class Links:
    def __init__(self, send_sem, recv_sem):
        self.g, self.d = lax.axis_index("grp"), lax.axis_index("dev")
        self.x, self.c = self.g // 2, self.g % 2
        self.y, self.z = self.d // 4, self.d % 4
        self.send_sem, self.recv_sem = send_sem, recv_sem
        self.used, self.copies = 0, []

    def to(self, src, dst, grp=None, dev=None):
        k = self.used
        self.used += 1
        copy = pltpu.make_async_remote_copy(
            src_ref=src,
            dst_ref=dst,
            send_sem=self.send_sem.at[k],
            recv_sem=self.recv_sem.at[k],
            device_id=(self.g if grp is None else grp, self.d if dev is None else dev),
            device_id_type=MESH,
        )
        copy.start()
        self.copies.append(copy)
        return copy

    def pos(self, axis):
        return {"x": self.x, "y": self.y, "z": self.z}[axis]

    def shift(self, src, dst, axis, step):
        if axis == "x":
            return self.to(src, dst, grp=(self.x + step) % 4 * 2 + self.c)
        if axis == "y":
            return self.to(src, dst, dev=(self.y + step) % 4 * 4 + self.z)
        return self.to(src, dst, dev=self.y * 4 + (self.z + step) % 4)

    def core(self, src, dst):
        return self.to(src, dst, grp=self.x * 2 + 1 - self.c)

    def all_dev(self, src, dst):
        out = []
        for i in range(1, ND):
            e = (self.d + i) % ND
            out.append(self.to(src(e), dst, dev=e))
        return out

    def all_grp(self, src, dst):
        out = []
        for i in range(1, NG):
            e = (self.g + i) % NG
            out.append(self.to(src(e), dst, grp=e))
        return out


def arrived(copies):
    for copy in copies:
        copy.wait_recv()


class Plane:
    def __init__(self, links, buf):
        self.links, self.buf = links, buf
        self.outer, self.inner = ("y", "z"), ("z", "y")

    def at(self, h, out, into):
        links = self.links
        out = (links.pos(self.outer[h]) + out) % 4
        if into is None:
            return self.buf.at[0, out] if h == 0 else self.buf.at[1, :, out]
        into = (links.pos(self.inner[h]) + into) % 4
        return self.buf.at[0, out, into] if h == 0 else self.buf.at[1, into, out]

    def gather(self, on=lambda h, out: None):
        shift, at, outer, inner = self.links.shift, self.at, self.outer, self.inner
        near, away = {}, {}

        def send_out(h, o):
            view = at(h, 0, o)
            for i in (2, 1, 3):
                away[h, i, o] = shift(view, view, outer[h], i)

        for h in (0, 1):
            view = at(h, 0, 0)
            for i in (2, 1, 3):
                near[h, i] = shift(view, view, inner[h], i)
        for h in (0, 1):
            send_out(h, 0)
        yield
        for i in (2, 1, 3):
            for h in (0, 1):
                near[h, i].wait_recv()
                send_out(h, 4 - i)
        yield
        for h in (0, 1):
            on(h, 0)
        for i in (2, 1, 3):
            for h in (0, 1):
                for o in (0, 2, 3, 1):
                    away[h, i, o].wait_recv()
                on(h, 4 - i)
        yield

    def reduce(self, land):
        shift, at, outer, inner = self.links.shift, self.at, self.outer, self.inner
        order = (2, 1, 3, 0)
        away, near = {}, {}
        for h in (0, 1):
            for o in order:
                for i in (2, 1, 3):
                    away[h, i, o] = shift(at(h, i, o), land.at[h, 4 * (i - 1) + o], outer[h], i)
            yield
        for o in order:
            for h in (0, 1):
                for i in (2, 1, 3):
                    away[h, i, o].wait_recv()
                view = at(h, 0, o)
                view[...] += land[h, o] + land[h, 4 + o] + land[h, 8 + o]
                if o:
                    near[h, o] = shift(view, land.at[h, 11 + o], inner[h], o)
            yield
        for h in (0, 1):
            for o in (2, 1, 3):
                near[h, o].wait_recv()
            view = at(h, 0, 0)
            view[...] += land[h, 12] + land[h, 13] + land[h, 14]
        yield


class Line:
    def __init__(self, links, buf):
        self.links, self.buf = links, buf

    def gather(self):
        links = self.links
        x, c = links.x, links.c
        own = self.buf.at[x, c]
        ways = [links.shift(own, own, "x", i) for i in (2, 1, 3)]
        crossed = [links.core(own, own)]
        yield
        for i, way in zip((2, 1, 3), ways):
            way.wait_recv()
            view = self.buf.at[(x + 4 - i) % 4, c]
            crossed.append(links.core(view, view))
        yield
        arrived(crossed)
        yield

    def reduce(self, pair, land):
        links = self.links
        x, c = links.x, links.c
        copy = links.core(self.buf.at[:, 1 - c], pair)
        yield
        copy.wait_recv()
        view = self.buf.at[:, c]
        view[...] += pair[...]
        ways = [
            links.shift(self.buf.at[(x + i) % 4, c], land.at[i - 1], "x", i) for i in (2, 1, 3)
        ]
        yield
        arrived(ways)
        view = self.buf.at[x, c]
        view[...] += land[0] + land[1] + land[2]
        yield


def together(*runs):
    runs = list(runs)
    while runs:
        runs = [run for run in runs if next(run, "end") != "end"]


def to_lanes(column):
    n = column.shape[0]
    wide = jnp.broadcast_to(column, (n, 128)).T
    rows = [wide[:1, 128 * i : 128 * (i + 1)] for i in range(n // 128)]
    return jnp.concatenate(rows + [jnp.zeros((8 - len(rows), 128), F32)], axis=0)


def as_row(packed, n):
    return jnp.concatenate([packed[i : i + 1] for i in range(n // 128)], axis=1)


def main_kernel(
    rows_ref, local_ref, spot_ref, own_ref, nodes_hbm, weight_hbm, texts_ref,
    loss_ref, gn_out, gw_out, gt_ref,
    nodes_ref, weight_ref, rounded, gn_ref,
    near_in, far_in, spread, spread_t, wh, wl,
    npart, nland, fpart, fpair, fsmall,
    units, cols, spart, sland, tpart, tpair, tsmall,
    row_in, col_in, loss_dev, loss_grp, slices_out, slices, pre_all, g_far,
    u_hi, u_lo, p_hi, p_lo, score_ref,
    gpart, gpair, gx, gfull, chosen,
    send_sem, recv_sem, local_sem,
):
    links = Links(send_sem, recv_sem)
    g, d, x, c, y, z = links.g, links.d, links.x, links.c, links.y, links.z
    sel_dev, feat = texts_ref.shape
    half = feat // 2
    nodes_dev = nodes_ref.shape[0]
    block = near_in.shape[3]
    nb = nodes_dev // block
    total_sel = sel_dev * NG * ND
    rows_all = ND * sel_dev
    cols_all = NG * sel_dev
    takes = [slice(h * half, (h + 1) * half) for h in (0, 1)]

    barrier = pltpu.get_barrier_semaphore()
    for i in range(1, ND):
        pl.semaphore_signal(barrier, inc=1, device_id=(g, (d + i) % ND), device_id_type=MESH)
    for i in range(1, NG):
        pl.semaphore_signal(barrier, inc=1, device_id=((g + i) % NG, d), device_id_type=MESH)

    nodes_copy = pltpu.make_async_copy(nodes_hbm, nodes_ref, local_sem.at[0])
    weight_copy = pltpu.make_async_copy(weight_hbm, weight_ref, local_sem.at[1])
    nodes_copy.start()
    weight_copy.start()

    texts = texts_ref[...]
    text_norm = jnp.sqrt(jnp.sum(texts * texts, axis=1, keepdims=True) + EPS)
    unit_texts = texts / text_norm
    cols[x, c] = unit_texts
    near_in[2, d] = rows_ref[2, d]
    pl.semaphore_wait(barrier, ND + NG - 2)

    near_copies = links.all_dev(lambda e: rows_ref.at[:, e], near_in.at[:, d])
    far_copies = links.all_grp(lambda e: rows_ref.at[:, ND + e], far_in.at[:, g])
    text_run = Line(links, cols).gather()
    next(text_run)
    nodes_copy.wait()
    rounded[...] = nodes_ref[...].astype(BF16)
    for k in range(sel_dev):
        chosen[pl.ds(k, 1), :] = nodes_ref[pl.ds(own_ref[k], 1), :]
    weight_copy.wait()
    hi, lo = split(weight_ref[...])
    wh[...] = hi
    wl[...] = lo

    def expand(into, rows):
        tag = rows[2].astype(F32)[:, :1]
        second = jnp.floor(tag * (1.0 / nb) + 0.01)
        first = tag - second * nb
        for q, which in ((0, first), (1, second)):
            for b in range(nb):
                spread[q, into, :, b * block : (b + 1) * block] = jnp.where(
                    which == float(b), rows[q].astype(F32), 0.0
                ).astype(BF16)

    for i, copy in enumerate(near_copies):
        copy.wait_recv()
        p = (d + ND - 1 - i) % ND
        expand(p, near_in[:, p])
    spread[0, d] = local_ref[0]
    spread[1, d] = local_ref[1]
    flat = (rows_all, nb * block)
    s0, s1 = spread[0, :ND].reshape(flat), spread[1, :ND].reshape(flat)
    near_run = Plane(links, npart).reduce(nland)
    for h in (0, 1):
        table = rounded[:, takes[h]]
        npart[h] = (dot(s0, table) + dot(s1, table)).reshape(4, 4, sel_dev, half)
        next(near_run)
    for i, copy in enumerate(far_copies):
        copy.wait_recv()
        p = (g + NG - 1 - i) % NG
        expand(ND + p, far_in[:, p])
    spread[:, ND + g] = jnp.zeros((2, sel_dev, nb * block), BF16)
    flat = (cols_all, nb * block)
    s0, s1 = spread[0, ND:].reshape(flat), spread[1, ND:].reshape(flat)
    fpart[...] = (dot(s0, rounded[...]) + dot(s1, rounded[...])).reshape(4, 2, sel_dev, feat)
    far_run = Line(links, fpart).reduce(fpair, fsmall)
    next(far_run)
    next(far_run)
    together(near_run, far_run, text_run)

    far_sum = fpart[x, c]
    for h in (0, 1):
        chosen[:, takes[h]] += npart[h, y, z] + far_sum[:, takes[h]]
    picked = chosen[...]
    picked_parts = split(picked)
    before = dot3(picked_parts, (wh[...], wl[...]))
    curve = 0.5 * (1.0 + lax.erf(before * ROOT_HALF))
    hidden = before * curve
    node_norm = jnp.sqrt(jnp.sum(hidden * hidden, axis=1, keepdims=True) + EPS)
    unit_nodes = hidden / node_norm
    for h in (0, 1):
        units[h, y, z] = unit_nodes[:, takes[h]]
    col_parts = split(cols[...].reshape(cols_all, feat))
    text_halves = [tuple(v[:, takes[h]] for v in col_parts) for h in (0, 1)]
    some = 4 * sel_dev

    def score(h, out):
        parts = split(Plane(links, units).at(h, out, None)[...].reshape(some, half))
        for v, into in zip(parts, (u_hi, u_lo)):
            Plane(links, into).at(h, out, None)[...] = v.reshape(4, sel_dev, half)
        part = dot3(parts, text_halves[h], 1, 1)
        Plane(links, score_ref).at(h, out, None)[...] = part.reshape(4, sel_dev, cols_all)

    unit_run = Plane(links, units).gather(score)
    next(unit_run)
    next(unit_run)
    lane = lax.broadcasted_iota(jnp.int32, (8, cols_all), 1)
    ids = ((lane // sel_dev * ND + d) * sel_dev + lane % sel_dev)[:1]
    tags = near_in[2].reshape(rows_all, block).astype(F32)
    target = (tags[:, 1:2] * 64.0 + tags[:, 2:3] == ids.astype(F32)).astype(F32)
    wide = jnp.concatenate(
        [v.astype(F32) for v in (*picked_parts, picked_parts[0])] + [jnp.zeros_like(picked)], axis=0
    )
    slices_out[...] = wide.T.astype(BF16).reshape(slices_out.shape)
    slices[d] = slices_out[d]
    together(unit_run)

    unit_parts = [tuple(v[h].reshape(rows_all, half) for v in (u_hi, u_lo)) for h in (0, 1)]
    scores = SCALE * (score_ref[0] + score_ref[1]).reshape(rows_all, cols_all)
    exps = jnp.exp(scores)
    row_in[d] = to_lanes(jnp.sum(exps, axis=1, keepdims=True))
    row_copies = links.all_dev(lambda e: row_in.at[d], row_in.at[d])
    col_sum = jnp.sum(exps, axis=0, keepdims=True)
    col_in[g] = jnp.broadcast_to(col_sum, (8, cols_all))
    col_copies = links.all_grp(lambda e: col_in.at[g], col_in.at[g])
    slice_copies = links.all_dev(lambda e: slices_out.at[e], slices.at[d])
    positive = jnp.sum(jnp.sum(target * scores, axis=1, keepdims=True), axis=0, keepdims=True)
    arrived(col_copies)
    col_total = jnp.sum(col_in[...], axis=0)[:1]
    arrived(row_copies)
    row_total = as_row(jnp.sum(row_in[...], axis=0), rows_all)
    row_recip = jnp.broadcast_to(1.0 / row_total, (128, rows_all)).T[:, :1]
    col_recip = 1.0 / col_total
    slope = 0.5 * exps * (row_recip + col_recip) - target
    slope_parts = split(slope)
    node_run = Plane(links, spart).reduce(sland)
    for h in (0, 1):
        spart[h] = dot3(slope_parts, text_halves[h]).reshape(4, 4, sel_dev, half)
        next(node_run)
    log_rows = jnp.sum(jnp.log(row_total), axis=1, keepdims=True)
    log_cols = jnp.sum(jnp.log(col_total), axis=1, keepdims=True)
    part = (log_rows / ND + log_cols / NG) / (2.0 * total_sel) - positive / total_sel
    loss_dev[d] = jnp.broadcast_to(part, (8, 128))
    for h in (0, 1):
        grown = dot3(slope_parts, unit_parts[h], 0, 0)
        tpart[:, :, :, takes[h]] = grown.reshape(4, 2, sel_dev, half)
    text_run = Line(links, tpart).reduce(tpair, tsmall)
    next(text_run)
    loss_copies = links.all_dev(lambda e: loss_dev.at[d], loss_dev.at[d])
    together(node_run, text_run)

    node_dir = SCALE * jnp.concatenate([spart[0, y, z], spart[1, y, z]], axis=1)
    node_back = (
        node_dir - unit_nodes * jnp.sum(unit_nodes * node_dir, axis=1, keepdims=True)
    ) / node_norm
    pre_grad = node_back * (curve + before * jnp.exp(-0.5 * before * before) * INV_ROOT_TWO_PI)
    for h in (0, 1):
        pre_all[h, y, z] = pre_grad[:, takes[h]]
    pieces = {0: 0.0, 1: 0.0}

    def weigh(h, out):
        hi, lo = split(Plane(links, pre_all).at(h, out, None)[...].reshape(some, half))
        for v, into in ((hi, p_hi), (lo, p_lo)):
            Plane(links, into).at(h, out, None)[...] = v.reshape(4, sel_dev, half)
        across = ((y if h == 0 else z) + out) % 4
        for k in range(4):
            rows = slice(k * sel_dev, (k + 1) * sel_dev)
            stack = jnp.concatenate([hi[rows], hi[rows], lo[rows], hi[rows]], axis=0)
            p = across * 4 + k if h == 0 else k * 4 + across
            pieces[h] += dot(slices[p], stack)

    pre_run = Plane(links, pre_all).gather(weigh)
    next(pre_run)
    row_grads = dot3(split(pre_grad), (wh[...], wl[...]), 1, 1)
    g_far[x, c] = row_grads.astype(BF16)
    far_run = Line(links, g_far).gather()
    next(far_run)
    arrived(slice_copies)
    next(pre_run)
    next(far_run)
    arrived(loss_copies)
    loss_grp[g] = jnp.sum(loss_dev[...], axis=0)
    loss_copies = links.all_grp(lambda e: loss_grp.at[g], loss_grp.at[g])
    for q in (0, 1):
        for i in range(NPEER // 4):
            rows = spread[q, 4 * i : 4 * i + 4].reshape(some, nb * block)
            spread_t[q, :, i * some : (i + 1) * some] = rows.astype(F32).T.astype(BF16)
    together(pre_run, far_run)

    pre_parts = [tuple(v[h].reshape(rows_all, half) for v in (p_hi, p_lo)) for h in (0, 1)]
    for h in (0, 1):
        gpart[:, h] = pieces[h].reshape(2, pieces[h].shape[0] // 2, half)
    core_copy = links.core(gpart.at[1 - c], gpair)
    group_grads = dot3(pre_parts[0], (wh[:, takes[0]], wl[:, takes[0]]), 1, 1)
    group_grads += dot3(pre_parts[1], (wh[:, takes[1]], wl[:, takes[1]]), 1, 1)
    group_grads = group_grads.astype(BF16)
    core_copy.wait_recv()
    gx[x] = gpart[c] + gpair[...]
    copies = [links.shift(gx.at[x], gx.at[x], "x", i) for i in (1, 2, 3)]

    spot = lax.broadcasted_iota(jnp.int32, (sel_dev, nodes_dev), 1)
    hot = (spot_ref[:, :1] == spot).astype(F32).astype(BF16)
    top, mid = split(row_grads)
    low = (row_grads - top.astype(F32) - mid.astype(F32)).astype(BF16)

    def node_grads(h):
        take = takes[h]
        near = group_grads[:, take]
        far = g_far[:, :, :, take].reshape(cols_all, half)
        total = dot(spread_t[0, :, :rows_all], near) + dot(spread_t[1, :, :rows_all], near)
        total += dot(spread_t[0, :, rows_all:], far) + dot(spread_t[1, :, rows_all:], far)
        total += dot(hot, top[:, take], 0, 0) + dot(hot, mid[:, take], 0, 0)
        gn_ref[:, take] = total + dot(hot, low[:, take], 0, 0)
        copy = pltpu.make_async_copy(gn_ref.at[:, take], gn_out.at[:, take], local_sem.at[2 + h])
        copy.start()
        return copy

    out_copies = [node_grads(0)]
    arrived(copies)
    gfull[c, :, y, z] = gx[0] + gx[1] + gx[2] + gx[3]
    crossings = []
    weight_plane = Plane(links, gfull.at[c])

    def cross(h, out):
        view = weight_plane.at(h, out, None)
        crossings.append(links.core(view, view))

    weight_run = weight_plane.gather(cross)
    next(weight_run)
    next(weight_run)
    out_copies.append(node_grads(1))
    text_dir = SCALE * tpart[x, c]
    gt_ref[...] = (
        text_dir - unit_texts * jnp.sum(unit_texts * text_dir, axis=1, keepdims=True)
    ) / text_norm
    arrived(loss_copies)
    loss_ref[...] = jnp.sum(loss_grp[...], axis=0)[:1, :1]
    together(weight_run)
    for i, core in enumerate((c, 1 - c)):
        if i:
            arrived(crossings)
        copy = pltpu.make_async_copy(gfull.at[core], gw_out.at[core], local_sem.at[4 + i])
        copy.start()
        out_copies.append(copy)
    for copy in links.copies:
        copy.wait_send()
    for copy in out_copies:
        copy.wait()


def finish_kernel(
    loss_in, gn_in, gw_in, gt_in,
    loss_out, gn_out, gw_out, gt_out,
    gn, gw, gt, in_sem, out_sem,
):
    half = gw_in.shape[5]
    rows = gn_in.shape[0] // 4
    steps = []
    for i in range(4):
        some = pl.ds(i * rows, rows)
        steps.append((gn_in.at[some], gn.at[some], gn_out.at[some]))
    for core in (0, 1):
        for h in (0, 1):
            for y in (0, 2):
                some = pl.ds(y, 2)
                out = gw_out.at[some, :, core, :, pl.ds(h * half, half)]
                steps.append((gw_in.at[core, h, some], gw.at[core, h, some], out))
    steps.append((gt_in, gt, gt_out))
    fetches = [pltpu.make_async_copy(a, b, in_sem.at[i]) for i, (a, b, _) in enumerate(steps)]
    stores = [pltpu.make_async_copy(b, c, out_sem.at[i]) for i, (_, b, c) in enumerate(steps)]
    for copy in fetches:
        copy.start()
    loss_out[...] = loss_in[...]
    for fetch, store in zip(fetches, stores):
        fetch.wait()
        store.start()
    for copy in stores:
        copy.wait()


def shards(node_features, tiles, tile_list, weight, texts, selected, pairing):
    block = tiles.shape[1]
    nodes_dev, feat = node_features.shape
    sel_dev = selected.shape[0]
    nb = nodes_dev // block
    half = feat // 2
    deep = feat // 32
    vmem = pl.BlockSpec(memory_space=pltpu.VMEM)
    smem = pl.BlockSpec(memory_space=pltpu.SMEM)
    hbm = pl.BlockSpec(memory_space=pl.ANY)
    made = pl.pallas_call(
        prep_kernel,
        out_shape=(
            jax.ShapeDtypeStruct((3, NPEER + 1, sel_dev, block), BF16),
            jax.ShapeDtypeStruct((2, sel_dev, nb * block), BF16),
            jax.ShapeDtypeStruct((sel_dev, block), jnp.int32),
            jax.ShapeDtypeStruct((sel_dev,), jnp.int32),
        ),
        in_specs=[hbm, smem, smem, vmem],
        out_specs=(vmem, vmem, vmem, smem),
        scratch_shapes=[
            pltpu.VMEM((nb, sel_dev, block), F32),
            pltpu.VMEM((nb, sel_dev, block), BF16),
            pltpu.VMEM((sel_dev, block), jnp.int32),
            pltpu.SMEM((NPEER + 1,), jnp.int32),
            pltpu.SMEM((NPEER + 1,), jnp.int32),
            pltpu.SMEM((2, 256), jnp.int32),
            pltpu.SemaphoreType.DMA,
        ],
        compiler_params=pltpu.CompilerParams(vmem_limit_bytes=60 * 2**20),
    )(tile_list.T, selected, pairing, tiles)

    def f32(*shape):
        return pltpu.VMEM(shape, F32)

    def bf16(*shape):
        return pltpu.VMEM(shape, BF16)

    plane = f32(2, 4, 4, sel_dev, half)
    landing = f32(2, 15, sel_dev, half)
    line = [f32(4, 2, sel_dev, feat), f32(4, sel_dev, feat), f32(3, sel_dev, feat)]
    results = pl.pallas_call(
        main_kernel,
        out_shape=(
            jax.ShapeDtypeStruct((1, 1), F32),
            jax.ShapeDtypeStruct((nodes_dev, feat), F32),
            jax.ShapeDtypeStruct((2, 2, 4, 4, deep, half), F32),
            jax.ShapeDtypeStruct((sel_dev, feat), F32),
        ),
        in_specs=[vmem, vmem, vmem, smem, hbm, hbm, vmem],
        out_specs=(vmem, hbm, hbm, vmem),
        scratch_shapes=[
            f32(nodes_dev, feat),
            f32(feat, feat),
            bf16(nodes_dev, feat),
            f32(nodes_dev, feat),
            bf16(3, ND, sel_dev, block),
            bf16(3, NG, sel_dev, block),
            bf16(2, NPEER, sel_dev, nb * block),
            bf16(2, nb * block, NPEER * sel_dev),
            bf16(feat, feat),
            bf16(feat, feat),
            plane, landing, *line,
            plane, f32(4, 2, sel_dev, feat),
            plane, landing, *line,
            f32(ND, 8, 128),
            f32(NG, 8, NG * sel_dev),
            f32(ND, 8, 128),
            f32(NG, 8, 128),
            bf16(ND, 2 * deep, 4 * sel_dev),
            bf16(ND, 2 * deep, 4 * sel_dev),
            plane,
            bf16(4, 2, sel_dev, feat),
            *[bf16(2, 4, 4, sel_dev, half)] * 4,
            f32(2, 4, 4, sel_dev, NG * sel_dev),
            f32(2, 2, deep, half),
            f32(2, deep, half),
            f32(4, 2, deep, half),
            f32(2, 2, 4, 4, deep, half),
            f32(sel_dev, feat),
            pltpu.SemaphoreType.DMA((SEMS,)),
            pltpu.SemaphoreType.DMA((SEMS,)),
            pltpu.SemaphoreType.DMA((6,)),
        ],
        compiler_params=pltpu.CompilerParams(
            collective_id=0, has_side_effects=True, vmem_limit_bytes=60 * 2**20
        ),
    )(*made, node_features, weight, texts)
    loss, grad_nodes, grad_weight, grad_texts = pl.pallas_call(
        finish_kernel,
        out_shape=(
            jax.ShapeDtypeStruct((1, 1), F32),
            jax.ShapeDtypeStruct((nodes_dev, feat), F32),
            jax.ShapeDtypeStruct((4, 4, 2, deep, feat), F32),
            jax.ShapeDtypeStruct((sel_dev, feat), F32),
        ),
        in_specs=[vmem, hbm, hbm, hbm],
        out_specs=(vmem, hbm, hbm, hbm),
        scratch_shapes=[
            f32(nodes_dev, feat),
            f32(2, 2, 4, 4, deep, half),
            f32(sel_dev, feat),
            pltpu.SemaphoreType.DMA((13,)),
            pltpu.SemaphoreType.DMA((13,)),
        ],
        compiler_params=pltpu.CompilerParams(vmem_limit_bytes=60 * 2**20),
    )(*results)
    return loss.reshape(()), grad_nodes, grad_weight.reshape(feat, feat), grad_texts


def solution(mesh):
    both = ("grp", "dev")
    placed = (
        P(both, None),
        P(both, None, None),
        P(),
        P(),
        P(both, None),
        P(both),
        P(both),
    )
    return jax.shard_map(
        shards,
        mesh=mesh,
        in_specs=placed,
        out_specs=(P(), P(both, None), P(), P(both, None)),
        check_vma=False,
    )
```

```python
import functools

import jax
import jax.numpy as jnp
from jax import lax
from jax.experimental import pallas as pl
from jax.experimental.pallas import tpu as pltpu
from jax.sharding import PartitionSpec as P

MESH = pl.DeviceIdType.MESH
CAP = 2
SCALE = 1.0 / 0.07
EPS = 1e-06
ROOT_HALF = 0.7071067811865476
INV_ROOT_TWO_PI = 0.3989422804014327
F32 = jnp.float32
BF16 = jnp.bfloat16
NG, ND = 8, 16
NPEER = NG + ND
SEMS = 384


def split(value):
    hi = value.astype(BF16)
    return hi, (value - hi.astype(F32)).astype(BF16)


def dot(a, b, ca=1, cb=0):
    return lax.dot_general(a, b, (((ca,), (cb,)), ((), ())), preferred_element_type=F32)


def dot3(a, b, ca=1, cb=0):
    return dot(a[0], b[0], ca, cb) + (dot(a[0], b[1], ca, cb) + dot(a[1], b[0], ca, cb))


def prep_kernel(
    list_ref, sel_ref, pair_ref, tiles_hbm,
    rows_ref, local_ref, spot_ref, own_ref,
    acc, onehot, column, count, meta, window, tiles_ref, sem, tiles_sem,
):
    g, d = lax.axis_index("grp"), lax.axis_index("dev")
    device = g * ND + d
    n_tiles, block = tiles_hbm.shape[0], tiles_hbm.shape[1]
    wide = window.shape[1]
    first = jnp.minimum(device * n_tiles // 128 * 128, list_ref.shape[1] - wide)
    first = pl.multiple_of(first, 128)
    fetch = pltpu.make_async_copy(list_ref.at[:, pl.ds(first, wide)], window, sem)
    fetch.start()
    chunk = n_tiles // 4
    chunks = []
    for i in range(4):
        some = pl.ds(i * chunk, chunk)
        chunks.append(
            pltpu.make_async_copy(tiles_hbm.at[some], tiles_ref.at[some], tiles_sem.at[i])
        )
        chunks[i].start()
    sel_dev = sel_ref.shape[0]
    nb = local_ref.shape[2] // block
    nodes_dev = nb * block
    rows_ref[...] = jnp.zeros_like(rows_ref)
    acc[...] = jnp.zeros_like(acc)
    for k in range(sel_dev):
        own = sel_ref[k] - device * nodes_dev
        own_ref[k] = own
        spot_ref[pl.ds(k, 1), :] = jnp.full((1, block), own, jnp.int32)
        column[pl.ds(k, 1), :] = jnp.full((1, block), pair_ref[k], jnp.int32)
    lane = lax.broadcasted_iota(jnp.int32, (sel_dev, block), 1)
    sel = spot_ref[...]
    for b in range(nb):
        onehot[b] = (sel == lane + b * block).astype(F32).astype(BF16)
    for p in range(NPEER + 1):
        count[p] = 0
        meta[p] = 0
    fetch.wait()
    skip = device * n_tiles - first
    for t in range(n_tiles):
        if t % chunk == 0:
            chunks[t // chunk].wait()
        row_block = window[0, skip + t] - device * nb
        col = window[1, skip + t]
        owner = col // nb
        col_block = col - owner * nb
        og = owner // ND
        od = owner - og * ND
        local = owner == device
        peer = jnp.where(local, NPEER, jnp.where(og == g, od, ND + og))
        rank = jnp.minimum(count[peer], 1)
        count[peer] = rank + 1
        meta[peer] = meta[peer] + col_block * jnp.where(rank == 0, 1, nb)
        picked = dot(onehot[row_block], tiles_ref[t])
        start = pl.multiple_of(rank * sel_dev, sel_dev)
        rows_ref[peer, pl.ds(start, sel_dev)] = picked.astype(BF16)
        acc[col_block] += picked * local.astype(F32)
    pair = column[...]
    high = pair // 64
    low = pair - high * 64
    lane = lane[:16]
    tag = jnp.where(lane == 1, high[:16], low[:16])
    tag = jnp.where(lane == 3, high[16:], jnp.where(lane == 4, low[16:], tag))
    tail = pl.ds(2 * sel_dev, 16)
    for p in range(NPEER):
        rows_ref[p, tail] = jnp.where(lane == 0, meta[p], tag).astype(F32).astype(BF16)
    for b in range(nb):
        hi, lo = split(acc[b])
        local_ref[0, :, b * block : (b + 1) * block] = hi
        local_ref[1, :, b * block : (b + 1) * block] = lo


class Links:
    def __init__(self, send_sem, recv_sem):
        self.g, self.d = lax.axis_index("grp"), lax.axis_index("dev")
        self.x, self.c = self.g // 2, self.g % 2
        self.y, self.z = self.d // 4, self.d % 4
        self.send_sem, self.recv_sem = send_sem, recv_sem
        self.used, self.copies = 0, []

    def to(self, src, dst, grp=None, dev=None):
        k = self.used
        self.used += 1
        copy = pltpu.make_async_remote_copy(
            src_ref=src,
            dst_ref=dst,
            send_sem=self.send_sem.at[k],
            recv_sem=self.recv_sem.at[k],
            device_id=(self.g if grp is None else grp, self.d if dev is None else dev),
            device_id_type=MESH,
        )
        copy.start()
        self.copies.append(copy)
        return copy

    def pos(self, axis):
        return {"x": self.x, "y": self.y, "z": self.z}[axis]

    def shift(self, src, dst, axis, step):
        if axis == "x":
            return self.to(src, dst, grp=(self.x + step) % 4 * 2 + self.c)
        if axis == "y":
            return self.to(src, dst, dev=(self.y + step) % 4 * 4 + self.z)
        return self.to(src, dst, dev=self.y * 4 + (self.z + step) % 4)

    def core(self, src, dst):
        return self.to(src, dst, grp=self.x * 2 + 1 - self.c)

    def all_dev(self, src, dst):
        out = []
        for i in range(1, ND):
            e = (self.d + i) % ND
            out.append(self.to(src(e), dst, dev=e))
        return out

    def all_grp(self, src, dst):
        out = []
        for i in range(1, NG):
            e = (self.g + i) % NG
            out.append(self.to(src(e), dst, grp=e))
        return out


def arrived(copies):
    for copy in copies:
        copy.wait_recv()


class Plane:
    def __init__(self, links, buf):
        self.links, self.buf = links, buf
        self.outer, self.inner = ("y", "z"), ("z", "y")

    def at(self, h, out, into):
        links = self.links
        out = (links.pos(self.outer[h]) + out) % 4
        if into is None:
            return self.buf.at[0, out] if h == 0 else self.buf.at[1, :, out]
        into = (links.pos(self.inner[h]) + into) % 4
        return self.buf.at[0, out, into] if h == 0 else self.buf.at[1, into, out]

    def gather(self, on=lambda h, out: None):
        shift, at, outer, inner = self.links.shift, self.at, self.outer, self.inner
        near, away = {}, {}

        def send_out(h, o):
            view = at(h, 0, o)
            for i in (2, 1, 3):
                away[h, i, o] = shift(view, view, outer[h], i)

        for h in (0, 1):
            view = at(h, 0, 0)
            for i in (2, 1, 3):
                near[h, i] = shift(view, view, inner[h], i)
        for h in (0, 1):
            send_out(h, 0)
        yield
        for i in (2, 1, 3):
            for h in (0, 1):
                near[h, i].wait_recv()
                send_out(h, 4 - i)
        yield
        for h in (0, 1):
            on(h, 0)
        for i in (2, 1, 3):
            for h in (0, 1):
                for o in (0, 2, 3, 1):
                    away[h, i, o].wait_recv()
                on(h, 4 - i)
        yield

    def reduce(self, land):
        shift, at, outer, inner = self.links.shift, self.at, self.outer, self.inner
        order = (2, 1, 3, 0)
        away, near = {}, {}
        for h in (0, 1):
            for o in order:
                for i in (2, 1, 3):
                    away[h, i, o] = shift(at(h, i, o), land.at[h, 4 * (i - 1) + o], outer[h], i)
            yield
        for o in order:
            for h in (0, 1):
                for i in (2, 1, 3):
                    away[h, i, o].wait_recv()
                view = at(h, 0, o)
                view[...] += land[h, o] + land[h, 4 + o] + land[h, 8 + o]
                if o:
                    near[h, o] = shift(view, land.at[h, 11 + o], inner[h], o)
            yield
        for h in (0, 1):
            for o in (2, 1, 3):
                near[h, o].wait_recv()
            view = at(h, 0, 0)
            view[...] += land[h, 12] + land[h, 13] + land[h, 14]
        yield


class Line:
    def __init__(self, links, buf):
        self.links, self.buf = links, buf

    def gather(self):
        links = self.links
        x, c = links.x, links.c
        own = self.buf.at[x, c]
        ways = [links.shift(own, own, "x", i) for i in (2, 1, 3)]
        crossed = [links.core(own, own)]
        yield
        for i, way in zip((2, 1, 3), ways):
            way.wait_recv()
            view = self.buf.at[(x + 4 - i) % 4, c]
            crossed.append(links.core(view, view))
        yield
        arrived(crossed)
        yield

    def reduce(self, pair, land):
        links = self.links
        x, c = links.x, links.c
        copy = links.core(self.buf.at[:, 1 - c], pair)
        yield
        copy.wait_recv()
        view = self.buf.at[:, c]
        view[...] += pair[...]
        ways = [
            links.shift(self.buf.at[(x + i) % 4, c], land.at[i - 1], "x", i) for i in (2, 1, 3)
        ]
        yield
        arrived(ways)
        view = self.buf.at[x, c]
        view[...] += land[0] + land[1] + land[2]
        yield


def together(*runs):
    runs = list(runs)
    while runs:
        runs = [run for run in runs if next(run, "end") != "end"]


def to_lanes(column):
    n = column.shape[0]
    wide = jnp.broadcast_to(column, (n, 128)).T
    rows = [wide[:1, 128 * i : 128 * (i + 1)] for i in range(n // 128)]
    return jnp.concatenate(rows + [jnp.zeros((8 - len(rows), 128), F32)], axis=0)


def as_row(packed, n):
    return jnp.concatenate([packed[i : i + 1] for i in range(n // 128)], axis=1)


def main_kernel(
    rows_ref, local_ref, spot_ref, own_ref, nodes_hbm, weight_hbm, texts_ref,
    loss_ref, gn_out, gw_out, gt_ref,
    nodes_ref, weight_ref, rounded, gn_ref,
    near_in, far_in, spread, spread_t, wh, wl,
    npart, nland, fpart, fpair, fsmall,
    units, cols, spart, sland, tpart, tpair, tsmall,
    row_in, col_in, loss_dev, loss_grp, slices_out, slices, pre_all, g_far,
    u_hi, u_lo, p_hi, p_lo, score_ref,
    gpart, gpair, gx, gfull, chosen,
    send_sem, recv_sem, local_sem,
):
    links = Links(send_sem, recv_sem)
    g, d, x, c, y, z = links.g, links.d, links.x, links.c, links.y, links.z
    sel_dev, feat = texts_ref.shape
    half = feat // 2
    nodes_dev = nodes_ref.shape[0]
    block = near_in.shape[2]
    nb = nodes_dev // block
    total_sel = sel_dev * NG * ND
    rows_all = ND * sel_dev
    cols_all = NG * sel_dev
    takes = [slice(h * half, (h + 1) * half) for h in (0, 1)]

    barrier = pltpu.get_barrier_semaphore()
    for i in range(1, ND):
        pl.semaphore_signal(barrier, inc=1, device_id=(g, (d + i) % ND), device_id_type=MESH)
    for i in range(1, NG):
        pl.semaphore_signal(barrier, inc=1, device_id=((g + i) % NG, d), device_id_type=MESH)

    nodes_copy = pltpu.make_async_copy(nodes_hbm, nodes_ref, local_sem.at[0])
    weight_copy = pltpu.make_async_copy(weight_hbm, weight_ref, local_sem.at[1])
    nodes_copy.start()
    weight_copy.start()

    texts = texts_ref[...]
    text_norm = jnp.sqrt(jnp.sum(texts * texts, axis=1, keepdims=True) + EPS)
    unit_texts = texts / text_norm
    cols[x, c] = unit_texts
    near_in[d] = rows_ref[d]
    pl.semaphore_wait(barrier, ND + NG - 2)

    near_copies = links.all_dev(lambda e: rows_ref.at[e], near_in.at[d])
    far_copies = links.all_grp(lambda e: rows_ref.at[ND + e], far_in.at[g])
    text_run = Line(links, cols).gather()
    next(text_run)
    nodes_copy.wait()
    rounded[...] = nodes_ref[...].astype(BF16)
    for k in range(sel_dev):
        chosen[pl.ds(k, 1), :] = nodes_ref[pl.ds(own_ref[k], 1), :]
    weight_copy.wait()
    hi, lo = split(weight_ref[...])
    wh[...] = hi
    wl[...] = lo

    def expand(into, rows):
        tag = rows[2 * sel_dev :].astype(F32)[:1, :1]
        second = jnp.floor(tag * (1.0 / nb) + 0.01)
        first = tag - second * nb
        for q, which in ((0, first), (1, second)):
            for b in range(nb):
                spread[q, into, :, b * block : (b + 1) * block] = jnp.where(
                    which == float(b), rows[q * sel_dev : (q + 1) * sel_dev].astype(F32), 0.0
                ).astype(BF16)

    for i, copy in enumerate(near_copies):
        copy.wait_recv()
        p = (d + ND - 1 - i) % ND
        expand(p, near_in[p])
    spread[0, d] = local_ref[0]
    spread[1, d] = local_ref[1]
    flat = (rows_all, nb * block)
    s0, s1 = spread[0, :ND].reshape(flat), spread[1, :ND].reshape(flat)
    near_run = Plane(links, npart).reduce(nland)
    for h in (0, 1):
        table = rounded[:, takes[h]]
        npart[h] = (dot(s0, table) + dot(s1, table)).reshape(4, 4, sel_dev, half)
        next(near_run)
    for i, copy in enumerate(far_copies):
        copy.wait_recv()
        p = (g + NG - 1 - i) % NG
        expand(ND + p, far_in[p])
    spread[:, ND + g] = jnp.zeros((2, sel_dev, nb * block), BF16)
    flat = (cols_all, nb * block)
    s0, s1 = spread[0, ND:].reshape(flat), spread[1, ND:].reshape(flat)
    fpart[...] = (dot(s0, rounded[...]) + dot(s1, rounded[...])).reshape(4, 2, sel_dev, feat)
    far_run = Line(links, fpart).reduce(fpair, fsmall)
    next(far_run)
    next(far_run)
    together(near_run, far_run, text_run)

    far_sum = fpart[x, c]
    for h in (0, 1):
        chosen[:, takes[h]] += npart[h, y, z] + far_sum[:, takes[h]]
    picked = chosen[...]
    picked_parts = split(picked)
    before = dot3(picked_parts, (wh[...], wl[...]))
    curve = 0.5 * (1.0 + lax.erf(before * ROOT_HALF))
    hidden = before * curve
    node_norm = jnp.sqrt(jnp.sum(hidden * hidden, axis=1, keepdims=True) + EPS)
    unit_nodes = hidden / node_norm
    for h in (0, 1):
        units[h, y, z] = unit_nodes[:, takes[h]]
    col_parts = split(cols[...].reshape(cols_all, feat))
    text_halves = [tuple(v[:, takes[h]] for v in col_parts) for h in (0, 1)]
    some = 4 * sel_dev

    def score(h, out):
        parts = split(Plane(links, units).at(h, out, None)[...].reshape(some, half))
        for v, into in zip(parts, (u_hi, u_lo)):
            Plane(links, into).at(h, out, None)[...] = v.reshape(4, sel_dev, half)
        part = dot3(parts, text_halves[h], 1, 1)
        Plane(links, score_ref).at(h, out, None)[...] = part.reshape(4, sel_dev, cols_all)

    unit_run = Plane(links, units).gather(score)
    next(unit_run)
    next(unit_run)
    lane = lax.broadcasted_iota(jnp.int32, (8, cols_all), 1)
    ids = ((lane // sel_dev * ND + d) * sel_dev + lane % sel_dev)[:1]
    tags = near_in[:, 2 * sel_dev :].astype(F32)
    parts = [tags[:, :, k : k + 1] * 64.0 + tags[:, :, k + 1 : k + 2] for k in (1, 3)]
    pair = jnp.concatenate(parts, axis=1).reshape(rows_all, 1)
    target = (pair == ids.astype(F32)).astype(F32)
    wide = jnp.concatenate(
        [v.astype(F32) for v in (*picked_parts, picked_parts[0])] + [jnp.zeros_like(picked)], axis=0
    )
    slices_out[...] = wide.T.astype(BF16).reshape(slices_out.shape)
    slices[d] = slices_out[d]
    together(unit_run)

    unit_parts = [tuple(v[h].reshape(rows_all, half) for v in (u_hi, u_lo)) for h in (0, 1)]
    scores = SCALE * (score_ref[0] + score_ref[1]).reshape(rows_all, cols_all)
    exps = jnp.exp(scores)
    row_in[d] = to_lanes(jnp.sum(exps, axis=1, keepdims=True))
    row_copies = links.all_dev(lambda e: row_in.at[d], row_in.at[d])
    col_sum = jnp.sum(exps, axis=0, keepdims=True)
    col_in[g] = jnp.broadcast_to(col_sum, (8, cols_all))
    col_copies = links.all_grp(lambda e: col_in.at[g], col_in.at[g])
    slice_copies = links.all_dev(lambda e: slices_out.at[e], slices.at[d])
    positive = jnp.sum(jnp.sum(target * scores, axis=1, keepdims=True), axis=0, keepdims=True)
    arrived(col_copies)
    col_total = jnp.sum(col_in[...], axis=0)[:1]
    arrived(row_copies)
    row_total = as_row(jnp.sum(row_in[...], axis=0), rows_all)
    row_recip = jnp.broadcast_to(1.0 / row_total, (128, rows_all)).T[:, :1]
    col_recip = 1.0 / col_total
    slope = 0.5 * exps * (row_recip + col_recip) - target
    slope_parts = split(slope)
    node_run = Plane(links, spart).reduce(sland)
    for h in (0, 1):
        spart[h] = dot3(slope_parts, text_halves[h]).reshape(4, 4, sel_dev, half)
        next(node_run)
    log_rows = jnp.sum(jnp.log(row_total), axis=1, keepdims=True)
    log_cols = jnp.sum(jnp.log(col_total), axis=1, keepdims=True)
    part = (log_rows / ND + log_cols / NG) / (2.0 * total_sel) - positive / total_sel
    loss_dev[d] = jnp.broadcast_to(part, (8, 128))
    for h in (0, 1):
        grown = dot3(slope_parts, unit_parts[h], 0, 0)
        tpart[:, :, :, takes[h]] = grown.reshape(4, 2, sel_dev, half)
    text_run = Line(links, tpart).reduce(tpair, tsmall)
    next(text_run)
    loss_copies = links.all_dev(lambda e: loss_dev.at[d], loss_dev.at[d])
    together(node_run, text_run)

    node_dir = SCALE * jnp.concatenate([spart[0, y, z], spart[1, y, z]], axis=1)
    node_back = (
        node_dir - unit_nodes * jnp.sum(unit_nodes * node_dir, axis=1, keepdims=True)
    ) / node_norm
    pre_grad = node_back * (curve + before * jnp.exp(-0.5 * before * before) * INV_ROOT_TWO_PI)
    for h in (0, 1):
        pre_all[h, y, z] = pre_grad[:, takes[h]]
    pieces = {0: 0.0, 1: 0.0}

    def weigh(h, out):
        hi, lo = split(Plane(links, pre_all).at(h, out, None)[...].reshape(some, half))
        for v, into in ((hi, p_hi), (lo, p_lo)):
            Plane(links, into).at(h, out, None)[...] = v.reshape(4, sel_dev, half)
        across = ((y if h == 0 else z) + out) % 4
        for k in range(4):
            rows = slice(k * sel_dev, (k + 1) * sel_dev)
            stack = jnp.concatenate([hi[rows], hi[rows], lo[rows], hi[rows]], axis=0)
            p = across * 4 + k if h == 0 else k * 4 + across
            pieces[h] += dot(slices[p], stack)

    pre_run = Plane(links, pre_all).gather(weigh)
    next(pre_run)
    row_grads = dot3(split(pre_grad), (wh[...], wl[...]), 1, 1)
    g_far[x, c] = row_grads.astype(BF16)
    far_run = Line(links, g_far).gather()
    next(far_run)
    arrived(slice_copies)
    next(pre_run)
    next(far_run)
    arrived(loss_copies)
    loss_grp[g] = jnp.sum(loss_dev[...], axis=0)
    loss_copies = links.all_grp(lambda e: loss_grp.at[g], loss_grp.at[g])
    for q in (0, 1):
        for i in range(NPEER // 4):
            rows = spread[q, 4 * i : 4 * i + 4].reshape(some, nb * block)
            spread_t[q, :, i * some : (i + 1) * some] = rows.astype(F32).T.astype(BF16)
    together(pre_run, far_run)

    pre_parts = [tuple(v[h].reshape(rows_all, half) for v in (p_hi, p_lo)) for h in (0, 1)]
    for h in (0, 1):
        gpart[:, h] = pieces[h].reshape(2, pieces[h].shape[0] // 2, half)
    core_copy = links.core(gpart.at[1 - c], gpair)
    group_grads = dot3(pre_parts[0], (wh[:, takes[0]], wl[:, takes[0]]), 1, 1)
    group_grads += dot3(pre_parts[1], (wh[:, takes[1]], wl[:, takes[1]]), 1, 1)
    group_grads = group_grads.astype(BF16)
    core_copy.wait_recv()
    gx[x] = gpart[c] + gpair[...]
    copies = [links.shift(gx.at[x], gx.at[x], "x", i) for i in (1, 2, 3)]

    spot = lax.broadcasted_iota(jnp.int32, (sel_dev, nodes_dev), 1)
    hot = (spot_ref[:, :1] == spot).astype(F32).astype(BF16)
    top, mid = split(row_grads)
    low = (row_grads - top.astype(F32) - mid.astype(F32)).astype(BF16)

    def node_grads(h):
        take = takes[h]
        near = group_grads[:, take]
        far = g_far[:, :, :, take].reshape(cols_all, half)
        total = dot(spread_t[0, :, :rows_all], near) + dot(spread_t[1, :, :rows_all], near)
        total += dot(spread_t[0, :, rows_all:], far) + dot(spread_t[1, :, rows_all:], far)
        total += dot(hot, top[:, take], 0, 0) + dot(hot, mid[:, take], 0, 0)
        gn_ref[:, take] = total + dot(hot, low[:, take], 0, 0)
        copy = pltpu.make_async_copy(gn_ref.at[:, take], gn_out.at[:, take], local_sem.at[2 + h])
        copy.start()
        return copy

    out_copies = [node_grads(0)]
    arrived(copies)
    gfull[c, :, y, z] = gx[0] + gx[1] + gx[2] + gx[3]
    crossings = []
    weight_plane = Plane(links, gfull.at[c])

    def cross(h, out):
        view = weight_plane.at(h, out, None)
        crossings.append(links.core(view, view))

    weight_run = weight_plane.gather(cross)
    next(weight_run)
    next(weight_run)
    out_copies.append(node_grads(1))
    text_dir = SCALE * tpart[x, c]
    gt_ref[...] = (
        text_dir - unit_texts * jnp.sum(unit_texts * text_dir, axis=1, keepdims=True)
    ) / text_norm
    arrived(loss_copies)
    loss_ref[...] = jnp.sum(loss_grp[...], axis=0)[:1, :1]
    together(weight_run)
    for i, core in enumerate((c, 1 - c)):
        if i:
            arrived(crossings)
        copy = pltpu.make_async_copy(gfull.at[core], gw_out.at[core], local_sem.at[4 + i])
        copy.start()
        out_copies.append(copy)
    for copy in links.copies:
        copy.wait_send()
    for copy in out_copies:
        copy.wait()


def finish_kernel(
    loss_in, gn_in, gw_in, gt_in,
    loss_out, gn_out, gw_out, gt_out,
    gn, gw, gt, in_sem, out_sem,
):
    half = gw_in.shape[5]
    rows = gn_in.shape[0] // 4
    steps = []
    for i in range(4):
        some = pl.ds(i * rows, rows)
        steps.append((gn_in.at[some], gn.at[some], gn_out.at[some]))
    for core in (0, 1):
        for h in (0, 1):
            for y in (0, 2):
                some = pl.ds(y, 2)
                out = gw_out.at[some, :, core, :, pl.ds(h * half, half)]
                steps.append((gw_in.at[core, h, some], gw.at[core, h, some], out))
    steps.append((gt_in, gt, gt_out))
    fetches = [pltpu.make_async_copy(a, b, in_sem.at[i]) for i, (a, b, _) in enumerate(steps)]
    stores = [pltpu.make_async_copy(b, c, out_sem.at[i]) for i, (_, b, c) in enumerate(steps)]
    for copy in fetches:
        copy.start()
    loss_out[...] = loss_in[...]
    for fetch, store in zip(fetches, stores):
        fetch.wait()
        store.start()
    for copy in stores:
        copy.wait()


def shards(node_features, tiles, tile_list, weight, texts, selected, pairing):
    block = tiles.shape[1]
    nodes_dev, feat = node_features.shape
    sel_dev = selected.shape[0]
    nb = nodes_dev // block
    half = feat // 2
    deep = feat // 32
    vmem = pl.BlockSpec(memory_space=pltpu.VMEM)
    smem = pl.BlockSpec(memory_space=pltpu.SMEM)
    hbm = pl.BlockSpec(memory_space=pl.ANY)
    made = pl.pallas_call(
        prep_kernel,
        out_shape=(
            jax.ShapeDtypeStruct((NPEER + 1, 2 * sel_dev + 16, block), BF16),
            jax.ShapeDtypeStruct((2, sel_dev, nb * block), BF16),
            jax.ShapeDtypeStruct((sel_dev, block), jnp.int32),
            jax.ShapeDtypeStruct((sel_dev,), jnp.int32),
        ),
        in_specs=[hbm, smem, smem, hbm],
        out_specs=(vmem, vmem, vmem, smem),
        scratch_shapes=[
            pltpu.VMEM((nb, sel_dev, block), F32),
            pltpu.VMEM((nb, sel_dev, block), BF16),
            pltpu.VMEM((sel_dev, block), jnp.int32),
            pltpu.SMEM((NPEER + 1,), jnp.int32),
            pltpu.SMEM((NPEER + 1,), jnp.int32),
            pltpu.SMEM((2, 256), jnp.int32),
            pltpu.VMEM(tiles.shape, BF16),
            pltpu.SemaphoreType.DMA,
            pltpu.SemaphoreType.DMA((4,)),
        ],
        compiler_params=pltpu.CompilerParams(vmem_limit_bytes=60 * 2**20),
    )(tile_list.T, selected, pairing, tiles)

    def f32(*shape):
        return pltpu.VMEM(shape, F32)

    def bf16(*shape):
        return pltpu.VMEM(shape, BF16)

    plane = f32(2, 4, 4, sel_dev, half)
    landing = f32(2, 15, sel_dev, half)
    line = [f32(4, 2, sel_dev, feat), f32(4, sel_dev, feat), f32(3, sel_dev, feat)]
    results = pl.pallas_call(
        main_kernel,
        out_shape=(
            jax.ShapeDtypeStruct((1, 1), F32),
            jax.ShapeDtypeStruct((nodes_dev, feat), F32),
            jax.ShapeDtypeStruct((2, 2, 4, 4, deep, half), F32),
            jax.ShapeDtypeStruct((sel_dev, feat), F32),
        ),
        in_specs=[vmem, vmem, vmem, smem, hbm, hbm, vmem],
        out_specs=(vmem, hbm, hbm, vmem),
        scratch_shapes=[
            f32(nodes_dev, feat),
            f32(feat, feat),
            bf16(nodes_dev, feat),
            f32(nodes_dev, feat),
            bf16(ND, 2 * sel_dev + 16, block),
            bf16(NG, 2 * sel_dev + 16, block),
            bf16(2, NPEER, sel_dev, nb * block),
            bf16(2, nb * block, NPEER * sel_dev),
            bf16(feat, feat),
            bf16(feat, feat),
            plane, landing, *line,
            plane, f32(4, 2, sel_dev, feat),
            plane, landing, *line,
            f32(ND, 8, 128),
            f32(NG, 8, NG * sel_dev),
            f32(ND, 8, 128),
            f32(NG, 8, 128),
            bf16(ND, 2 * deep, 4 * sel_dev),
            bf16(ND, 2 * deep, 4 * sel_dev),
            plane,
            bf16(4, 2, sel_dev, feat),
            *[bf16(2, 4, 4, sel_dev, half)] * 4,
            f32(2, 4, 4, sel_dev, NG * sel_dev),
            f32(2, 2, deep, half),
            f32(2, deep, half),
            f32(4, 2, deep, half),
            f32(2, 2, 4, 4, deep, half),
            f32(sel_dev, feat),
            pltpu.SemaphoreType.DMA((SEMS,)),
            pltpu.SemaphoreType.DMA((SEMS,)),
            pltpu.SemaphoreType.DMA((6,)),
        ],
        compiler_params=pltpu.CompilerParams(
            collective_id=0, has_side_effects=True, vmem_limit_bytes=60 * 2**20
        ),
    )(*made, node_features, weight, texts)
    loss, grad_nodes, grad_weight, grad_texts = pl.pallas_call(
        finish_kernel,
        out_shape=(
            jax.ShapeDtypeStruct((1, 1), F32),
            jax.ShapeDtypeStruct((nodes_dev, feat), F32),
            jax.ShapeDtypeStruct((4, 4, 2, deep, feat), F32),
            jax.ShapeDtypeStruct((sel_dev, feat), F32),
        ),
        in_specs=[vmem, hbm, hbm, hbm],
        out_specs=(vmem, hbm, hbm, hbm),
        scratch_shapes=[
            f32(nodes_dev, feat),
            f32(2, 2, 4, 4, deep, half),
            f32(sel_dev, feat),
            pltpu.SemaphoreType.DMA((13,)),
            pltpu.SemaphoreType.DMA((13,)),
        ],
        compiler_params=pltpu.CompilerParams(vmem_limit_bytes=60 * 2**20),
    )(*results)
    return loss.reshape(()), grad_nodes, grad_weight.reshape(feat, feat), grad_texts


def solution(mesh):
    both = ("grp", "dev")
    placed = (
        P(both, None),
        P(both, None, None),
        P(),
        P(),
        P(both, None),
        P(both),
        P(both),
    )
    return jax.shard_map(
        shards,
        mesh=mesh,
        in_specs=placed,
        out_specs=(P(), P(both, None), P(), P(both, None)),
        check_vma=False,
    )
```

```python
import functools

import jax
import jax.numpy as jnp
from jax import lax
from jax.experimental import pallas as pl
from jax.experimental.pallas import tpu as pltpu
from jax.sharding import PartitionSpec as P

MESH = pl.DeviceIdType.MESH
CAP = 2
SCALE = 1.0 / 0.07
EPS = 1e-06
ROOT_HALF = 0.7071067811865476
INV_ROOT_TWO_PI = 0.3989422804014327
F32 = jnp.float32
BF16 = jnp.bfloat16
NG, ND = 8, 16
NPEER = NG + ND
SEMS = 384


def split(value):
    hi = value.astype(BF16)
    return hi, (value - hi.astype(F32)).astype(BF16)


def dot(a, b, ca=1, cb=0):
    return lax.dot_general(a, b, (((ca,), (cb,)), ((), ())), preferred_element_type=F32)


def dot3(a, b, ca=1, cb=0):
    return dot(a[0], b[0], ca, cb) + (dot(a[0], b[1], ca, cb) + dot(a[1], b[0], ca, cb))


def prep_kernel(
    list_ref, sel_ref, pair_ref, tiles_hbm,
    rows_ref, local_ref, spot_ref, own_ref,
    acc, onehot, column, count, meta, window, tiles_ref, sem, tiles_sem,
):
    g, d = lax.axis_index("grp"), lax.axis_index("dev")
    device = g * ND + d
    n_tiles, block = tiles_hbm.shape[0], tiles_hbm.shape[1]
    wide = window.shape[1]
    first = jnp.minimum(device * n_tiles // 128 * 128, list_ref.shape[1] - wide)
    first = pl.multiple_of(first, 128)
    fetch = pltpu.make_async_copy(list_ref.at[:, pl.ds(first, wide)], window, sem)
    fetch.start()
    chunk = n_tiles // 4
    chunks = []
    for i in range(4):
        some = pl.ds(i * chunk, chunk)
        chunks.append(
            pltpu.make_async_copy(tiles_hbm.at[some], tiles_ref.at[some], tiles_sem.at[i])
        )
        chunks[i].start()
    sel_dev = sel_ref.shape[0]
    nb = local_ref.shape[2] // block
    nodes_dev = nb * block
    rows_ref[...] = jnp.zeros_like(rows_ref)
    acc[...] = jnp.zeros_like(acc)
    for k in range(sel_dev):
        own = sel_ref[k] - device * nodes_dev
        own_ref[k] = own
        spot_ref[pl.ds(k, 1), :] = jnp.full((1, block), own, jnp.int32)
        column[pl.ds(k, 1), :] = jnp.full((1, block), pair_ref[k], jnp.int32)
    lane = lax.broadcasted_iota(jnp.int32, (sel_dev, block), 1)
    sel = spot_ref[...]
    for b in range(nb):
        onehot[b] = (sel == lane + b * block).astype(F32).astype(BF16)
    for p in range(NPEER + 1):
        count[p] = 0
        meta[p] = 0
    fetch.wait()
    skip = device * n_tiles - first
    for t in range(n_tiles):
        if t % chunk == 0:
            chunks[t // chunk].wait()
        row_block = window[0, skip + t] - device * nb
        col = window[1, skip + t]
        owner = col // nb
        col_block = col - owner * nb
        og = owner // ND
        od = owner - og * ND
        local = owner == device
        peer = jnp.where(local, NPEER, jnp.where(og == g, od, ND + og))
        rank = jnp.minimum(count[peer], 1)
        count[peer] = rank + 1
        meta[peer] = meta[peer] + col_block * jnp.where(rank == 0, 1, nb)
        picked = dot(onehot[row_block], tiles_ref[t])
        start = pl.multiple_of(rank * sel_dev, sel_dev)
        rows_ref[peer, pl.ds(start, sel_dev)] = picked.astype(BF16)
        acc[col_block] += picked * local.astype(F32)
    pair = column[...]
    high = pair // 64
    low = pair - high * 64
    lane = lane[:16]
    tag = jnp.where(lane == 1, high[:16], low[:16])
    tag = jnp.where(lane == 3, high[16:], jnp.where(lane == 4, low[16:], tag))
    tail = pl.ds(2 * sel_dev, 16)
    for p in range(NPEER):
        rows_ref[p, tail] = jnp.where(lane == 0, meta[p], tag).astype(F32).astype(BF16)
    for b in range(nb):
        hi, lo = split(acc[b])
        local_ref[0, :, b * block : (b + 1) * block] = hi
        local_ref[1, :, b * block : (b + 1) * block] = lo


class Links:
    def __init__(self, send_sem, recv_sem):
        self.g, self.d = lax.axis_index("grp"), lax.axis_index("dev")
        self.x, self.c = self.g // 2, self.g % 2
        self.y, self.z = self.d // 4, self.d % 4
        self.send_sem, self.recv_sem = send_sem, recv_sem
        self.used, self.copies = 0, []

    def to(self, src, dst, grp=None, dev=None):
        k = self.used
        self.used += 1
        copy = pltpu.make_async_remote_copy(
            src_ref=src,
            dst_ref=dst,
            send_sem=self.send_sem.at[k],
            recv_sem=self.recv_sem.at[k],
            device_id=(self.g if grp is None else grp, self.d if dev is None else dev),
            device_id_type=MESH,
        )
        copy.start()
        self.copies.append(copy)
        return copy

    def pos(self, axis):
        return {"x": self.x, "y": self.y, "z": self.z}[axis]

    def shift(self, src, dst, axis, step):
        if axis == "x":
            return self.to(src, dst, grp=(self.x + step) % 4 * 2 + self.c)
        if axis == "y":
            return self.to(src, dst, dev=(self.y + step) % 4 * 4 + self.z)
        return self.to(src, dst, dev=self.y * 4 + (self.z + step) % 4)

    def core(self, src, dst):
        return self.to(src, dst, grp=self.x * 2 + 1 - self.c)

    def all_dev(self, src, dst):
        out = []
        for i in range(1, ND):
            e = (self.d + i) % ND
            out.append(self.to(src(e), dst, dev=e))
        return out

    def all_grp(self, src, dst):
        out = []
        for i in range(1, NG):
            e = (self.g + i) % NG
            out.append(self.to(src(e), dst, grp=e))
        return out


def arrived(copies):
    for copy in copies:
        copy.wait_recv()


class Plane:
    def __init__(self, links, buf):
        self.links, self.buf = links, buf
        self.outer, self.inner = ("y", "z"), ("z", "y")

    def at(self, h, out, into):
        links = self.links
        out = (links.pos(self.outer[h]) + out) % 4
        if into is None:
            return self.buf.at[0, out] if h == 0 else self.buf.at[1, :, out]
        into = (links.pos(self.inner[h]) + into) % 4
        return self.buf.at[0, out, into] if h == 0 else self.buf.at[1, into, out]

    def gather(self, on=lambda h, out: None):
        shift, at, outer, inner = self.links.shift, self.at, self.outer, self.inner
        near, away = {}, {}

        def send_out(h, o):
            view = at(h, 0, o)
            for i in (2, 1, 3):
                away[h, i, o] = shift(view, view, outer[h], i)

        for h in (0, 1):
            view = at(h, 0, 0)
            for i in (2, 1, 3):
                near[h, i] = shift(view, view, inner[h], i)
        for h in (0, 1):
            send_out(h, 0)
        yield
        for i in (2, 1, 3):
            for h in (0, 1):
                near[h, i].wait_recv()
                send_out(h, 4 - i)
        yield
        for h in (0, 1):
            on(h, 0)
        for i in (2, 1, 3):
            for h in (0, 1):
                for o in (0, 2, 3, 1):
                    away[h, i, o].wait_recv()
                on(h, 4 - i)
        yield

    def reduce(self, land):
        shift, at, outer, inner = self.links.shift, self.at, self.outer, self.inner
        order = (2, 1, 3, 0)
        away, near = {}, {}
        for h in (0, 1):
            for o in order:
                for i in (2, 1, 3):
                    away[h, i, o] = shift(at(h, i, o), land.at[h, 4 * (i - 1) + o], outer[h], i)
            yield
        for o in order:
            for h in (0, 1):
                for i in (2, 1, 3):
                    away[h, i, o].wait_recv()
                view = at(h, 0, o)
                view[...] += land[h, o] + land[h, 4 + o] + land[h, 8 + o]
                if o:
                    near[h, o] = shift(view, land.at[h, 11 + o], inner[h], o)
            yield
        for h in (0, 1):
            for o in (2, 1, 3):
                near[h, o].wait_recv()
            view = at(h, 0, 0)
            view[...] += land[h, 12] + land[h, 13] + land[h, 14]
        yield


class Line:
    def __init__(self, links, buf):
        self.links, self.buf = links, buf

    def gather(self):
        links = self.links
        x, c = links.x, links.c
        own = self.buf.at[x, c]
        ways = [links.shift(own, own, "x", i) for i in (2, 1, 3)]
        crossed = [links.core(own, own)]
        yield
        for i, way in zip((2, 1, 3), ways):
            way.wait_recv()
            view = self.buf.at[(x + 4 - i) % 4, c]
            crossed.append(links.core(view, view))
        yield
        arrived(crossed)
        yield

    def reduce(self, pair, land):
        links = self.links
        x, c = links.x, links.c
        copy = links.core(self.buf.at[:, 1 - c], pair)
        yield
        copy.wait_recv()
        view = self.buf.at[:, c]
        view[...] += pair[...]
        ways = [
            links.shift(self.buf.at[(x + i) % 4, c], land.at[i - 1], "x", i) for i in (2, 1, 3)
        ]
        yield
        arrived(ways)
        view = self.buf.at[x, c]
        view[...] += land[0] + land[1] + land[2]
        yield


def together(*runs):
    runs = list(runs)
    while runs:
        runs = [run for run in runs if next(run, "end") != "end"]


def to_lanes(column):
    n = column.shape[0]
    wide = jnp.broadcast_to(column, (n, 128)).T
    rows = [wide[:1, 128 * i : 128 * (i + 1)] for i in range(n // 128)]
    return jnp.concatenate(rows + [jnp.zeros((8 - len(rows), 128), F32)], axis=0)


def as_row(packed, n):
    return jnp.concatenate([packed[i : i + 1] for i in range(n // 128)], axis=1)


def main_kernel(
    rows_ref, local_ref, spot_ref, own_ref, nodes_hbm, weight_hbm, texts_ref,
    loss_ref, gn_out, gw_out, gt_ref,
    nodes_ref, weight_ref, rounded, gn_ref,
    near_in, far_in, spread, spread_t, wh, wl,
    npart, nland, fpart, fpair, fsmall,
    units, cols, spart, sland, tpart, tpair, tsmall,
    row_in, col_in, loss_dev, loss_grp, slices_out, slices, pre_all, g_far,
    u_hi, u_lo, p_hi, p_lo, score_ref,
    gpart, gpair, gx, gfull, chosen,
    send_sem, recv_sem, local_sem,
):
    links = Links(send_sem, recv_sem)
    g, d, x, c, y, z = links.g, links.d, links.x, links.c, links.y, links.z
    sel_dev, feat = texts_ref.shape
    half = feat // 2
    nodes_dev = nodes_ref.shape[0]
    block = near_in.shape[2]
    nb = nodes_dev // block
    total_sel = sel_dev * NG * ND
    rows_all = ND * sel_dev
    cols_all = NG * sel_dev
    takes = [slice(h * half, (h + 1) * half) for h in (0, 1)]

    barrier = pltpu.get_barrier_semaphore()
    for i in range(1, ND):
        pl.semaphore_signal(barrier, inc=1, device_id=(g, (d + i) % ND), device_id_type=MESH)
    for i in range(1, NG):
        pl.semaphore_signal(barrier, inc=1, device_id=((g + i) % NG, d), device_id_type=MESH)

    nodes_copy = pltpu.make_async_copy(nodes_hbm, nodes_ref, local_sem.at[0])
    weight_copy = pltpu.make_async_copy(weight_hbm, weight_ref, local_sem.at[1])
    nodes_copy.start()
    weight_copy.start()

    texts = texts_ref[...]
    text_norm = jnp.sqrt(jnp.sum(texts * texts, axis=1, keepdims=True) + EPS)
    unit_texts = texts / text_norm
    cols[x, c] = unit_texts
    near_in[d] = rows_ref[d]
    pl.semaphore_wait(barrier, ND + NG - 2)

    near_copies = links.all_dev(lambda e: rows_ref.at[e], near_in.at[d])
    far_copies = links.all_grp(lambda e: rows_ref.at[ND + e], far_in.at[g])
    text_run = Line(links, cols).gather()
    next(text_run)
    nodes_copy.wait()
    rounded[...] = nodes_ref[...].astype(BF16)
    for k in range(sel_dev):
        chosen[pl.ds(k, 1), :] = nodes_ref[pl.ds(own_ref[k], 1), :]
    weight_copy.wait()
    hi, lo = split(weight_ref[...])
    wh[...] = hi
    wl[...] = lo

    def expand(into, rows):
        tag = rows[2 * sel_dev :].astype(F32)[:1, :1]
        second = jnp.floor(tag * (1.0 / nb) + 0.01)
        first = tag - second * nb
        for q, which in ((0, first), (1, second)):
            for b in range(nb):
                spread[q, into, :, b * block : (b + 1) * block] = jnp.where(
                    which == float(b), rows[q * sel_dev : (q + 1) * sel_dev].astype(F32), 0.0
                ).astype(BF16)

    for i, copy in enumerate(near_copies):
        copy.wait_recv()
        p = (d + ND - 1 - i) % ND
        expand(p, near_in[p])
    spread[0, d] = local_ref[0]
    spread[1, d] = local_ref[1]
    flat = (rows_all, nb * block)
    s0, s1 = spread[0, :ND].reshape(flat), spread[1, :ND].reshape(flat)
    near_run = Plane(links, npart).reduce(nland)
    for h in (0, 1):
        table = rounded[:, takes[h]]
        npart[h] = (dot(s0, table) + dot(s1, table)).reshape(4, 4, sel_dev, half)
        next(near_run)
    for i, copy in enumerate(far_copies):
        copy.wait_recv()
        p = (g + NG - 1 - i) % NG
        expand(ND + p, far_in[p])
    spread[:, ND + g] = jnp.zeros((2, sel_dev, nb * block), BF16)
    flat = (cols_all, nb * block)
    s0, s1 = spread[0, ND:].reshape(flat), spread[1, ND:].reshape(flat)
    fpart[...] = (dot(s0, rounded[...]) + dot(s1, rounded[...])).reshape(4, 2, sel_dev, feat)
    far_run = Line(links, fpart).reduce(fpair, fsmall)
    next(far_run)
    next(far_run)
    together(near_run, far_run, text_run)

    far_sum = fpart[x, c]
    for h in (0, 1):
        chosen[:, takes[h]] += npart[h, y, z] + far_sum[:, takes[h]]
    picked = chosen[...]
    picked_parts = split(picked)
    before = dot3(picked_parts, (wh[...], wl[...]))
    curve = 0.5 * (1.0 + lax.erf(before * ROOT_HALF))
    hidden = before * curve
    node_norm = jnp.sqrt(jnp.sum(hidden * hidden, axis=1, keepdims=True) + EPS)
    unit_nodes = hidden / node_norm
    for h in (0, 1):
        units[h, y, z] = unit_nodes[:, takes[h]]
    col_parts = split(cols[...].reshape(cols_all, feat))
    text_halves = [tuple(v[:, takes[h]] for v in col_parts) for h in (0, 1)]
    some = 4 * sel_dev

    def score(h, out):
        parts = split(Plane(links, units).at(h, out, None)[...].reshape(some, half))
        for v, into in zip(parts, (u_hi, u_lo)):
            Plane(links, into).at(h, out, None)[...] = v.reshape(4, sel_dev, half)
        part = dot3(parts, text_halves[h], 1, 1)
        Plane(links, score_ref).at(h, out, None)[...] = part.reshape(4, sel_dev, cols_all)

    unit_run = Plane(links, units).gather(score)
    next(unit_run)
    next(unit_run)
    lane = lax.broadcasted_iota(jnp.int32, (8, cols_all), 1)
    ids = ((lane // sel_dev * ND + d) * sel_dev + lane % sel_dev)[:1]
    tags = near_in[:, 2 * sel_dev :].astype(F32)
    parts = [tags[:, :, k : k + 1] * 64.0 + tags[:, :, k + 1 : k + 2] for k in (1, 3)]
    pair = jnp.concatenate(parts, axis=1).reshape(rows_all, 1)
    target = (pair == ids.astype(F32)).astype(F32)
    wide = jnp.concatenate(
        [v.astype(F32) for v in (*picked_parts, picked_parts[0])] + [jnp.zeros_like(picked)], axis=0
    )
    slices_out[...] = wide.T.astype(BF16).reshape(slices_out.shape)
    slices[d] = slices_out[d]
    together(unit_run)

    unit_parts = [tuple(v[h].reshape(rows_all, half) for v in (u_hi, u_lo)) for h in (0, 1)]
    scores = SCALE * (score_ref[0] + score_ref[1]).reshape(rows_all, cols_all)
    exps = jnp.exp(scores)
    row_in[d] = to_lanes(jnp.sum(exps, axis=1, keepdims=True))
    row_copies = links.all_dev(lambda e: row_in.at[d], row_in.at[d])
    col_sum = jnp.sum(exps, axis=0, keepdims=True)
    col_in[g] = jnp.broadcast_to(col_sum, (8, cols_all))
    col_copies = links.all_grp(lambda e: col_in.at[g], col_in.at[g])
    slice_copies = links.all_dev(lambda e: slices_out.at[e], slices.at[d])
    positive = jnp.sum(jnp.sum(target * scores, axis=1, keepdims=True), axis=0, keepdims=True)
    arrived(col_copies)
    col_total = jnp.sum(col_in[...], axis=0)[:1]
    arrived(row_copies)
    row_total = as_row(jnp.sum(row_in[...], axis=0), rows_all)
    row_recip = jnp.broadcast_to(1.0 / row_total, (128, rows_all)).T[:, :1]
    col_recip = 1.0 / col_total
    slope = 0.5 * exps * (row_recip + col_recip) - target
    slope_parts = split(slope)
    node_run = Plane(links, spart).reduce(sland)
    for h in (0, 1):
        spart[h] = dot3(slope_parts, text_halves[h]).reshape(4, 4, sel_dev, half)
        next(node_run)
    log_rows = jnp.sum(jnp.log(row_total), axis=1, keepdims=True)
    log_cols = jnp.sum(jnp.log(col_total), axis=1, keepdims=True)
    part = (log_rows / ND + log_cols / NG) / (2.0 * total_sel) - positive / total_sel
    loss_dev[d] = jnp.broadcast_to(part, (8, 128))
    for h in (0, 1):
        grown = dot3(slope_parts, unit_parts[h], 0, 0)
        tpart[:, :, :, takes[h]] = grown.reshape(4, 2, sel_dev, half)
    text_run = Line(links, tpart).reduce(tpair, tsmall)
    next(text_run)
    loss_copies = links.all_dev(lambda e: loss_dev.at[d], loss_dev.at[d])
    together(node_run, text_run)

    node_dir = SCALE * jnp.concatenate([spart[0, y, z], spart[1, y, z]], axis=1)
    node_back = (
        node_dir - unit_nodes * jnp.sum(unit_nodes * node_dir, axis=1, keepdims=True)
    ) / node_norm
    pre_grad = node_back * (curve + before * jnp.exp(-0.5 * before * before) * INV_ROOT_TWO_PI)
    for h in (0, 1):
        pre_all[h, y, z] = pre_grad[:, takes[h]]
    pieces = {0: 0.0, 1: 0.0}

    def weigh(h, out):
        hi, lo = split(Plane(links, pre_all).at(h, out, None)[...].reshape(some, half))
        for v, into in ((hi, p_hi), (lo, p_lo)):
            Plane(links, into).at(h, out, None)[...] = v.reshape(4, sel_dev, half)
        across = ((y if h == 0 else z) + out) % 4
        for k in range(4):
            rows = slice(k * sel_dev, (k + 1) * sel_dev)
            stack = jnp.concatenate([hi[rows], hi[rows], lo[rows], hi[rows]], axis=0)
            p = across * 4 + k if h == 0 else k * 4 + across
            pieces[h] += dot(slices[p], stack)

    pre_run = Plane(links, pre_all).gather(weigh)
    next(pre_run)
    row_grads = dot3(split(pre_grad), (wh[...], wl[...]), 1, 1)
    g_far[x, c] = row_grads.astype(BF16)
    far_run = Line(links, g_far).gather()
    next(far_run)
    arrived(slice_copies)
    next(pre_run)
    next(far_run)
    arrived(loss_copies)
    loss_grp[g] = jnp.sum(loss_dev[...], axis=0)
    loss_copies = links.all_grp(lambda e: loss_grp.at[g], loss_grp.at[g])
    for q in (0, 1):
        for i in range(NPEER // 4):
            rows = spread[q, 4 * i : 4 * i + 4].reshape(some, nb * block)
            spread_t[q, :, i * some : (i + 1) * some] = rows.astype(F32).T.astype(BF16)
    together(pre_run, far_run)

    pre_parts = [tuple(v[h].reshape(rows_all, half) for v in (p_hi, p_lo)) for h in (0, 1)]
    for h in (0, 1):
        gpart[:, h] = pieces[h].reshape(2, pieces[h].shape[0] // 2, half)
    core_copy = links.core(gpart.at[1 - c], gpair)
    group_grads = dot3(pre_parts[0], (wh[:, takes[0]], wl[:, takes[0]]), 1, 1)
    group_grads += dot3(pre_parts[1], (wh[:, takes[1]], wl[:, takes[1]]), 1, 1)
    group_grads = group_grads.astype(BF16)
    core_copy.wait_recv()
    gx[x] = gpart[c] + gpair[...]
    copies = [links.shift(gx.at[x], gx.at[x], "x", i) for i in (1, 2, 3)]

    spot = lax.broadcasted_iota(jnp.int32, (sel_dev, nodes_dev), 1)
    hot = (spot_ref[:, :1] == spot).astype(F32).astype(BF16)
    top, mid = split(row_grads)
    low = (row_grads - top.astype(F32) - mid.astype(F32)).astype(BF16)

    def node_grads(h):
        take = takes[h]
        near = group_grads[:, take]
        far = g_far[:, :, :, take].reshape(cols_all, half)
        total = dot(spread_t[0, :, :rows_all], near) + dot(spread_t[1, :, :rows_all], near)
        total += dot(spread_t[0, :, rows_all:], far) + dot(spread_t[1, :, rows_all:], far)
        total += dot(hot, top[:, take], 0, 0) + dot(hot, mid[:, take], 0, 0)
        gn_ref[:, take] = total + dot(hot, low[:, take], 0, 0)
        copy = pltpu.make_async_copy(gn_ref.at[:, take], gn_out.at[:, take], local_sem.at[2 + h])
        copy.start()
        return copy

    out_copies = [node_grads(0), node_grads(1)]
    text_dir = SCALE * tpart[x, c]
    gt_ref[...] = (
        text_dir - unit_texts * jnp.sum(unit_texts * text_dir, axis=1, keepdims=True)
    ) / text_norm
    arrived(loss_copies)
    loss_ref[...] = jnp.sum(loss_grp[...], axis=0)[:1, :1]
    arrived(copies)
    gfull[c, :, y, z] = gx[0] + gx[1] + gx[2] + gx[3]
    crossings = []
    weight_plane = Plane(links, gfull.at[c])

    def cross(h, out):
        view = weight_plane.at(h, out, None)
        crossings.append(links.core(view, view))

    weight_run = weight_plane.gather(cross)
    next(weight_run)
    next(weight_run)
    together(weight_run)
    for i, core in enumerate((c, 1 - c)):
        if i:
            arrived(crossings)
        copy = pltpu.make_async_copy(gfull.at[core], gw_out.at[core], local_sem.at[4 + i])
        copy.start()
        out_copies.append(copy)
    for copy in links.copies:
        copy.wait_send()
    for copy in out_copies:
        copy.wait()


def finish_kernel(
    loss_in, gn_in, gw_in, gt_in,
    loss_out, gn_out, gw_out, gt_out,
    gn, gw, gt, in_sem, out_sem,
):
    half = gw_in.shape[5]
    rows = gn_in.shape[0] // 4
    steps = []
    for i in range(4):
        some = pl.ds(i * rows, rows)
        steps.append((gn_in.at[some], gn.at[some], gn_out.at[some]))
    for core in (0, 1):
        for h in (0, 1):
            for y in (0, 2):
                some = pl.ds(y, 2)
                out = gw_out.at[some, :, core, :, pl.ds(h * half, half)]
                steps.append((gw_in.at[core, h, some], gw.at[core, h, some], out))
    steps.append((gt_in, gt, gt_out))
    fetches = [pltpu.make_async_copy(a, b, in_sem.at[i]) for i, (a, b, _) in enumerate(steps)]
    stores = [pltpu.make_async_copy(b, c, out_sem.at[i]) for i, (_, b, c) in enumerate(steps)]
    for copy in fetches:
        copy.start()
    loss_out[...] = loss_in[...]
    for fetch, store in zip(fetches, stores):
        fetch.wait()
        store.start()
    for copy in stores:
        copy.wait()


def shards(node_features, tiles, tile_list, weight, texts, selected, pairing):
    block = tiles.shape[1]
    nodes_dev, feat = node_features.shape
    sel_dev = selected.shape[0]
    nb = nodes_dev // block
    half = feat // 2
    deep = feat // 32
    vmem = pl.BlockSpec(memory_space=pltpu.VMEM)
    smem = pl.BlockSpec(memory_space=pltpu.SMEM)
    hbm = pl.BlockSpec(memory_space=pl.ANY)
    made = pl.pallas_call(
        prep_kernel,
        out_shape=(
            jax.ShapeDtypeStruct((NPEER + 1, 2 * sel_dev + 16, block), BF16),
            jax.ShapeDtypeStruct((2, sel_dev, nb * block), BF16),
            jax.ShapeDtypeStruct((sel_dev, block), jnp.int32),
            jax.ShapeDtypeStruct((sel_dev,), jnp.int32),
        ),
        in_specs=[hbm, smem, smem, hbm],
        out_specs=(vmem, vmem, vmem, smem),
        scratch_shapes=[
            pltpu.VMEM((nb, sel_dev, block), F32),
            pltpu.VMEM((nb, sel_dev, block), BF16),
            pltpu.VMEM((sel_dev, block), jnp.int32),
            pltpu.SMEM((NPEER + 1,), jnp.int32),
            pltpu.SMEM((NPEER + 1,), jnp.int32),
            pltpu.SMEM((2, 256), jnp.int32),
            pltpu.VMEM(tiles.shape, BF16),
            pltpu.SemaphoreType.DMA,
            pltpu.SemaphoreType.DMA((4,)),
        ],
        compiler_params=pltpu.CompilerParams(vmem_limit_bytes=60 * 2**20),
    )(tile_list.T, selected, pairing, tiles)

    def f32(*shape):
        return pltpu.VMEM(shape, F32)

    def bf16(*shape):
        return pltpu.VMEM(shape, BF16)

    plane = f32(2, 4, 4, sel_dev, half)
    landing = f32(2, 15, sel_dev, half)
    line = [f32(4, 2, sel_dev, feat), f32(4, sel_dev, feat), f32(3, sel_dev, feat)]
    results = pl.pallas_call(
        main_kernel,
        out_shape=(
            jax.ShapeDtypeStruct((1, 1), F32),
            jax.ShapeDtypeStruct((nodes_dev, feat), F32),
            jax.ShapeDtypeStruct((2, 2, 4, 4, deep, half), F32),
            jax.ShapeDtypeStruct((sel_dev, feat), F32),
        ),
        in_specs=[vmem, vmem, vmem, smem, hbm, hbm, vmem],
        out_specs=(vmem, hbm, hbm, vmem),
        scratch_shapes=[
            f32(nodes_dev, feat),
            f32(feat, feat),
            bf16(nodes_dev, feat),
            f32(nodes_dev, feat),
            bf16(ND, 2 * sel_dev + 16, block),
            bf16(NG, 2 * sel_dev + 16, block),
            bf16(2, NPEER, sel_dev, nb * block),
            bf16(2, nb * block, NPEER * sel_dev),
            bf16(feat, feat),
            bf16(feat, feat),
            plane, landing, *line,
            plane, f32(4, 2, sel_dev, feat),
            plane, landing, *line,
            f32(ND, 8, 128),
            f32(NG, 8, NG * sel_dev),
            f32(ND, 8, 128),
            f32(NG, 8, 128),
            bf16(ND, 2 * deep, 4 * sel_dev),
            bf16(ND, 2 * deep, 4 * sel_dev),
            plane,
            bf16(4, 2, sel_dev, feat),
            *[bf16(2, 4, 4, sel_dev, half)] * 4,
            f32(2, 4, 4, sel_dev, NG * sel_dev),
            f32(2, 2, deep, half),
            f32(2, deep, half),
            f32(4, 2, deep, half),
            f32(2, 2, 4, 4, deep, half),
            f32(sel_dev, feat),
            pltpu.SemaphoreType.DMA((SEMS,)),
            pltpu.SemaphoreType.DMA((SEMS,)),
            pltpu.SemaphoreType.DMA((6,)),
        ],
        compiler_params=pltpu.CompilerParams(
            collective_id=0, has_side_effects=True, vmem_limit_bytes=60 * 2**20
        ),
    )(*made, node_features, weight, texts)
    loss, grad_nodes, grad_weight, grad_texts = pl.pallas_call(
        finish_kernel,
        out_shape=(
            jax.ShapeDtypeStruct((1, 1), F32),
            jax.ShapeDtypeStruct((nodes_dev, feat), F32),
            jax.ShapeDtypeStruct((4, 4, 2, deep, feat), F32),
            jax.ShapeDtypeStruct((sel_dev, feat), F32),
        ),
        in_specs=[vmem, hbm, hbm, hbm],
        out_specs=(vmem, hbm, hbm, hbm),
        scratch_shapes=[
            f32(nodes_dev, feat),
            f32(2, 2, 4, 4, deep, half),
            f32(sel_dev, feat),
            pltpu.SemaphoreType.DMA((13,)),
            pltpu.SemaphoreType.DMA((13,)),
        ],
        compiler_params=pltpu.CompilerParams(vmem_limit_bytes=60 * 2**20),
    )(*results)
    return loss.reshape(()), grad_nodes, grad_weight.reshape(feat, feat), grad_texts


def solution(mesh):
    both = ("grp", "dev")
    placed = (
        P(both, None),
        P(both, None, None),
        P(),
        P(),
        P(both, None),
        P(both),
        P(both),
    )
    return jax.shard_map(
        shards,
        mesh=mesh,
        in_specs=placed,
        out_specs=(P(), P(both, None), P(), P(both, None)),
        check_vma=False,
    )
```
